32 devices in a mesh: dp: 16 (over z, y, x), tensor: 2 (over core).
Axes of the slice: x: 2, y: 2, z: 4, core: 2. Of those that a mesh axis runs over, the one named last changes fastest.
Arguments:
- tokens: bfloat16 [32768, 1024], P(('dp', 'tensor')), may hold values from -6 to 6
- block_ids: int32 [32, 1024], P('dp'), may hold values from 0 to 4, never falling along the last dimension, each value on 1 to 256 neighbouring positions
- memory_index: int32 [32768, 8, 32], P('dp', 'tensor'), may hold values from 0 to 16383
- memory_keys: bfloat16 [8, 16384, 128], P('tensor'), may hold values from -6 to 6
- memory_values: bfloat16 [8, 16384, 128], P('tensor'), may hold values from -6 to 6
- attn_gain: float32 [1024], replicated, may hold values from 0.5 to 1.5
- query_weight: bfloat16 [1024, 1024], P(None, 'tensor'), may hold values from -0.1875 to 0.1875
- key_weight: bfloat16 [1024, 1024], P(None, 'tensor'), may hold values from -0.1875 to 0.1875
- value_weight: bfloat16 [1024, 1024], P(None, 'tensor'), may hold values from -0.1875 to 0.1875
- output_weight: bfloat16 [1024, 1024], P('tensor'), may hold values from -1.5 to 1.5
- position_table: float32 [32, 8], P(None, 'tensor'), may hold values from -3 to 3
- memory_gate: float32 [8], P('tensor'), may hold values from -4 to 4
- mlp_gain: float32 [1024], replicated, may hold values from 0.5 to 1.5
- hidden_weight: bfloat16 [1024, 4096], P(None, 'tensor'), may hold values from -0.1875 to 0.1875
- return_weight: bfloat16 [4096, 1024], P('tensor'), may hold values from -0.09375 to 0.09375
- grad_output: bfloat16 [32768, 1024], P(('dp', 'tensor')), may hold values from -6 to 6
Outputs:
- layer_output: bfloat16 [32768, 1024], P(('dp', 'tensor'))
- tokens_grad: bfloat16 [32768, 1024], P(('dp', 'tensor'))
- attn_gain_grad: float32 [1024], replicated
- query_grad: float32 [1024, 1024], P(None, 'tensor')
- key_grad: float32 [1024, 1024], P(None, 'tensor')
- value_grad: float32 [1024, 1024], P(None, 'tensor')
- output_weight_grad: float32 [1024, 1024], P('tensor')
- table_grad: float32 [32, 8], P(None, 'tensor')
- gate_grad: float32 [8], P('tensor')
- mlp_gain_grad: float32 [1024], replicated
- hidden_grad: float32 [1024, 4096], P(None, 'tensor')
- return_grad: float32 [4096, 1024], P('tensor')
The draws below stay inside these ranges and needn't reach their ends.
Inputs may be any that keep to these rules, and one draw needn't show every extreme that they name: `block_ids`: inside each sequence block numbers never fall; each of the 5 blocks holds 1 to 256 positions, one exactly 256.
All inputs are finite; a program needn't handle non-finite values.
Results may differ from the reference program's by a relative error of at most 0.023.
Values may be sent and summed in bfloat16 or wider, within the bound.
No kernel may reach another device: no remote copies, remote signals or barrier semaphores. Data moves between devices by JAX's collectives and lax.ppermute only.
A program may use at most 512 MiB of HBM per device.

```python
import math
import jax
import jax.numpy as jnp
import numpy as np
from jax import lax

D = 1024
HEADS = 8
HD = 128
FF = 4096
BUCKETS = 32
TOPK = 32
SEQ = 1024
BLOCK = 256
NBLK = 5
MEM = 16384
SEQS_DEV = 2
SEQS = 32
TOKENS = 32768


def plant(values, own_key, low, top_value):
    shape = values.shape
    place = [jax.random.randint(jax.random.fold_in(own_key, axis), (), 0, shape[axis]) for axis in range(len(shape))]
    values = values.at[tuple(place)].set(low)
    longest = shape.index(max(shape))
    place[longest] = (place[longest] + 1) % shape[longest]
    return values.at[tuple(place)].set(top_value)


def spiked(array, stream_key, source, target, shards_of, factor):
    def block_of(position):
        return (jnp.arange(array.shape[position]) // (array.shape[position] // shards_of)).reshape((-1,) + (1,) * (array.ndim - 1 - position))

    first = jax.random.permutation(stream_key, shards_of)[block_of(target)]
    far = (block_of(target) + shards_of // 2) % shards_of
    return jnp.where((block_of(source) == first) | (block_of(source) == far), factor * array, array)


def level_of(stream_key, shape, pieces, smallest, largest):
    factor_of, own = 1.0, jax.random.fold_in(stream_key, 6)
    for position, parts in pieces:
        draws = jnp.exp(jax.random.uniform(jax.random.fold_in(own, position), (parts,), jnp.float32, smallest / len(pieces), largest / len(pieces)))
        factor_of = factor_of * jnp.repeat(draws, shape[position] // parts).reshape([-1 if axis == position else 1 for axis in range(len(shape))])
    return factor_of


def profile(count, total, reach, lean):
    loads = [(1 << 20) // math.isqrt(standing ** lean) + 1 for standing in range(2, count + 1)]
    surplus, holding = total - reach - (count - 1), [1] * (count - 1)
    while surplus > 0:
        free = [i for i in range(count - 1) if holding[i] < reach]
        pool, budget = sum([loads[i] for i in free]), surplus
        for i in free:
            more = min(reach - holding[i], max(1, budget * loads[i] // pool), surplus)
            holding[i] = holding[i] + more
            surplus = surplus - more
    return np.array([reach] + holding)


def ragged_sizes(own_key, count, total, limit, skew):
    if count == 2:
        one = jax.random.randint(own_key, (), max(1, total - limit), min(limit, total - 1) + 1)
        return jnp.stack([one, total - one])
    lengths = jnp.asarray(profile(count, total, limit, skew), jnp.int32)
    twos = (count - 1) // 2
    donor, sink = lengths[1:1 + 2 * twos:2], lengths[2:2 + 2 * twos:2]
    slack = jnp.minimum(donor - 1, limit - sink)
    shifted = jax.random.randint(jax.random.fold_in(own_key, 1), (twos,), 0, 1 << 20) % (slack + 1)
    lengths = lengths.at[1:1 + 2 * twos:2].set(donor - shifted).at[2:2 + 2 * twos:2].set(sink + shifted)
    return lengths[jax.random.permutation(jax.random.fold_in(own_key, 2), count)]


def noise(own_key, dims, scale, bound, pieces=(), kind=jnp.bfloat16):
    level = level_of(own_key, dims, pieces, -0.22, 0.18) if pieces else 1.0
    values = jax.random.normal(own_key, dims, jnp.float32) * scale * level
    return jnp.minimum(jnp.maximum(values, -bound), bound).astype(kind)


def gaussian_with(key, shape, scale, bound, cuts, heavy, kind=jnp.bfloat16):
    values = scale * jax.random.normal(key, shape, jnp.float32)
    if cuts:
        values = values * level_of(key, shape, cuts, -0.22, 0.18)
    return jnp.clip(spiked(values, jax.random.fold_in(key, 3), *heavy), -bound, bound).astype(kind)


def setup_inputs(seed: int = 0) -> dict:
    key_list = jax.random.split(jax.random.key(seed), 17)
    tokens = noise(key_list[0], (TOKENS, D), 1.0, 6.0, ((0, 32),))
    block_ids = jax.vmap(lambda own: jnp.searchsorted(jnp.cumsum(ragged_sizes(own, NBLK, SEQ, BLOCK, 1)), jnp.arange(SEQ), side="right"))(jax.random.split(key_list[1], SEQS)).reshape((SEQS, SEQ)).astype(jnp.int32)
    memory_index = plant(jax.random.randint(key_list[2], (TOKENS, HEADS, TOPK), 0, MEM), jax.random.fold_in(key_list[2], 1), 0, MEM - 1).astype(jnp.int32)
    memory_keys = noise(key_list[3], (HEADS, MEM, HD), 1.0, 6.0, ((0, 2),))
    memory_values = noise(key_list[4], (HEADS, MEM, HD), 1.0, 6.0, ((0, 2),))
    attn_gain = jnp.clip(1.0 + 0.1 * jax.random.normal(key_list[5], (D,), jnp.float32), 0.5, 1.5)
    query_weight = noise(key_list[6], (D, HEADS * HD), D ** -0.5, 0.1875, ((1, 2),))
    key_weight = noise(key_list[7], (D, HEADS * HD), D ** -0.5, 0.1875, ((1, 2),))
    value_weight = noise(key_list[8], (D, HEADS * HD), D ** -0.5, 0.1875, ((1, 2),))
    output_weight = noise(key_list[9], (HEADS * HD, D), 16 ** -0.5, 1.5, ((0, 2),))
    position_table = noise(key_list[10], (BUCKETS, HEADS), 1.0, 3.0, ((1, 2),), jnp.float32)
    memory_gate = noise(key_list[11], (HEADS,), 1.5, 4.0, ((0, 2),), jnp.float32)
    mlp_gain = jnp.clip(1.0 + 0.1 * jax.random.normal(key_list[12], (D,), jnp.float32), 0.5, 1.5)
    hidden_weight = noise(key_list[13], (D, FF), D ** -0.5, 0.1875, ((1, 2),))
    return_weight = noise(key_list[14], (FF, D), FF ** -0.5, 0.09375, ((0, 2),))
    grad_output = gaussian_with(key_list[15], (TOKENS, D), 1.0, 6.0, ((0, 32),), (0, 1, 32, 2.75))
    return dict(tokens=tokens, block_ids=block_ids, memory_index=memory_index, memory_keys=memory_keys, memory_values=memory_values, attn_gain=attn_gain, query_weight=query_weight, key_weight=key_weight, value_weight=value_weight, output_weight=output_weight, position_table=position_table, memory_gate=memory_gate, mlp_gain=mlp_gain, hidden_weight=hidden_weight, return_weight=return_weight, grad_output=grad_output)


eps_norm = 1e-06
far_steps = (12, 16, 23, 32, 46, 64, 91)
exact_mode = lax.Precision.HIGHEST

@jax.custom_vjp
def low(v):
    return lax.optimization_barrier(v.astype(jnp.bfloat16)).astype(jnp.float32)

@jax.custom_vjp
def low_back(v):
    return v

def low_keep(v):
    return (low(v), None)

def low_pass(kept, grad):
    return (grad,)

def back_keep(v):
    return (v, None)

def back_low(kept, grad):
    return (low(grad),)
low.defvjp(low_keep, low_pass)
low_back.defvjp(back_keep, back_low)

def bucket_of(relative):
    upper_half = jnp.where(relative > 0, 16, 0).astype(jnp.int32)
    distance = jnp.abs(relative).astype(jnp.int32)
    far_bucket = 8 + sum(((distance >= step_size).astype(jnp.int32) for step_size in far_steps))
    return upper_half + jnp.where(distance < 8, distance, far_bucket).astype(jnp.int32)

def rms_scaled(rows, gain):
    return rows * lax.rsqrt(lax.optimization_barrier(jnp.mean(rows * rows, -1, keepdims=True)) + eps_norm) * gain

def softmax_rows(scores):
    row_top = lax.optimization_barrier(jnp.max(scores, -1, keepdims=True))
    exponent = jnp.exp(scores - row_top)
    return exponent / lax.optimization_barrier(jnp.sum(exponent, -1, keepdims=True))

def pair_attend(pair_items, position_table, memory_gate, memory_keys, memory_values, buckets):
    query_pair, key_pair, value_pair, index_pair, block_row, head_index = pair_items
    score_scale = HD ** (-0.5)
    column = lax.dynamic_index_in_dim(position_table, head_index, 1, False)
    bias_matrix = jnp.take(column, buckets)
    scores = jnp.dot(query_pair, key_pair.T, precision=exact_mode) * score_scale + bias_matrix
    scores = low_back(scores)
    step_gap = block_row[:, None] - block_row[None, :]
    allowed = (step_gap >= 0) & (step_gap <= 1)
    probabilities = softmax_rows(jnp.where(allowed, scores, -jnp.inf))
    local_read = low_back(jnp.dot(low(probabilities), value_pair, precision=exact_mode))
    keys_head = lax.dynamic_index_in_dim(memory_keys, head_index, 0, False)
    values_head = lax.dynamic_index_in_dim(memory_values, head_index, 0, False)
    keys_found = jnp.take(keys_head, index_pair, axis=0)
    values_found = jnp.take(values_head, index_pair, axis=0)
    memory_scores = jnp.einsum('qd,qkd->qk', query_pair, keys_found, precision=exact_mode) * score_scale
    memory_read = jnp.einsum('qk,qkd->qd', softmax_rows(memory_scores), values_found, precision=exact_mode)
    gate_value = jax.nn.sigmoid(lax.dynamic_index_in_dim(memory_gate, head_index, 0, False))
    return gate_value * memory_read + (1.0 - gate_value) * local_read

def layer(params, token_rows, blocks, index_rows, memory_keys, memory_values, buckets):
    attn_gain, query_weight, key_weight, value_weight, output_weight, position_table, memory_gate, mlp_gain, hidden_weight, return_weight = params
    seq_count = blocks.shape[0]
    seq_len = blocks.shape[1]
    normed = low(rms_scaled(token_rows, attn_gain))
    queries = low(low_back(jnp.dot(normed, query_weight, precision=exact_mode)))
    keys = low(low_back(jnp.dot(normed, key_weight, precision=exact_mode)))
    values = low(low_back(jnp.dot(normed, value_weight, precision=exact_mode)))

    def to_pairs(rows):
        return rows.reshape(seq_count, seq_len, HEADS, -1).transpose(0, 2, 1, 3).reshape(seq_count * HEADS, seq_len, -1)
    head_ids = jnp.tile(jnp.arange(HEADS, dtype=jnp.int32), seq_count)
    pair_blocks = jnp.repeat(blocks, HEADS, axis=0)
    index_pairs = to_pairs(index_rows.reshape(index_rows.shape[0], -1))

    def attend(pair_items):
        return pair_attend(pair_items, position_table, memory_gate, memory_keys, memory_values, buckets)
    mixed_pairs = lax.map(jax.checkpoint(attend), (to_pairs(queries), to_pairs(keys), to_pairs(values), index_pairs, pair_blocks, head_ids))
    mixed_rows = mixed_pairs.reshape(seq_count, HEADS, seq_len, HD).transpose(0, 2, 1, 3).reshape(seq_count * seq_len, HEADS * HD)
    mixed = low(low_back(mixed_rows))
    middle = token_rows + low_back(jnp.dot(mixed, output_weight, precision=exact_mode))
    second = low(rms_scaled(middle, mlp_gain))
    hidden = low_back(jnp.dot(second, hidden_weight, precision=exact_mode))
    active = low(jax.nn.gelu(hidden))
    return middle + low_back(jnp.dot(active, return_weight, precision=exact_mode))

def reference(tokens, block_ids, memory_index, memory_keys, memory_values, attn_gain, query_weight, key_weight, value_weight, output_weight, position_table, memory_gate, mlp_gain, hidden_weight, return_weight, grad_output):
    weights = tuple((item.astype(jnp.float32) for item in (attn_gain, query_weight, key_weight, value_weight, output_weight, position_table, memory_gate, mlp_gain, hidden_weight, return_weight)))
    keys_all = memory_keys.astype(jnp.float32)
    values_all = memory_values.astype(jnp.float32)
    groups = SEQS // SEQS_DEV
    group_rows = SEQS_DEV * SEQ
    token_groups = tokens.astype(jnp.float32).reshape(groups, group_rows, D)
    block_groups = block_ids.reshape(groups, SEQS_DEV, SEQ)
    index_groups = memory_index.reshape(groups, group_rows, HEADS, TOPK)
    positions = jnp.arange(SEQ, dtype=jnp.int32)
    buckets = bucket_of(positions[None, :] - positions[:, None])
    layer_saved = jax.checkpoint(layer)

    def run(params, token_all):

        def step(carry, group_items):
            token_rows, blocks, index_rows = group_items
            return (carry, layer_saved(params, token_rows, blocks, index_rows, keys_all, values_all, buckets))
        unused, outputs = lax.scan(step, jnp.zeros((), jnp.float32), (token_all, block_groups, index_groups))
        return outputs
    result, back = jax.vjp(run, weights, token_groups)
    grads, token_grad = back(grad_output.astype(jnp.float32).reshape(groups, group_rows, D))
    return (result.reshape(TOKENS, D).astype(jnp.bfloat16), token_grad.reshape(TOKENS, D).astype(jnp.bfloat16), grads[0], grads[1], grads[2], grads[3], grads[4], grads[5], grads[6], grads[7], grads[8], grads[9])
```

```python
import functools
import math

import jax
import jax.numpy as jnp
from jax import lax
from jax.experimental import pallas as pl
from jax.experimental.pallas import tpu as pltpu
from jax.sharding import PartitionSpec as P

eps_norm = 1e-06
far_steps = (12, 16, 23, 32, 46, 64, 91)
exact_mode = lax.Precision.HIGHEST
low_type = jnp.bfloat16
full_type = jnp.float32
log2_e = math.log2(math.e)
tile = 256
span = 3 * tile
ring = 1024
mask_gap = -(2.0**100)
vmem_most = 60 * 2**20


def bucket_of(relative):
    upper_half = jnp.where(relative > 0, 16, 0).astype(jnp.int32)
    distance = jnp.abs(relative)
    far_bucket = 8 + sum(((distance >= step_size).astype(jnp.int32) for step_size in far_steps))
    return upper_half + jnp.where(distance < 8, distance, far_bucket)


def rms_scaled(rows, gain):
    return rows * lax.rsqrt(jnp.mean(rows * rows, -1, keepdims=True) + eps_norm) * gain


def dot_rows(left, right):
    return jnp.dot(left, right, preferred_element_type=full_type)


def dot_outer(left, right):
    return lax.dot_general(
        left, right, (((0,), (0,)), ((), ())), preferred_element_type=full_type
    )


def dot_inner(left, right):
    return lax.dot_general(
        left, right, (((1,), (1,)), ((), ())), preferred_element_type=full_type
    )


def interleave_kernel(key_ref, value_ref, table_ref):
    rows = key_ref.shape[1]
    flat = table_ref.reshape(1, 2 * rows, 128)
    row = lax.broadcasted_iota(jnp.int32, (256, 256), 0)
    column = lax.broadcasted_iota(jnp.int32, (256, 256), 1)
    order = jnp.where(column == (row // 2 + (row % 2) * 128), 1.0, 0.0).astype(low_type)
    for part in range(rows // 128):
        both = jnp.concatenate(
            [key_ref[0, pl.ds(part * 128, 128)], value_ref[0, pl.ds(part * 128, 128)]], 0
        )
        flat[0, pl.ds(part * 256, 256)] = dot_rows(order, both).astype(low_type)


def interleave(memory_keys, memory_values):
    heads, rows, width = memory_keys.shape
    step = min(2048, rows)
    spec = pl.BlockSpec((1, step, width), lambda h, i: (h, i, 0))
    return pl.pallas_call(
        interleave_kernel,
        grid=(heads, rows // step),
        in_specs=[spec, spec],
        out_specs=pl.BlockSpec((1, step, 2, width), lambda h, i: (h, i, 0, 0)),
        out_shape=jax.ShapeDtypeStruct((heads, rows, 2, width), low_type),
        name="interleave",
    )(memory_keys, memory_values)


def gather_kernel(
    index_hbm, table_hbm, found_ref, table_ref, table_sems, index_a, index_b, index_sems
):
    heads = pl.num_programs(0)
    head = pl.program_id(0)
    step = head * pl.num_programs(1) + pl.program_id(1)
    steps = heads * pl.num_programs(1)
    chunk = found_ref.shape[0] // 2
    rows = table_ref.shape[0] // table_sems.shape[0]
    slots = (index_a, index_b)

    def index_copy(number, slot):
        return pltpu.make_async_copy(index_hbm.at[number], slots[slot], index_sems.at[slot])

    def table_copy(number):
        where = pl.ds(number * rows, rows)
        return pltpu.make_async_copy(
            table_hbm.at[where], table_ref.at[where], table_sems.at[number]
        )

    @pl.when(step == 0)
    def start_all():
        index_copy(0, 0).start()
        index_copy(1, 1).start()
        for number in range(table_sems.shape[0]):
            table_copy(number).start()

    @pl.when(pl.program_id(1) == 0)
    def wait_table():
        table_copy(head).wait()

    following = jnp.minimum(step + 1, steps - 1)
    for slot in range(2):
        index_copy(2 * step + slot, slot).wait()
        picked = slots[slot]
        for start in range(0, chunk, 8):
            rows_now = [
                table_ref[picked[(start + j) // 128, (start + j) % 128]] for j in range(8)
            ]
            for j in range(8):
                found_ref[slot * chunk + start + j] = rows_now[j]
        index_copy(2 * following + slot, slot).start()

    @pl.when(step == steps - 1)
    def drain():
        index_copy(2 * following, 0).wait()
        index_copy(2 * following + 1, 1).wait()


def gather_found(index_rows, table):
    heads, rows, unused, width = table.shape
    total = index_rows.size // heads
    chunk = min(4096, total // 2)
    blocks = total // (2 * chunk)
    return pl.pallas_call(
        gather_kernel,
        grid=(heads, blocks),
        in_specs=[pl.BlockSpec(memory_space=pl.ANY), pl.BlockSpec(memory_space=pl.ANY)],
        out_specs=pl.BlockSpec((2 * chunk, 2, width), lambda h, i: (h * blocks + i, 0, 0)),
        out_shape=jax.ShapeDtypeStruct((heads * total, 2, width), low_type),
        scratch_shapes=[
            pltpu.VMEM((heads * rows, 2, width), low_type),
            pltpu.SemaphoreType.DMA((heads,)),
            pltpu.SMEM((chunk // 128, 128), jnp.int32),
            pltpu.SMEM((chunk // 128, 128), jnp.int32),
            pltpu.SemaphoreType.DMA((2,)),
        ],
        compiler_params=pltpu.CompilerParams(vmem_limit_bytes=vmem_most),
        name="gather_found",
    )(index_rows.reshape(-1, chunk // 128, 128), table.reshape(heads * rows, 2, width))


def own_columns(picks):
    shape = (8, 8 * picks * 2)
    lane = lax.broadcasted_iota(jnp.int32, shape, 1)
    row = lax.broadcasted_iota(jnp.int32, shape, 0)
    return jnp.logical_and(lane // (2 * picks) == row, lane % 2 == 0)


def recall_kernel(picks, scale, found_ref, query_ref, read_ref):
    tokens = query_ref.shape[0]
    wide = 8 * picks * 2
    own = own_columns(picks)
    groups = range(tokens // 8)
    scores = [
        dot_inner(query_ref[pl.ds(g * 8, 8), :], found_ref[pl.ds(g * wide, wide), :])
        for g in groups
    ]
    for g in groups:
        masked = jnp.where(own, scores[g] * (scale * log2_e), -jnp.inf)
        exponent = jnp.exp2(masked - jnp.max(masked, 1, keepdims=True))
        total = jnp.sum(exponent, 1, keepdims=True)
        shifted = pltpu.roll(exponent, 1, 1).astype(low_type)
        read_ref[pl.ds(g * 8, 8), :] = (
            dot_rows(shifted, found_ref[pl.ds(g * wide, wide), :]) / total
        )


def recall(found, queries, heads, picks, scale):
    tokens = queries.shape[0]
    width = queries.shape[1] // (3 * heads)
    step = min(256, tokens)
    blocks = tokens // step
    return pl.pallas_call(
        functools.partial(recall_kernel, picks, scale),
        grid=(heads, blocks),
        in_specs=[
            pl.BlockSpec((step * picks * 2, width), lambda h, i: (h * blocks + i, 0)),
            pl.BlockSpec((step, width), lambda h, i: (i, h)),
        ],
        out_specs=pl.BlockSpec((step, width), lambda h, i: (i, h)),
        out_shape=jax.ShapeDtypeStruct((tokens, heads * width), full_type),
        compiler_params=pltpu.CompilerParams(vmem_limit_bytes=vmem_most),
        name="recall",
    )(found, queries)


def recall_back_kernel(
    picks, scale, gate_ref, found_ref, query_ref, delta_ref, query_delta_ref, sums_ref
):
    tokens = query_ref.shape[0]
    wide = 8 * picks * 2
    own = own_columns(picks)
    gate = gate_ref[pl.program_id(0)]
    groups = range(tokens // 8)
    both = []
    for g in groups:
        rows = jnp.concatenate(
            [query_ref[pl.ds(g * 8, 8), :], delta_ref[pl.ds(g * 8, 8), :]], 0
        )
        both.append(dot_inner(rows, found_ref[pl.ds(g * wide, wide), :]))
    gained = jnp.zeros((8, 1), full_type)
    for g in groups:
        masked = jnp.where(own, both[g][:8] * (scale * log2_e), -jnp.inf)
        exponent = jnp.exp2(masked - jnp.max(masked, 1, keepdims=True))
        weights = exponent / jnp.sum(exponent, 1, keepdims=True)
        reads = pltpu.roll(both[g][8:], wide - 1, 1)
        expected = jnp.sum(weights * reads, 1, keepdims=True)
        gained = gained + expected
        score_delta = (weights * (reads - expected)).astype(low_type)
        query_delta_ref[pl.ds(g * 8, 8), :] = dot_rows(
            score_delta, found_ref[pl.ds(g * wide, wide), :]
        ) * (scale * gate)

    @pl.when(pl.program_id(1) == 0)
    def clear():
        sums_ref[...] = jnp.zeros(sums_ref.shape, full_type)

    sums_ref[0] += jnp.broadcast_to(gained, (8, 128))


def recall_back(found, queries, mixed_delta, gates, heads, picks, scale):
    tokens = queries.shape[0]
    width = mixed_delta.shape[1] // heads
    step = min(256, tokens)
    blocks = tokens // step
    rows_spec = pl.BlockSpec((step, width), lambda h, i: (i, h))
    return pl.pallas_call(
        functools.partial(recall_back_kernel, picks, scale),
        grid=(heads, blocks),
        in_specs=[
            pl.BlockSpec(memory_space=pltpu.SMEM),
            pl.BlockSpec((step * picks * 2, width), lambda h, i: (h * blocks + i, 0)),
            rows_spec,
            rows_spec,
        ],
        out_specs=[rows_spec, pl.BlockSpec((1, 8, 128), lambda h, i: (h, 0, 0))],
        out_shape=[
            jax.ShapeDtypeStruct((tokens, heads * width), full_type),
            jax.ShapeDtypeStruct((heads, 8, 128), full_type),
        ],
        compiler_params=pltpu.CompilerParams(vmem_limit_bytes=vmem_most),
        name="recall_back",
    )(gates, found, queries, mixed_delta)


def band(column_ref):
    wide = jnp.broadcast_to(column_ref[0], (tile, ring))
    return pltpu.roll(wide, 0, 1, stride=1, stride_axis=0)[:, :span]


def local_kernel(
    scale, gate_ref, far_ref, column_ref, query_ref, key_ref, value_ref, query_mask_ref,
    key_mask_ref, recall_ref, mixed_ref, bias_ref,
):
    head = pl.program_id(0)

    @pl.when(pl.program_id(1) == 0)
    def make_band():
        bias_ref[...] = band(column_ref)

    gate = gate_ref[head]
    count = query_ref.shape[0] // tile
    at = [pl.ds(t * tile, tile) for t in range(count)]
    keys = [jnp.concatenate([key_ref[a, :], key_mask_ref[0, a, :]], 1) for a in at]
    for t in range(count):
        rows = jnp.concatenate([query_ref[at[t], :], query_mask_ref[0, at[t], :]], 1)
        parts = []
        for j in range(count):
            step = j - t
            if step < -1:
                bias = far_ref[head, 0]
            elif step > 1:
                bias = far_ref[head, 1]
            else:
                bias = bias_ref[:, pl.ds((step + 1) * tile, tile)]
            parts.append(dot_inner(rows, keys[j]) * (scale * log2_e) + bias)
        top = jnp.max(functools.reduce(jnp.maximum, parts), 1, keepdims=True)
        parts = [jnp.exp2(part - top) for part in parts]
        total = jnp.sum(functools.reduce(jnp.add, parts), 1, keepdims=True)
        read = sum(dot_rows(parts[j].astype(low_type), value_ref[at[j], :]) for j in range(count))
        mixed_ref[at[t], :] = (
            gate * recall_ref[at[t], :] + ((1.0 - gate) / total) * read
        ).astype(low_type)


def local_read(projected, query_mask, key_mask, recalled, columns, far, gates, seq_len, scale):
    tokens = recalled.shape[0]
    heads = gates.shape[0]
    width = recalled.shape[1] // heads

    def rows_of(shift):
        return pl.BlockSpec((seq_len, width), lambda h, s: (s, h + shift * heads))

    mask_spec = pl.BlockSpec((1, seq_len, 128), lambda h, s: (s, 0, 0))
    smem = pl.BlockSpec(memory_space=pltpu.SMEM)
    return pl.pallas_call(
        functools.partial(local_kernel, scale),
        grid=(heads, tokens // seq_len),
        in_specs=[
            smem,
            smem,
            pl.BlockSpec((1, 1, ring), lambda h, s: (h, 0, 0)),
            rows_of(0),
            rows_of(1),
            rows_of(2),
            mask_spec,
            mask_spec,
            rows_of(0),
        ],
        out_specs=rows_of(0),
        out_shape=jax.ShapeDtypeStruct((tokens, heads * width), low_type),
        scratch_shapes=[pltpu.VMEM((tile, span), full_type)],
        compiler_params=pltpu.CompilerParams(vmem_limit_bytes=vmem_most),
        name="local_read",
    )(gates, far, columns, projected, projected, projected, query_mask, key_mask, recalled)


def local_back_kernel(
    scale, gate_ref, far_ref, column_ref, query_ref, key_ref, value_ref, query_mask_ref,
    key_mask_ref, delta_ref, recall_delta_ref, query_delta_ref, key_delta_ref, value_delta_ref,
    diagonal_ref, sums_ref, bias_ref, near_ref, key_sum_ref, value_sum_ref,
):
    head = pl.program_id(0)
    last = pl.program_id(1) == pl.num_programs(1) - 1

    @pl.when(pl.program_id(1) == 0)
    def make_band():
        bias_ref[...] = band(column_ref)
        near_ref[...] = jnp.zeros(near_ref.shape, full_type)
        sums_ref[...] = jnp.zeros(sums_ref.shape, full_type)

    gate = gate_ref[head]
    count = query_ref.shape[0] // tile
    at = [pl.ds(t * tile, tile) for t in range(count)]
    keys = [jnp.concatenate([key_ref[a, :], key_mask_ref[0, a, :]], 1) for a in at]
    turned = [key_ref[a, :].astype(full_type).T.astype(low_type) for a in at]
    gained = jnp.zeros((1, tile), full_type)
    far_sums = [jnp.zeros((8, tile), full_type) for side in range(2)]
    for t in range(count):
        rows = jnp.concatenate([query_ref[at[t], :], query_mask_ref[0, at[t], :]], 1)
        delta = ((1.0 - gate) * delta_ref[at[t], :].astype(full_type)).astype(low_type)
        parts = []
        for j in range(count):
            step = j - t
            if step < -1:
                bias = far_ref[head, 0]
            elif step > 1:
                bias = far_ref[head, 1]
            else:
                bias = bias_ref[:, pl.ds((1 - step) * tile, tile)]
            parts.append(dot_inner(keys[j], rows) * (scale * log2_e) + bias)
        top = jnp.max(functools.reduce(jnp.maximum, parts), 0, keepdims=True)
        parts = [jnp.exp2(part - top) for part in parts]
        total = jnp.sum(functools.reduce(jnp.add, parts), 0, keepdims=True)
        inverse = 1.0 / total
        parts = [part * inverse for part in parts]
        moves = [dot_inner(value_ref[at[j], :], delta) for j in range(count)]
        expected = jnp.sum(
            functools.reduce(jnp.add, [parts[j] * moves[j] for j in range(count)]),
            0,
            keepdims=True,
        )
        gained = gained + expected
        query_sum = None
        for j in range(count):
            step = j - t
            score_delta = parts[j] * (moves[j] - expected)
            if abs(step) > 1:
                side = 0 if step < 0 else 1
                far_sums[side] = far_sums[side] + jnp.sum(
                    score_delta.reshape(tile // 8, 8, tile), 0
                )
            else:
                near_ref[:, pl.ds((1 - step) * tile, tile)] += score_delta
            low_delta = score_delta.astype(low_type)
            value_part = dot_rows(parts[j].astype(low_type), delta)
            key_part = dot_rows(low_delta, query_ref[at[t], :])
            query_part = dot_rows(turned[j], low_delta)
            if t == 0:
                value_sum_ref[at[j], :] = value_part
                key_sum_ref[at[j], :] = key_part
            else:
                value_sum_ref[at[j], :] += value_part
                key_sum_ref[at[j], :] += key_part
            query_sum = query_part if j == 0 else query_sum + query_part
        query_delta_ref[at[t], :] = (
            query_sum.T * scale + recall_delta_ref[at[t], :]
        ).astype(low_type)
    key_delta_ref[...] = (key_sum_ref[...] * scale).astype(low_type)
    value_delta_ref[...] = value_sum_ref[...].astype(low_type)
    sums_ref[0, 0:1] += gained
    sums_ref[0, 8:16] += far_sums[0]
    sums_ref[0, 16:24] += far_sums[1]

    @pl.when(last)
    def fold_diagonals():
        total = jnp.zeros((8, ring), full_type)
        for g in range(tile // 8):
            part = jnp.concatenate(
                [near_ref[pl.ds(g * 8, 8), :], jnp.zeros((8, ring - span), full_type)], 1
            )
            total = total + (pltpu.roll(part, ring - 8 * g, 1) if g else part)
        row = lax.broadcasted_iota(jnp.int32, (8, ring), 0)
        for bit in (1, 2, 4):
            total = jnp.where((row & bit) != 0, pltpu.roll(total, ring - bit, 1), total)
        diagonal_ref[0] = total


def local_back(
    projected, query_mask, key_mask, mixed_delta, recall_delta, columns, far, gates, seq_len, scale
):
    tokens = mixed_delta.shape[0]
    heads = gates.shape[0]
    width = mixed_delta.shape[1] // heads

    def rows_of(shift):
        return pl.BlockSpec((seq_len, width), lambda h, s: (s, h + shift * heads))

    mask_spec = pl.BlockSpec((1, seq_len, 128), lambda h, s: (s, 0, 0))
    smem = pl.BlockSpec(memory_space=pltpu.SMEM)
    rows_shape = jax.ShapeDtypeStruct((tokens, heads * width), low_type)
    return pl.pallas_call(
        functools.partial(local_back_kernel, scale),
        grid=(heads, tokens // seq_len),
        in_specs=[
            smem,
            smem,
            pl.BlockSpec((1, 1, ring), lambda h, s: (h, 0, 0)),
            rows_of(0),
            rows_of(1),
            rows_of(2),
            mask_spec,
            mask_spec,
            rows_of(0),
            rows_of(0),
        ],
        out_specs=[
            rows_of(0),
            rows_of(0),
            rows_of(0),
            pl.BlockSpec((1, 8, ring), lambda h, s: (h, 0, 0)),
            pl.BlockSpec((1, 24, tile), lambda h, s: (h, 0, 0)),
        ],
        out_shape=[
            rows_shape,
            rows_shape,
            rows_shape,
            jax.ShapeDtypeStruct((heads, 8, ring), full_type),
            jax.ShapeDtypeStruct((heads, 24, tile), full_type),
        ],
        scratch_shapes=[
            pltpu.VMEM((tile, span), full_type),
            pltpu.VMEM((tile, span), full_type),
            pltpu.VMEM((seq_len, width), full_type),
            pltpu.VMEM((seq_len, width), full_type),
        ],
        compiler_params=pltpu.CompilerParams(vmem_limit_bytes=vmem_most),
        name="local_back",
    )(
        gates, far, columns, projected, projected, projected, query_mask, key_mask, mixed_delta,
        recall_delta,
    )


def mask_rows(block_ids):
    level = jnp.arange(128, dtype=jnp.int32)
    gap = block_ids[:, :, None] - level
    query_mask = jnp.where((gap >= 0) & (gap <= 1), 0.0, mask_gap).astype(low_type)
    key_mask = (gap == 0).astype(low_type)
    return query_mask, key_mask


def body(
    tokens,
    block_ids,
    memory_index,
    memory_keys,
    memory_values,
    attn_gain,
    query_weight,
    key_weight,
    value_weight,
    output_weight,
    position_table,
    memory_gate,
    mlp_gain,
    hidden_weight,
    return_weight,
    grad_output,
):
    share_rows = tokens.shape[0]
    seq_len = block_ids.shape[1]
    head_count, memory_rows, head_width = memory_keys.shape
    picks = memory_index.shape[2]
    inner_width = head_count * head_width
    scale = head_width ** (-0.5)
    group = lax.axis_size("tensor")
    group_rows = share_rows * group

    offsets = jnp.arange(head_count, dtype=jnp.int32) * memory_rows
    index_rows = memory_index.transpose(1, 0, 2) + offsets[:, None, None]
    found = gather_found(index_rows, interleave(memory_keys, memory_values))
    found = found.reshape(-1, head_width)

    token_full = tokens.astype(full_type)
    normed_rows = rms_scaled(token_full, attn_gain).astype(low_type)
    normed = lax.all_gather(normed_rows, "tensor", axis=0, tiled=True)
    joined = jnp.concatenate([query_weight, key_weight, value_weight], 1)
    projected = dot_rows(normed, joined).astype(low_type)

    query_mask, key_mask = mask_rows(block_ids)
    place = jnp.arange(ring, dtype=jnp.int32)
    place = jnp.where(place < span, place, place - ring)
    ahead = bucket_of(place - tile)
    behind = bucket_of(tile - place)
    level = jnp.arange(32, dtype=jnp.int32)
    ahead_hot = (ahead[:, None] == level).astype(full_type)
    behind_hot = (behind[:, None] == level).astype(full_type)
    scaled_table = position_table * log2_e
    ahead_columns = jnp.dot(ahead_hot, scaled_table, precision=exact_mode).T[:, None, :]
    behind_columns = jnp.dot(behind_hot, scaled_table, precision=exact_mode).T[:, None, :]
    far = jnp.stack([scaled_table[15], scaled_table[31]], 1)
    gates = jax.nn.sigmoid(memory_gate)

    recalled = recall(found, projected, head_count, picks, scale)
    mixed_rows = local_read(
        projected, query_mask, key_mask, recalled, ahead_columns, far, gates, seq_len, scale
    )
    middle = token_full + lax.psum_scatter(
        dot_rows(mixed_rows, output_weight), "tensor", scatter_dimension=0, tiled=True
    )
    second_rows = rms_scaled(middle, mlp_gain).astype(low_type)
    grad_rows = grad_output.astype(full_type)
    second = lax.all_gather(second_rows, "tensor", axis=0, tiled=True)
    hidden = dot_rows(second, hidden_weight)
    active = jax.nn.gelu(hidden).astype(low_type)
    layer_output = (
        middle
        + lax.psum_scatter(
            dot_rows(active, return_weight).astype(low_type),
            "tensor",
            scatter_dimension=0,
            tiled=True,
        ).astype(full_type)
    ).astype(low_type)
    grad_full = lax.all_gather(grad_output, "tensor", axis=0, tiled=True)
    return_part = dot_outer(active, grad_full)
    active_delta = dot_inner(grad_full, return_weight)
    gelu_back = jax.vjp(jax.nn.gelu, hidden)[1]
    hidden_delta = gelu_back(active_delta)[0].astype(low_type)
    hidden_part = dot_outer(second, hidden_delta)
    second_delta = lax.psum_scatter(
        dot_inner(hidden_delta, hidden_weight), "tensor", scatter_dimension=0, tiled=True
    )
    second_back = jax.vjp(rms_scaled, middle, mlp_gain)[1]
    middle_part, mlp_gain_part = second_back(second_delta)
    middle_delta = grad_rows + middle_part
    middle_low = middle_delta.astype(low_type)
    middle_full = lax.all_gather(middle_low, "tensor", axis=0, tiled=True)
    output_part = dot_outer(mixed_rows, middle_full)
    mixed_delta = dot_inner(middle_full, output_weight).astype(low_type)

    recall_delta, recall_sums = recall_back(
        found, projected, mixed_delta, gates, head_count, picks, scale
    )
    query_delta, key_delta, value_delta, diagonals, local_sums = local_back(
        projected, query_mask, key_mask, mixed_delta, recall_delta, behind_columns, far, gates,
        seq_len, scale,
    )
    recall_gain = jnp.sum(recall_sums[:, :, 0], 1)
    local_gain = jnp.sum(local_sums[:, 0], 1)
    gate_part = gates * (1.0 - gates) * recall_gain - gates * local_gain
    diagonal_sums = jnp.sum(diagonals, 1)
    table_part = jnp.dot(diagonal_sums, behind_hot, precision=exact_mode).T
    far_left = jnp.sum(local_sums[:, 8:16], (1, 2))
    far_right = jnp.sum(local_sums[:, 16:24], (1, 2))
    table_part = table_part.at[15].add(far_left).at[31].add(far_right)

    project_delta = jnp.concatenate([query_delta, key_delta, value_delta], 1)
    joined_part = dot_outer(normed, project_delta)
    query_part = joined_part[:, :inner_width]
    key_part = joined_part[:, inner_width : 2 * inner_width]
    value_part = joined_part[:, 2 * inner_width :]
    normed_delta = lax.psum_scatter(
        dot_inner(project_delta, joined).astype(low_type),
        "tensor",
        scatter_dimension=0,
        tiled=True,
    ).astype(full_type)
    first_back = jax.vjp(rms_scaled, token_full, attn_gain)[1]
    token_part, attn_gain_part = first_back(normed_delta)
    tokens_grad = (middle_delta + token_part).astype(low_type)
    (
        query_grad,
        key_grad,
        value_grad,
        output_weight_grad,
        table_grad,
        gate_grad,
        hidden_grad,
        return_grad,
    ) = (
        lax.psum(part.astype(low_type), "dp").astype(full_type)
        for part in (
            query_part,
            key_part,
            value_part,
            output_part,
            table_part,
            gate_part,
            hidden_part,
            return_part,
        )
    )
    attn_gain_grad, mlp_gain_grad = lax.psum((attn_gain_part, mlp_gain_part), ("dp", "tensor"))
    return (
        layer_output,
        tokens_grad,
        attn_gain_grad,
        query_grad,
        key_grad,
        value_grad,
        output_weight_grad,
        table_grad,
        gate_grad,
        mlp_gain_grad,
        hidden_grad,
        return_grad,
    )


def solution(mesh):
    def run(*arrays):
        with jax.sharding.use_abstract_mesh(mesh.abstract_mesh):
            return jax.shard_map(
                body,
                mesh=mesh,
                in_specs=(
                    P(("dp", "tensor"), None),
                    P("dp", None),
                    P("dp", "tensor", None),
                    P("tensor", None, None),
                    P("tensor", None, None),
                    P(),
                    P(None, "tensor"),
                    P(None, "tensor"),
                    P(None, "tensor"),
                    P("tensor", None),
                    P(None, "tensor"),
                    P("tensor"),
                    P(),
                    P(None, "tensor"),
                    P("tensor", None),
                    P(("dp", "tensor"), None),
                ),
                out_specs=(
                    P(("dp", "tensor"), None),
                    P(("dp", "tensor"), None),
                    P(),
                    P(None, "tensor"),
                    P(None, "tensor"),
                    P(None, "tensor"),
                    P("tensor", None),
                    P(None, "tensor"),
                    P("tensor"),
                    P(),
                    P(None, "tensor"),
                    P("tensor", None),
                ),
                check_vma=False,
            )(*arrays)

    return run
```

```python
import functools
import math

import jax
import jax.numpy as jnp
from jax import lax
from jax.experimental import pallas as pl
from jax.experimental.pallas import tpu as pltpu
from jax.sharding import PartitionSpec as P

eps_norm = 1e-06
far_steps = (12, 16, 23, 32, 46, 64, 91)
exact_mode = lax.Precision.HIGHEST
low_type = jnp.bfloat16
full_type = jnp.float32
log2_e = math.log2(math.e)
tile = 256
span = 3 * tile
ring = 1024
mask_gap = -(2.0**100)
vmem_most = 60 * 2**20


def bucket_of(relative):
    upper_half = jnp.where(relative > 0, 16, 0).astype(jnp.int32)
    distance = jnp.abs(relative)
    far_bucket = 8 + sum(((distance >= step_size).astype(jnp.int32) for step_size in far_steps))
    return upper_half + jnp.where(distance < 8, distance, far_bucket)


def rms_scaled(rows, gain):
    return rows * lax.rsqrt(jnp.mean(rows * rows, -1, keepdims=True) + eps_norm) * gain


def dot_rows(left, right):
    return jnp.dot(left, right, preferred_element_type=full_type)


def dot_outer(left, right):
    return lax.dot_general(
        left, right, (((0,), (0,)), ((), ())), preferred_element_type=full_type
    )


def dot_inner(left, right):
    return lax.dot_general(
        left, right, (((1,), (1,)), ((), ())), preferred_element_type=full_type
    )


def interleave_kernel(key_ref, value_ref, table_ref):
    rows = key_ref.shape[1]
    row = lax.broadcasted_iota(jnp.int32, (256, 256), 0)
    column = lax.broadcasted_iota(jnp.int32, (256, 256), 1)
    order = jnp.where(column == (row // 2 + (row % 2) * 128), 1.0, 0.0).astype(low_type)
    for part in range(rows // 128):
        both = jnp.concatenate(
            [key_ref[0, pl.ds(part * 128, 128)], value_ref[0, pl.ds(part * 128, 128)]], 0
        )
        table_ref[pl.ds(part * 256, 256), :] = dot_rows(order, both).astype(low_type)


def interleave(memory_keys, memory_values):
    heads, rows, width = memory_keys.shape
    step = min(2048, rows)
    spec = pl.BlockSpec((1, step, width), lambda h, i: (h, i, 0))
    return pl.pallas_call(
        interleave_kernel,
        grid=(heads, rows // step),
        in_specs=[spec, spec],
        out_specs=pl.BlockSpec((2 * step, width), lambda h, i: (h * (rows // step) + i, 0)),
        out_shape=jax.ShapeDtypeStruct((heads * rows * 2, width), low_type),
        cost_estimate=pl.CostEstimate(
            flops=heads * rows * 4 * 256 * width,
            bytes_accessed=heads * rows * width * 8,
            transcendentals=0,
        ),
        name="interleave",
    )(memory_keys, memory_values).reshape(heads, rows, 2, width)


def gather_kernel(
    index_hbm, table_hbm, found_ref, table_ref, table_sems, index_a, index_b, index_sems
):
    heads = pl.num_programs(0)
    head = pl.program_id(0)
    step = head * pl.num_programs(1) + pl.program_id(1)
    steps = heads * pl.num_programs(1)
    chunk = found_ref.shape[0] // 2
    rows = table_ref.shape[0] // table_sems.shape[0]
    slots = (index_a, index_b)

    def index_copy(number, slot):
        return pltpu.make_async_copy(index_hbm.at[number], slots[slot], index_sems.at[slot])

    def table_copy(number):
        where = pl.ds(number * rows, rows)
        return pltpu.make_async_copy(
            table_hbm.at[where], table_ref.at[where], table_sems.at[number]
        )

    @pl.when(step == 0)
    def start_all():
        index_copy(0, 0).start()
        index_copy(1, 1).start()
        for number in range(table_sems.shape[0]):
            table_copy(number).start()

    @pl.when(pl.program_id(1) == 0)
    def wait_table():
        table_copy(head).wait()

    following = jnp.minimum(step + 1, steps - 1)
    for slot in range(2):
        index_copy(2 * step + slot, slot).wait()
        picked = slots[slot]
        for start in range(0, chunk, 8):
            rows_now = [
                table_ref[picked[(start + j) // 128, (start + j) % 128]] for j in range(8)
            ]
            for j in range(8):
                found_ref[slot * chunk + start + j] = rows_now[j]
        index_copy(2 * following + slot, slot).start()

    @pl.when(step == steps - 1)
    def drain():
        index_copy(2 * following, 0).wait()
        index_copy(2 * following + 1, 1).wait()


def gather_found(index_rows, table):
    heads, rows, unused, width = table.shape
    total = index_rows.size // heads
    chunk = min(4096, total // 2)
    blocks = total // (2 * chunk)
    return pl.pallas_call(
        gather_kernel,
        grid=(heads, blocks),
        in_specs=[pl.BlockSpec(memory_space=pl.ANY), pl.BlockSpec(memory_space=pl.ANY)],
        out_specs=pl.BlockSpec((2 * chunk, 2, width), lambda h, i: (h * blocks + i, 0, 0)),
        out_shape=jax.ShapeDtypeStruct((heads * total, 2, width), low_type),
        scratch_shapes=[
            pltpu.VMEM((heads * rows, 2, width), low_type),
            pltpu.SemaphoreType.DMA((heads,)),
            pltpu.SMEM((chunk // 128, 128), jnp.int32),
            pltpu.SMEM((chunk // 128, 128), jnp.int32),
            pltpu.SemaphoreType.DMA((2,)),
        ],
        compiler_params=pltpu.CompilerParams(vmem_limit_bytes=vmem_most),
        cost_estimate=pl.CostEstimate(
            flops=0, bytes_accessed=4 * heads * total * width * 4, transcendentals=0
        ),
        name="gather_found",
    )(index_rows.reshape(-1, chunk // 128, 128), table.reshape(heads * rows, 2, width))


def own_columns(picks):
    shape = (8, 8 * picks * 2)
    lane = lax.broadcasted_iota(jnp.int32, shape, 1)
    row = lax.broadcasted_iota(jnp.int32, shape, 0)
    return jnp.logical_and(lane // (2 * picks) == row, lane % 2 == 0)


def recall_kernel(picks, scale, found_ref, query_ref, read_ref):
    tokens = query_ref.shape[0]
    wide = 8 * picks * 2
    own = own_columns(picks)
    groups = range(tokens // 8)
    scores = [
        dot_inner(query_ref[pl.ds(g * 8, 8), :], found_ref[pl.ds(g * wide, wide), :])
        for g in groups
    ]
    for g in groups:
        masked = jnp.where(own, scores[g] * (scale * log2_e), -jnp.inf)
        exponent = jnp.exp2(masked - jnp.max(masked, 1, keepdims=True))
        total = jnp.sum(exponent, 1, keepdims=True)
        shifted = pltpu.roll(exponent, 1, 1).astype(low_type)
        read_ref[pl.ds(g * 8, 8), :] = (
            dot_rows(shifted, found_ref[pl.ds(g * wide, wide), :]) / total
        )


def recall(found, queries, heads, picks, scale):
    tokens = queries.shape[0]
    width = queries.shape[1] // (3 * heads)
    step = min(512, tokens)
    blocks = tokens // step
    return pl.pallas_call(
        functools.partial(recall_kernel, picks, scale),
        grid=(heads, blocks),
        in_specs=[
            pl.BlockSpec((step * picks * 2, width), lambda h, i: (h * blocks + i, 0)),
            pl.BlockSpec((step, width), lambda h, i: (i, h)),
        ],
        out_specs=pl.BlockSpec((step, width), lambda h, i: (i, h)),
        out_shape=jax.ShapeDtypeStruct((tokens, heads * width), full_type),
        compiler_params=pltpu.CompilerParams(vmem_limit_bytes=vmem_most),
        cost_estimate=pl.CostEstimate(
            flops=0, bytes_accessed=heads * tokens * picks * width * 8, transcendentals=0
        ),
        name="recall",
    )(found, queries)


def recall_back_kernel(
    picks, scale, gate_ref, found_ref, query_ref, delta_ref, query_delta_ref, sums_ref
):
    tokens = query_ref.shape[0]
    wide = 8 * picks * 2
    own = own_columns(picks)
    gate = gate_ref[pl.program_id(0)]
    groups = range(tokens // 8)
    both = []
    for g in groups:
        rows = jnp.concatenate(
            [query_ref[pl.ds(g * 8, 8), :], delta_ref[pl.ds(g * 8, 8), :]], 0
        )
        both.append(dot_inner(rows, found_ref[pl.ds(g * wide, wide), :]))
    gained = jnp.zeros((8, 1), full_type)
    for g in groups:
        masked = jnp.where(own, both[g][:8] * (scale * log2_e), -jnp.inf)
        exponent = jnp.exp2(masked - jnp.max(masked, 1, keepdims=True))
        weights = exponent / jnp.sum(exponent, 1, keepdims=True)
        reads = pltpu.roll(both[g][8:], wide - 1, 1)
        expected = jnp.sum(weights * reads, 1, keepdims=True)
        gained = gained + expected
        score_delta = (weights * (reads - expected)).astype(low_type)
        query_delta_ref[pl.ds(g * 8, 8), :] = dot_rows(
            score_delta, found_ref[pl.ds(g * wide, wide), :]
        ) * (scale * gate)

    @pl.when(pl.program_id(1) == 0)
    def clear():
        sums_ref[...] = jnp.zeros(sums_ref.shape, full_type)

    sums_ref[0] += jnp.broadcast_to(gained, (8, 128))


def recall_back(found, queries, mixed_delta, gates, heads, picks, scale):
    tokens = queries.shape[0]
    width = mixed_delta.shape[1] // heads
    step = min(512, tokens)
    blocks = tokens // step
    rows_spec = pl.BlockSpec((step, width), lambda h, i: (i, h))
    return pl.pallas_call(
        functools.partial(recall_back_kernel, picks, scale),
        grid=(heads, blocks),
        in_specs=[
            pl.BlockSpec(memory_space=pltpu.SMEM),
            pl.BlockSpec((step * picks * 2, width), lambda h, i: (h * blocks + i, 0)),
            rows_spec,
            rows_spec,
        ],
        out_specs=[rows_spec, pl.BlockSpec((1, 8, 128), lambda h, i: (h, 0, 0))],
        out_shape=[
            jax.ShapeDtypeStruct((tokens, heads * width), full_type),
            jax.ShapeDtypeStruct((heads, 8, 128), full_type),
        ],
        compiler_params=pltpu.CompilerParams(vmem_limit_bytes=vmem_most),
        cost_estimate=pl.CostEstimate(
            flops=0, bytes_accessed=heads * tokens * picks * width * 8, transcendentals=0
        ),
        name="recall_back",
    )(gates, found, queries, mixed_delta)


def band(column_ref):
    wide = jnp.broadcast_to(column_ref[0], (tile, ring))
    return pltpu.roll(wide, 0, 1, stride=1, stride_axis=0)[:, :span]


def local_kernel(
    scale, gate_ref, far_ref, column_ref, query_ref, key_ref, value_ref, query_mask_ref,
    key_mask_ref, recall_ref, mixed_ref, bias_ref,
):
    head = pl.program_id(0)

    @pl.when(pl.program_id(1) == 0)
    def make_band():
        bias_ref[...] = band(column_ref)

    gate = gate_ref[head]
    count = query_ref.shape[0] // tile
    at = [pl.ds(t * tile, tile) for t in range(count)]
    keys = [jnp.concatenate([key_ref[a, :], key_mask_ref[0, a, :]], 1) for a in at]
    for t in range(count):
        rows = jnp.concatenate([query_ref[at[t], :], query_mask_ref[0, at[t], :]], 1)
        parts = []
        for j in range(count):
            step = j - t
            if step < -1:
                bias = far_ref[head, 0]
            elif step > 1:
                bias = far_ref[head, 1]
            else:
                bias = bias_ref[:, pl.ds((step + 1) * tile, tile)]
            parts.append(dot_inner(rows, keys[j]) * (scale * log2_e) + bias)
        top = jnp.max(functools.reduce(jnp.maximum, parts), 1, keepdims=True)
        parts = [jnp.exp2(part - top) for part in parts]
        total = jnp.sum(functools.reduce(jnp.add, parts), 1, keepdims=True)
        read = sum(dot_rows(parts[j].astype(low_type), value_ref[at[j], :]) for j in range(count))
        mixed_ref[at[t], :] = (
            gate * recall_ref[at[t], :] + ((1.0 - gate) / total) * read
        ).astype(low_type)


def local_read(projected, query_mask, key_mask, recalled, columns, far, gates, seq_len, scale):
    tokens = recalled.shape[0]
    heads = gates.shape[0]
    width = recalled.shape[1] // heads

    def rows_of(shift):
        return pl.BlockSpec((seq_len, width), lambda h, s: (s, h + shift * heads))

    mask_spec = pl.BlockSpec((1, seq_len, 128), lambda h, s: (s, 0, 0))
    smem = pl.BlockSpec(memory_space=pltpu.SMEM)
    return pl.pallas_call(
        functools.partial(local_kernel, scale),
        grid=(heads, tokens // seq_len),
        in_specs=[
            smem,
            smem,
            pl.BlockSpec((1, 1, ring), lambda h, s: (h, 0, 0)),
            rows_of(0),
            rows_of(1),
            rows_of(2),
            mask_spec,
            mask_spec,
            rows_of(0),
        ],
        out_specs=rows_of(0),
        out_shape=jax.ShapeDtypeStruct((tokens, heads * width), low_type),
        scratch_shapes=[pltpu.VMEM((tile, span), full_type)],
        compiler_params=pltpu.CompilerParams(vmem_limit_bytes=vmem_most),
        cost_estimate=pl.CostEstimate(
            flops=0, bytes_accessed=heads * tokens * seq_len * 20, transcendentals=0
        ),
        name="local_read",
    )(gates, far, columns, projected, projected, projected, query_mask, key_mask, recalled)


def local_back_kernel(
    scale, gate_ref, far_ref, column_ref, query_ref, key_ref, value_ref, query_mask_ref,
    key_mask_ref, delta_ref, recall_delta_ref, query_delta_ref, key_delta_ref, value_delta_ref,
    diagonal_ref, sums_ref, bias_ref, near_ref, key_sum_ref, value_sum_ref,
):
    head = pl.program_id(0)
    last = pl.program_id(1) == pl.num_programs(1) - 1

    @pl.when(pl.program_id(1) == 0)
    def make_band():
        bias_ref[...] = band(column_ref)
        near_ref[...] = jnp.zeros(near_ref.shape, full_type)
        sums_ref[...] = jnp.zeros(sums_ref.shape, full_type)

    gate = gate_ref[head]
    count = query_ref.shape[0] // tile
    at = [pl.ds(t * tile, tile) for t in range(count)]
    keys = [jnp.concatenate([key_ref[a, :], key_mask_ref[0, a, :]], 1) for a in at]
    turned = [key_ref[a, :].astype(full_type).T.astype(low_type) for a in at]
    gained = jnp.zeros((1, tile), full_type)
    far_sums = [jnp.zeros((8, tile), full_type) for side in range(2)]
    for t in range(count):
        rows = jnp.concatenate([query_ref[at[t], :], query_mask_ref[0, at[t], :]], 1)
        delta = ((1.0 - gate) * delta_ref[at[t], :].astype(full_type)).astype(low_type)
        parts = []
        for j in range(count):
            step = j - t
            if step < -1:
                bias = far_ref[head, 0]
            elif step > 1:
                bias = far_ref[head, 1]
            else:
                bias = bias_ref[:, pl.ds((1 - step) * tile, tile)]
            parts.append(dot_inner(keys[j], rows) * (scale * log2_e) + bias)
        top = jnp.max(functools.reduce(jnp.maximum, parts), 0, keepdims=True)
        parts = [jnp.exp2(part - top) for part in parts]
        total = jnp.sum(functools.reduce(jnp.add, parts), 0, keepdims=True)
        inverse = 1.0 / total
        parts = [part * inverse for part in parts]
        moves = [dot_inner(value_ref[at[j], :], delta) for j in range(count)]
        expected = jnp.sum(
            functools.reduce(jnp.add, [parts[j] * moves[j] for j in range(count)]),
            0,
            keepdims=True,
        )
        gained = gained + expected
        query_sum = None
        for j in range(count):
            step = j - t
            score_delta = parts[j] * (moves[j] - expected)
            if abs(step) > 1:
                side = 0 if step < 0 else 1
                far_sums[side] = far_sums[side] + jnp.sum(
                    score_delta.reshape(tile // 8, 8, tile), 0
                )
            else:
                near_ref[:, pl.ds((1 - step) * tile, tile)] += score_delta
            low_delta = score_delta.astype(low_type)
            value_part = dot_rows(parts[j].astype(low_type), delta)
            key_part = dot_rows(low_delta, query_ref[at[t], :])
            query_part = dot_rows(turned[j], low_delta)
            if t == 0:
                value_sum_ref[at[j], :] = value_part
                key_sum_ref[at[j], :] = key_part
            else:
                value_sum_ref[at[j], :] += value_part
                key_sum_ref[at[j], :] += key_part
            query_sum = query_part if j == 0 else query_sum + query_part
        query_delta_ref[at[t], :] = (
            query_sum.T * scale + recall_delta_ref[at[t], :]
        ).astype(low_type)
    key_delta_ref[...] = (key_sum_ref[...] * scale).astype(low_type)
    value_delta_ref[...] = value_sum_ref[...].astype(low_type)
    sums_ref[0, 0:1] += gained
    sums_ref[0, 8:16] += far_sums[0]
    sums_ref[0, 16:24] += far_sums[1]

    @pl.when(last)
    def fold_diagonals():
        total = jnp.zeros((8, ring), full_type)
        for g in range(tile // 8):
            part = jnp.concatenate(
                [near_ref[pl.ds(g * 8, 8), :], jnp.zeros((8, ring - span), full_type)], 1
            )
            total = total + (pltpu.roll(part, ring - 8 * g, 1) if g else part)
        row = lax.broadcasted_iota(jnp.int32, (8, ring), 0)
        for bit in (1, 2, 4):
            total = jnp.where((row & bit) != 0, pltpu.roll(total, ring - bit, 1), total)
        diagonal_ref[0] = total


def local_back(
    projected, query_mask, key_mask, mixed_delta, recall_delta, columns, far, gates, seq_len, scale
):
    tokens = mixed_delta.shape[0]
    heads = gates.shape[0]
    width = mixed_delta.shape[1] // heads

    def rows_of(shift):
        return pl.BlockSpec((seq_len, width), lambda h, s: (s, h + shift * heads))

    mask_spec = pl.BlockSpec((1, seq_len, 128), lambda h, s: (s, 0, 0))
    smem = pl.BlockSpec(memory_space=pltpu.SMEM)
    rows_shape = jax.ShapeDtypeStruct((tokens, heads * width), low_type)
    return pl.pallas_call(
        functools.partial(local_back_kernel, scale),
        grid=(heads, tokens // seq_len),
        in_specs=[
            smem,
            smem,
            pl.BlockSpec((1, 1, ring), lambda h, s: (h, 0, 0)),
            rows_of(0),
            rows_of(1),
            rows_of(2),
            mask_spec,
            mask_spec,
            rows_of(0),
            rows_of(0),
        ],
        out_specs=[
            rows_of(0),
            rows_of(0),
            rows_of(0),
            pl.BlockSpec((1, 8, ring), lambda h, s: (h, 0, 0)),
            pl.BlockSpec((1, 24, tile), lambda h, s: (h, 0, 0)),
        ],
        out_shape=[
            rows_shape,
            rows_shape,
            rows_shape,
            jax.ShapeDtypeStruct((heads, 8, ring), full_type),
            jax.ShapeDtypeStruct((heads, 24, tile), full_type),
        ],
        scratch_shapes=[
            pltpu.VMEM((tile, span), full_type),
            pltpu.VMEM((tile, span), full_type),
            pltpu.VMEM((seq_len, width), full_type),
            pltpu.VMEM((seq_len, width), full_type),
        ],
        compiler_params=pltpu.CompilerParams(vmem_limit_bytes=vmem_most),
        cost_estimate=pl.CostEstimate(
            flops=0, bytes_accessed=heads * tokens * seq_len * 40, transcendentals=0
        ),
        name="local_back",
    )(
        gates, far, columns, projected, projected, projected, query_mask, key_mask, mixed_delta,
        recall_delta,
    )


def mask_rows(block_ids):
    level = jnp.arange(128, dtype=jnp.int32)
    gap = block_ids[:, :, None] - level
    query_mask = jnp.where((gap >= 0) & (gap <= 1), 0.0, mask_gap).astype(low_type)
    key_mask = (gap == 0).astype(low_type)
    return query_mask, key_mask


def fetch(rows):
    group = lax.axis_size("tensor")
    return [rows] + [
        lax.ppermute(rows, "tensor", [((i + k) % group, i) for i in range(group)])
        for k in range(1, group)
    ]


def in_order(shares):
    group = lax.axis_size("tensor")
    rows = shares[0].shape[0]
    whole = jnp.zeros((group * rows,) + shares[0].shape[1:], shares[0].dtype)
    for k in range(group):
        start = ((lax.axis_index("tensor") + k) % group) * rows
        whole = lax.dynamic_update_slice_in_dim(whole, shares[k], start, 0)
    return whole


def share_of(whole, k, rows):
    start = ((lax.axis_index("tensor") + k) % lax.axis_size("tensor")) * rows
    return lax.dynamic_slice_in_dim(whole, start, rows, 0)


def fold(term, piece):
    group = lax.axis_size("tensor")
    sent = [
        lax.ppermute(
            term(piece(k)).astype(low_type), "tensor", [(i, (i + k) % group) for i in range(group)]
        )
        for k in range(1, group)
    ]
    return sum((part.astype(full_type) for part in sent), term(piece(0)))


def body(
    tokens,
    block_ids,
    memory_index,
    memory_keys,
    memory_values,
    attn_gain,
    query_weight,
    key_weight,
    value_weight,
    output_weight,
    position_table,
    memory_gate,
    mlp_gain,
    hidden_weight,
    return_weight,
    grad_output,
):
    share_rows = tokens.shape[0]
    seq_len = block_ids.shape[1]
    head_count, memory_rows, head_width = memory_keys.shape
    picks = memory_index.shape[2]
    inner_width = head_count * head_width
    scale = head_width ** (-0.5)

    offsets = jnp.arange(head_count, dtype=jnp.int32) * memory_rows
    index_rows = memory_index.transpose(1, 0, 2) + offsets[:, None, None]
    found = gather_found(index_rows, interleave(memory_keys, memory_values))
    found = found.reshape(-1, head_width)

    token_full = tokens.astype(full_type)
    normed_rows = rms_scaled(token_full, attn_gain).astype(low_type)
    normed = lax.all_gather(normed_rows, "tensor", axis=0, tiled=True)
    joined = jnp.concatenate([query_weight, key_weight, value_weight], 1)
    projected = dot_rows(normed, joined).astype(low_type)

    query_mask, key_mask = mask_rows(block_ids)
    place = jnp.arange(ring, dtype=jnp.int32)
    place = jnp.where(place < span, place, place - ring)
    ahead = bucket_of(place - tile)
    behind = bucket_of(tile - place)
    level = jnp.arange(32, dtype=jnp.int32)
    ahead_hot = (ahead[:, None] == level).astype(full_type)
    behind_hot = (behind[:, None] == level).astype(full_type)
    scaled_table = position_table * log2_e
    ahead_columns = jnp.dot(ahead_hot, scaled_table, precision=exact_mode).T[:, None, :]
    behind_columns = jnp.dot(behind_hot, scaled_table, precision=exact_mode).T[:, None, :]
    far = jnp.stack([scaled_table[15], scaled_table[31]], 1)
    gates = jax.nn.sigmoid(memory_gate)

    recalled = recall(found, projected, head_count, picks, scale)
    mixed_rows = local_read(
        projected, query_mask, key_mask, recalled, ahead_columns, far, gates, seq_len, scale
    )
    middle = token_full + fold(
        lambda rows: dot_rows(rows, output_weight), lambda k: share_of(mixed_rows, k, share_rows)
    )
    second_rows = rms_scaled(middle, mlp_gain).astype(low_type)
    grad_full = jnp.concatenate(fetch(grad_output), 0)
    second = jnp.concatenate(fetch(second_rows), 0)
    hidden = dot_rows(second, hidden_weight)
    active = jax.nn.gelu(hidden).astype(low_type)
    return_low = dot_outer(active, grad_full).astype(low_type)
    return_sum = lax.psum(return_low, "dp")
    active_delta = dot_inner(grad_full, return_weight)
    gelu_back = jax.vjp(jax.nn.gelu, hidden)[1]
    hidden_delta = gelu_back(active_delta)[0].astype(low_type)
    second_delta = fold(
        lambda rows: dot_inner(rows, hidden_weight),
        lambda k: lax.slice_in_dim(hidden_delta, k * share_rows, (k + 1) * share_rows),
    )
    hidden_low = dot_outer(second, hidden_delta).astype(low_type)
    hidden_low, return_sum = lax.optimization_barrier((hidden_low, return_sum))
    hidden_sum = lax.psum(hidden_low, "dp")
    second_back = jax.vjp(rms_scaled, middle, mlp_gain)[1]
    middle_part, mlp_gain_part = second_back(second_delta)
    middle_delta = grad_output.astype(full_type) + middle_part
    middle_full = in_order(fetch(middle_delta.astype(low_type)))
    mixed_delta = dot_inner(middle_full, output_weight).astype(low_type)
    layer_output = (
        middle
        + fold(
            lambda rows: dot_rows(rows, return_weight),
            lambda k: lax.slice_in_dim(active, k * share_rows, (k + 1) * share_rows),
        )
    ).astype(low_type)

    recall_delta, recall_sums = recall_back(
        found, projected, mixed_delta, gates, head_count, picks, scale
    )
    query_delta, key_delta, value_delta, diagonals, local_sums = local_back(
        projected, query_mask, key_mask, mixed_delta, recall_delta, behind_columns, far, gates,
        seq_len, scale,
    )
    output_part = dot_outer(mixed_rows, middle_full)
    recall_gain = jnp.sum(recall_sums[:, :, 0], 1)
    local_gain = jnp.sum(local_sums[:, 0], 1)
    gate_part = gates * (1.0 - gates) * recall_gain - gates * local_gain
    diagonal_sums = jnp.sum(diagonals, 1)
    table_part = jnp.dot(diagonal_sums, behind_hot, precision=exact_mode)
    far_left = jnp.sum(local_sums[:, 8:16], (1, 2))
    far_right = jnp.sum(local_sums[:, 16:24], (1, 2))
    table_part = table_part + far_left[:, None] * (level == 15) + far_right[:, None] * (level == 31)

    project_delta = jnp.concatenate([query_delta, key_delta, value_delta], 1)
    joined_part = dot_outer(normed, project_delta)
    attn_gain_part = jnp.sum(joined_part * joined.astype(full_type), 1) / attn_gain
    model_width = tokens.shape[1]
    small = jnp.concatenate([table_part.reshape(-1), gate_part])
    small = jnp.pad(small, (0, model_width - small.shape[0]))
    extra = jnp.stack([attn_gain_part, mlp_gain_part, small])
    extra = jnp.pad(extra, ((0, 13), (0, 0)))
    last_low = (
        jnp.concatenate([output_part, extra], 0).astype(low_type),
        joined_part.astype(low_type),
    )
    last_low, hidden_sum = lax.optimization_barrier((last_low, hidden_sum))
    output_sum, joined_sum = lax.psum(last_low, "dp")

    normed_delta = fold(
        lambda rows: dot_inner(rows, joined), lambda k: share_of(project_delta, k, share_rows)
    )
    first_back = jax.vjp(rms_scaled, token_full, attn_gain)[1]
    tokens_grad = (middle_delta + first_back(normed_delta)[0]).astype(low_type)

    joined_grad = joined_sum.astype(full_type)
    output_grad = output_sum.astype(full_type)
    gains = sum(fetch(output_grad[inner_width : inner_width + 2]))
    small_sum = output_grad[inner_width + 2]
    table_size = head_count * 32
    return (
        layer_output,
        tokens_grad,
        gains[0],
        joined_grad[:, :inner_width],
        joined_grad[:, inner_width : 2 * inner_width],
        joined_grad[:, 2 * inner_width :],
        output_grad[:inner_width],
        small_sum[:table_size].reshape(head_count, 32).T,
        small_sum[table_size : table_size + head_count],
        gains[1],
        hidden_sum.astype(full_type),
        return_sum.astype(full_type),
    )


def solution(mesh):
    def run(*arrays):
        with jax.sharding.use_abstract_mesh(mesh.abstract_mesh):
            return jax.shard_map(
                body,
                mesh=mesh,
                in_specs=(
                    P(("dp", "tensor"), None),
                    P("dp", None),
                    P("dp", "tensor", None),
                    P("tensor", None, None),
                    P("tensor", None, None),
                    P(),
                    P(None, "tensor"),
                    P(None, "tensor"),
                    P(None, "tensor"),
                    P("tensor", None),
                    P(None, "tensor"),
                    P("tensor"),
                    P(),
                    P(None, "tensor"),
                    P("tensor", None),
                    P(("dp", "tensor"), None),
                ),
                out_specs=(
                    P(("dp", "tensor"), None),
                    P(("dp", "tensor"), None),
                    P(),
                    P(None, "tensor"),
                    P(None, "tensor"),
                    P(None, "tensor"),
                    P("tensor", None),
                    P(None, "tensor"),
                    P("tensor"),
                    P(),
                    P(None, "tensor"),
                    P("tensor", None),
                ),
                check_vma=False,
            )(*arrays)

    return run
```

```python
import functools
import math

import jax
import jax.numpy as jnp
from jax import lax
from jax.experimental import pallas as pl
from jax.experimental.pallas import tpu as pltpu
from jax.sharding import PartitionSpec as P

eps_norm = 1e-06
far_steps = (12, 16, 23, 32, 46, 64, 91)
exact_mode = lax.Precision.HIGHEST
low_type = jnp.bfloat16
full_type = jnp.float32
log2_e = math.log2(math.e)
tile = 256
span = 3 * tile
ring = 1024
mask_gap = -(2.0**100)
vmem_most = 60 * 2**20


def bucket_of(relative):
    upper_half = jnp.where(relative > 0, 16, 0).astype(jnp.int32)
    distance = jnp.abs(relative)
    far_bucket = 8 + sum(((distance >= step_size).astype(jnp.int32) for step_size in far_steps))
    return upper_half + jnp.where(distance < 8, distance, far_bucket)


def rms_scaled(rows, gain):
    return rows * lax.rsqrt(jnp.mean(rows * rows, -1, keepdims=True) + eps_norm) * gain


def dot_rows(left, right):
    return jnp.dot(left, right, preferred_element_type=full_type)


def dot_outer(left, right):
    return lax.dot_general(
        left, right, (((0,), (0,)), ((), ())), preferred_element_type=full_type
    )


def dot_inner(left, right):
    return lax.dot_general(
        left, right, (((1,), (1,)), ((), ())), preferred_element_type=full_type
    )


def interleave_kernel(key_ref, value_ref, table_ref):
    rows = key_ref.shape[1]
    row = lax.broadcasted_iota(jnp.int32, (256, 256), 0)
    column = lax.broadcasted_iota(jnp.int32, (256, 256), 1)
    order = jnp.where(column == (row // 2 + (row % 2) * 128), 1.0, 0.0).astype(low_type)
    for part in range(rows // 128):
        both = jnp.concatenate(
            [key_ref[0, pl.ds(part * 128, 128)], value_ref[0, pl.ds(part * 128, 128)]], 0
        )
        table_ref[pl.ds(part * 256, 256), :] = dot_rows(order, both).astype(low_type)


def interleave(memory_keys, memory_values):
    heads, rows, width = memory_keys.shape
    step = min(2048, rows)
    spec = pl.BlockSpec((1, step, width), lambda h, i: (h, i, 0))
    return pl.pallas_call(
        interleave_kernel,
        grid=(heads, rows // step),
        in_specs=[spec, spec],
        out_specs=pl.BlockSpec((2 * step, width), lambda h, i: (h * (rows // step) + i, 0)),
        out_shape=jax.ShapeDtypeStruct((heads * rows * 2, width), low_type),
        cost_estimate=pl.CostEstimate(
            flops=heads * rows * 4 * 256 * width,
            bytes_accessed=heads * rows * width * 8,
            transcendentals=0,
        ),
        name="interleave",
    )(memory_keys, memory_values).reshape(heads, rows, 2, width)


def gather_kernel(
    index_hbm, table_hbm, found_ref, table_ref, table_sems, index_a, index_b, index_sems
):
    heads = pl.num_programs(0)
    head = pl.program_id(0)
    step = head * pl.num_programs(1) + pl.program_id(1)
    steps = heads * pl.num_programs(1)
    chunk = found_ref.shape[0] // 2
    rows = table_ref.shape[0] // table_sems.shape[0]
    slots = (index_a, index_b)

    def index_copy(number, slot):
        return pltpu.make_async_copy(index_hbm.at[number], slots[slot], index_sems.at[slot])

    def table_copy(number):
        where = pl.ds(number * rows, rows)
        return pltpu.make_async_copy(
            table_hbm.at[where], table_ref.at[where], table_sems.at[number]
        )

    @pl.when(step == 0)
    def start_all():
        index_copy(0, 0).start()
        index_copy(1, 1).start()
        for number in range(table_sems.shape[0]):
            table_copy(number).start()

    @pl.when(pl.program_id(1) == 0)
    def wait_table():
        table_copy(head).wait()

    following = jnp.minimum(step + 1, steps - 1)
    for slot in range(2):
        index_copy(2 * step + slot, slot).wait()
        picked = slots[slot]
        for start in range(0, chunk, 8):
            rows_now = [
                table_ref[picked[(start + j) // 128, (start + j) % 128]] for j in range(8)
            ]
            for j in range(8):
                found_ref[slot * chunk + start + j] = rows_now[j]
        index_copy(2 * following + slot, slot).start()

    @pl.when(step == steps - 1)
    def drain():
        index_copy(2 * following, 0).wait()
        index_copy(2 * following + 1, 1).wait()


def gather_found(index_rows, table):
    heads, rows, unused, width = table.shape
    total = index_rows.size // heads
    chunk = min(4096, total // 2)
    blocks = total // (2 * chunk)
    return pl.pallas_call(
        gather_kernel,
        grid=(heads, blocks),
        in_specs=[pl.BlockSpec(memory_space=pl.ANY), pl.BlockSpec(memory_space=pl.ANY)],
        out_specs=pl.BlockSpec((2 * chunk, 2, width), lambda h, i: (h * blocks + i, 0, 0)),
        out_shape=jax.ShapeDtypeStruct((heads * total, 2, width), low_type),
        scratch_shapes=[
            pltpu.VMEM((heads * rows, 2, width), low_type),
            pltpu.SemaphoreType.DMA((heads,)),
            pltpu.SMEM((chunk // 128, 128), jnp.int32),
            pltpu.SMEM((chunk // 128, 128), jnp.int32),
            pltpu.SemaphoreType.DMA((2,)),
        ],
        compiler_params=pltpu.CompilerParams(vmem_limit_bytes=vmem_most),
        cost_estimate=pl.CostEstimate(
            flops=0, bytes_accessed=4 * heads * total * width * 4, transcendentals=0
        ),
        name="gather_found",
    )(index_rows.reshape(-1, chunk // 128, 128), table.reshape(heads * rows, 2, width))


def own_columns(picks):
    shape = (8, 8 * picks * 2)
    lane = lax.broadcasted_iota(jnp.int32, shape, 1)
    row = lax.broadcasted_iota(jnp.int32, shape, 0)
    return jnp.logical_and(lane // (2 * picks) == row, lane % 2 == 0)


def recall_kernel(picks, scale, found_ref, query_ref, read_ref):
    tokens = query_ref.shape[0]
    wide = 8 * picks * 2
    own = own_columns(picks)
    groups = range(tokens // 8)
    scores = [
        dot_inner(query_ref[pl.ds(g * 8, 8), :], found_ref[pl.ds(g * wide, wide), :])
        for g in groups
    ]
    for g in groups:
        masked = jnp.where(own, scores[g] * (scale * log2_e), -jnp.inf)
        exponent = jnp.exp2(masked - jnp.max(masked, 1, keepdims=True))
        total = jnp.sum(exponent, 1, keepdims=True)
        shifted = pltpu.roll(exponent, 1, 1).astype(low_type)
        read_ref[pl.ds(g * 8, 8), :] = (
            dot_rows(shifted, found_ref[pl.ds(g * wide, wide), :]) / total
        )


def recall(found, queries, heads, picks, scale):
    tokens = queries.shape[0]
    width = queries.shape[1] // (3 * heads)
    step = min(512, tokens)
    blocks = tokens // step
    return pl.pallas_call(
        functools.partial(recall_kernel, picks, scale),
        grid=(heads, blocks),
        in_specs=[
            pl.BlockSpec((step * picks * 2, width), lambda h, i: (h * blocks + i, 0)),
            pl.BlockSpec((step, width), lambda h, i: (i, h)),
        ],
        out_specs=pl.BlockSpec((step, width), lambda h, i: (i, h)),
        out_shape=jax.ShapeDtypeStruct((tokens, heads * width), full_type),
        compiler_params=pltpu.CompilerParams(vmem_limit_bytes=vmem_most),
        cost_estimate=pl.CostEstimate(
            flops=0, bytes_accessed=heads * tokens * picks * width * 8, transcendentals=0
        ),
        name="recall",
    )(found, queries)


def recall_back_kernel(
    picks, scale, gate_ref, found_ref, query_ref, delta_ref, query_delta_ref, sums_ref
):
    tokens = query_ref.shape[0]
    wide = 8 * picks * 2
    own = own_columns(picks)
    gate = gate_ref[0]
    groups = range(tokens // 8)
    both = []
    for g in groups:
        rows = jnp.concatenate(
            [query_ref[pl.ds(g * 8, 8), :], delta_ref[pl.ds(g * 8, 8), :]], 0
        )
        both.append(dot_inner(rows, found_ref[pl.ds(g * wide, wide), :]))
    gained = jnp.zeros((8, 1), full_type)
    for g in groups:
        masked = jnp.where(own, both[g][:8] * (scale * log2_e), -jnp.inf)
        exponent = jnp.exp2(masked - jnp.max(masked, 1, keepdims=True))
        weights = exponent / jnp.sum(exponent, 1, keepdims=True)
        reads = pltpu.roll(both[g][8:], wide - 1, 1)
        expected = jnp.sum(weights * reads, 1, keepdims=True)
        gained = gained + expected
        score_delta = (weights * (reads - expected)).astype(low_type)
        query_delta_ref[pl.ds(g * 8, 8), :] = dot_rows(
            score_delta, found_ref[pl.ds(g * wide, wide), :]
        ) * (scale * gate)

    @pl.when(pl.program_id(0) == 0)
    def clear():
        sums_ref[...] = jnp.zeros(sums_ref.shape, full_type)

    sums_ref[0] += jnp.broadcast_to(gained, (8, 128))


def recall_back(found, queries, mixed_delta, gates, head, carried, kept, heads, picks, scale):
    tokens = queries.shape[0]
    width = mixed_delta.shape[1] // heads
    step = min(512, tokens)
    blocks = tokens // step
    rows_spec = pl.BlockSpec((step, width), lambda i: (i, head))
    anywhere = pl.BlockSpec(memory_space=pl.ANY)
    extra = [kept] if kept is not None else []
    first = 4 + len(extra)

    def kernel(gate_ref, found_ref, query_ref, delta_ref, *rest):
        query_delta_ref, sums_ref = rest[len(extra) + len(carried) :][:2]
        recall_back_kernel(
            picks, scale, gate_ref, found_ref, query_ref, delta_ref, query_delta_ref, sums_ref
        )

    out = pl.pallas_call(
        kernel,
        grid=(blocks,),
        in_specs=[
            pl.BlockSpec(memory_space=pltpu.SMEM),
            pl.BlockSpec((step * picks * 2, width), lambda i: (head * blocks + i, 0)),
            rows_spec,
            rows_spec,
        ]
        + [anywhere] * (len(extra) + len(carried)),
        out_specs=[rows_spec, pl.BlockSpec((1, 8, 128), lambda i: (0, 0, 0))]
        + [anywhere] * len(carried),
        out_shape=[
            jax.ShapeDtypeStruct((tokens, heads * width), full_type),
            jax.ShapeDtypeStruct((1, 8, 128), full_type),
        ]
        + [jax.ShapeDtypeStruct(part.shape, part.dtype) for part in carried],
        input_output_aliases=({4: 0} if extra else {})
        | {first + i: 2 + i for i in range(len(carried))},
        compiler_params=pltpu.CompilerParams(vmem_limit_bytes=vmem_most),
        cost_estimate=pl.CostEstimate(
            flops=0, bytes_accessed=tokens * picks * width * 8, transcendentals=0
        ),
        name="recall_back",
    )(gates[head : head + 1], found, queries, mixed_delta, *extra, *carried)
    return out[0], out[1], list(out[2:])


def band(column_ref):
    wide = jnp.broadcast_to(column_ref[0], (tile, ring))
    return pltpu.roll(wide, 0, 1, stride=1, stride_axis=0)[:, :span]


def local_kernel(
    scale, gate_ref, far_ref, column_ref, query_ref, key_ref, value_ref, query_mask_ref,
    key_mask_ref, recall_ref, mixed_ref, bias_ref,
):
    head = pl.program_id(0)

    @pl.when(pl.program_id(1) == 0)
    def make_band():
        bias_ref[...] = band(column_ref)

    gate = gate_ref[head]
    count = query_ref.shape[0] // tile
    at = [pl.ds(t * tile, tile) for t in range(count)]
    keys = [jnp.concatenate([key_ref[a, :], key_mask_ref[0, a, :]], 1) for a in at]
    for t in range(count):
        rows = jnp.concatenate([query_ref[at[t], :], query_mask_ref[0, at[t], :]], 1)
        parts = []
        for j in range(count):
            step = j - t
            if step < -1:
                bias = far_ref[head, 0]
            elif step > 1:
                bias = far_ref[head, 1]
            else:
                bias = bias_ref[:, pl.ds((step + 1) * tile, tile)]
            parts.append(dot_inner(rows, keys[j]) * (scale * log2_e) + bias)
        top = jnp.max(functools.reduce(jnp.maximum, parts), 1, keepdims=True)
        parts = [jnp.exp2(part - top) for part in parts]
        total = jnp.sum(functools.reduce(jnp.add, parts), 1, keepdims=True)
        read = sum(dot_rows(parts[j].astype(low_type), value_ref[at[j], :]) for j in range(count))
        mixed_ref[at[t], :] = (
            gate * recall_ref[at[t], :] + ((1.0 - gate) / total) * read
        ).astype(low_type)


def local_read(projected, query_mask, key_mask, recalled, columns, far, gates, seq_len, scale):
    tokens = recalled.shape[0]
    heads = gates.shape[0]
    width = recalled.shape[1] // heads

    def rows_of(shift):
        return pl.BlockSpec((seq_len, width), lambda h, s: (s, h + shift * heads))

    mask_spec = pl.BlockSpec((1, seq_len, 128), lambda h, s: (s, 0, 0))
    smem = pl.BlockSpec(memory_space=pltpu.SMEM)
    return pl.pallas_call(
        functools.partial(local_kernel, scale),
        grid=(heads, tokens // seq_len),
        in_specs=[
            smem,
            smem,
            pl.BlockSpec((1, 1, ring), lambda h, s: (h, 0, 0)),
            rows_of(0),
            rows_of(1),
            rows_of(2),
            mask_spec,
            mask_spec,
            rows_of(0),
        ],
        out_specs=rows_of(0),
        out_shape=jax.ShapeDtypeStruct((tokens, heads * width), low_type),
        scratch_shapes=[pltpu.VMEM((tile, span), full_type)],
        compiler_params=pltpu.CompilerParams(vmem_limit_bytes=vmem_most),
        cost_estimate=pl.CostEstimate(
            flops=0, bytes_accessed=heads * tokens * seq_len * 20, transcendentals=0
        ),
        name="local_read",
    )(gates, far, columns, projected, projected, projected, query_mask, key_mask, recalled)


def local_back_kernel(
    scale, gate_ref, far_ref, column_ref, query_ref, key_ref, value_ref, query_mask_ref,
    key_mask_ref, delta_ref, recall_delta_ref, query_delta_ref, key_delta_ref, value_delta_ref,
    diagonal_ref, sums_ref, bias_ref, near_ref, key_sum_ref, value_sum_ref,
):
    head = pl.program_id(0)
    last = pl.program_id(1) == pl.num_programs(1) - 1

    @pl.when(pl.program_id(1) == 0)
    def make_band():
        bias_ref[...] = band(column_ref)
        near_ref[...] = jnp.zeros(near_ref.shape, full_type)
        sums_ref[...] = jnp.zeros(sums_ref.shape, full_type)

    gate = gate_ref[head]
    count = query_ref.shape[0] // tile
    at = [pl.ds(t * tile, tile) for t in range(count)]
    keys = [jnp.concatenate([key_ref[a, :], key_mask_ref[0, a, :]], 1) for a in at]
    turned = [key_ref[a, :].astype(full_type).T.astype(low_type) for a in at]
    gained = jnp.zeros((1, tile), full_type)
    far_sums = [jnp.zeros((8, tile), full_type) for side in range(2)]
    for t in range(count):
        rows = jnp.concatenate([query_ref[at[t], :], query_mask_ref[0, at[t], :]], 1)
        delta = ((1.0 - gate) * delta_ref[at[t], :].astype(full_type)).astype(low_type)
        parts = []
        for j in range(count):
            step = j - t
            if step < -1:
                bias = far_ref[head, 0]
            elif step > 1:
                bias = far_ref[head, 1]
            else:
                bias = bias_ref[:, pl.ds((1 - step) * tile, tile)]
            parts.append(dot_inner(keys[j], rows) * (scale * log2_e) + bias)
        top = jnp.max(functools.reduce(jnp.maximum, parts), 0, keepdims=True)
        parts = [jnp.exp2(part - top) for part in parts]
        total = jnp.sum(functools.reduce(jnp.add, parts), 0, keepdims=True)
        inverse = 1.0 / total
        parts = [part * inverse for part in parts]
        moves = [dot_inner(value_ref[at[j], :], delta) for j in range(count)]
        expected = jnp.sum(
            functools.reduce(jnp.add, [parts[j] * moves[j] for j in range(count)]),
            0,
            keepdims=True,
        )
        gained = gained + expected
        query_sum = None
        for j in range(count):
            step = j - t
            score_delta = parts[j] * (moves[j] - expected)
            if abs(step) > 1:
                side = 0 if step < 0 else 1
                far_sums[side] = far_sums[side] + jnp.sum(
                    score_delta.reshape(tile // 8, 8, tile), 0
                )
            else:
                near_ref[:, pl.ds((1 - step) * tile, tile)] += score_delta
            low_delta = score_delta.astype(low_type)
            value_part = dot_rows(parts[j].astype(low_type), delta)
            key_part = dot_rows(low_delta, query_ref[at[t], :])
            query_part = dot_rows(turned[j], low_delta)
            if t == 0:
                value_sum_ref[at[j], :] = value_part
                key_sum_ref[at[j], :] = key_part
            else:
                value_sum_ref[at[j], :] += value_part
                key_sum_ref[at[j], :] += key_part
            query_sum = query_part if j == 0 else query_sum + query_part
        query_delta_ref[at[t], :] = (
            query_sum.T * scale + recall_delta_ref[at[t], :]
        ).astype(low_type)
    key_delta_ref[...] = (key_sum_ref[...] * scale).astype(low_type)
    value_delta_ref[...] = value_sum_ref[...].astype(low_type)
    sums_ref[0, 0:1] += gained
    sums_ref[0, 8:16] += far_sums[0]
    sums_ref[0, 16:24] += far_sums[1]

    @pl.when(last)
    def fold_diagonals():
        total = jnp.zeros((8, ring), full_type)
        for g in range(tile // 8):
            part = jnp.concatenate(
                [near_ref[pl.ds(g * 8, 8), :], jnp.zeros((8, ring - span), full_type)], 1
            )
            total = total + (pltpu.roll(part, ring - 8 * g, 1) if g else part)
        row = lax.broadcasted_iota(jnp.int32, (8, ring), 0)
        for bit in (1, 2, 4):
            total = jnp.where((row & bit) != 0, pltpu.roll(total, ring - bit, 1), total)
        diagonal_ref[0] = total


def local_back(
    projected, query_mask, key_mask, mixed_delta, recall_delta, columns, far, gates, seq_len, scale,
    heads_now, carried, kept, after,
):
    tokens = mixed_delta.shape[0]
    heads = gates.shape[0]
    width = mixed_delta.shape[1] // heads
    start, count = heads_now
    anywhere = pl.BlockSpec(memory_space=pl.ANY)
    chosen = slice(start, start + count)

    def rows_of(shift):
        return pl.BlockSpec((seq_len, width), lambda h, s: (s, h + start + shift * heads))

    def kernel(*refs):
        inputs, rest = refs[:10], refs[10 + len(kept) + len(carried) + len(after) :]
        local_back_kernel(scale, *inputs, *rest[:5], *rest[5 + len(carried) :])

    mask_spec = pl.BlockSpec((1, seq_len, 128), lambda h, s: (s, 0, 0))
    smem = pl.BlockSpec(memory_space=pltpu.SMEM)
    rows_shape = jax.ShapeDtypeStruct((tokens, heads * width), low_type)
    first = 10 + len(kept)
    out = pl.pallas_call(
        kernel,
        grid=(count, tokens // seq_len),
        in_specs=[
            smem,
            smem,
            pl.BlockSpec((1, 1, ring), lambda h, s: (h, 0, 0)),
            rows_of(0),
            rows_of(1),
            rows_of(2),
            mask_spec,
            mask_spec,
            rows_of(0),
            rows_of(0),
        ]
        + [anywhere] * (len(kept) + len(carried) + len(after)),
        out_specs=[
            rows_of(0),
            rows_of(0),
            rows_of(0),
            pl.BlockSpec((1, 8, ring), lambda h, s: (h, 0, 0)),
            pl.BlockSpec((1, 24, tile), lambda h, s: (h, 0, 0)),
        ]
        + [anywhere] * len(carried),
        out_shape=[
            rows_shape,
            rows_shape,
            rows_shape,
            jax.ShapeDtypeStruct((count, 8, ring), full_type),
            jax.ShapeDtypeStruct((count, 24, tile), full_type),
        ]
        + [jax.ShapeDtypeStruct(part.shape, part.dtype) for part in carried],
        input_output_aliases={10 + i: i for i in range(len(kept))}
        | {first + i: 5 + i for i in range(len(carried))},
        scratch_shapes=[
            pltpu.VMEM((tile, span), full_type),
            pltpu.VMEM((tile, span), full_type),
            pltpu.VMEM((seq_len, width), full_type),
            pltpu.VMEM((seq_len, width), full_type),
        ],
        compiler_params=pltpu.CompilerParams(vmem_limit_bytes=vmem_most),
        cost_estimate=pl.CostEstimate(
            flops=0, bytes_accessed=count * tokens * seq_len * 40, transcendentals=0
        ),
        name="local_back",
    )(
        gates[chosen], far[chosen], columns[chosen], projected, projected, projected, query_mask,
        key_mask, mixed_delta, recall_delta, *kept, *carried, *after,
    )
    return list(out[:3]), out[3], out[4], list(out[5:])


def mask_rows(block_ids):
    level = jnp.arange(128, dtype=jnp.int32)
    gap = block_ids[:, :, None] - level
    query_mask = jnp.where((gap >= 0) & (gap <= 1), 0.0, mask_gap).astype(low_type)
    key_mask = (gap == 0).astype(low_type)
    return query_mask, key_mask


def fetch(rows):
    group = lax.axis_size("tensor")
    return [rows] + [
        lax.ppermute(rows, "tensor", [((i + k) % group, i) for i in range(group)])
        for k in range(1, group)
    ]


def in_order(shares):
    group = lax.axis_size("tensor")
    rows = shares[0].shape[0]
    whole = jnp.zeros((group * rows,) + shares[0].shape[1:], shares[0].dtype)
    for k in range(group):
        start = ((lax.axis_index("tensor") + k) % group) * rows
        whole = lax.dynamic_update_slice_in_dim(whole, shares[k], start, 0)
    return whole


def share_of(whole, k, rows):
    start = ((lax.axis_index("tensor") + k) % lax.axis_size("tensor")) * rows
    return lax.dynamic_slice_in_dim(whole, start, rows, 0)


def fold(term, piece):
    group = lax.axis_size("tensor")
    sent = [
        lax.ppermute(
            term(piece(k)).astype(low_type), "tensor", [(i, (i + k) % group) for i in range(group)]
        )
        for k in range(1, group)
    ]
    return sum((part.astype(full_type) for part in sent), term(piece(0)))


def bit_orders():
    bits = lax.axis_size("dp").bit_length() - 1
    near = [(0, 1, 2), (1, 2, 0), (2, 0, 1)]
    return [list(head) + list(range(3, bits)) for head in near]


def swap_over(rows, bit):
    return lax.ppermute(rows, "dp", [(i, i ^ (1 << bit)) for i in range(lax.axis_size("dp"))])


def side_of(bit):
    return (lax.axis_index("dp") >> bit) & 1


def halve_step(parts, step):
    kept, sent = [], []
    for part, order in zip(parts, bit_orders()):
        half = part.shape[0] // 2
        side = side_of(order[step])
        sent.append(
            swap_over(
                lax.dynamic_slice_in_dim(part, (1 - side) * half, half, 0), order[step]
            )
        )
        kept.append(lax.dynamic_slice_in_dim(part, side * half, half, 0))
    return kept, sent


def add_low(kept, sent):
    return [
        (a.astype(full_type) + b.astype(full_type)).astype(low_type) for a, b in zip(kept, sent)
    ]


def double_all(parts):
    orders = bit_orders()
    for step in reversed(range(len(orders[0]))):
        got = [swap_over(part, order[step]) for part, order in zip(parts, orders)]
        wider = []
        for part, other, order in zip(parts, got, orders):
            rows = part.shape[0]
            side = side_of(order[step])
            whole = jnp.zeros((2 * rows,) + part.shape[1:], part.dtype)
            whole = lax.dynamic_update_slice_in_dim(whole, part, side * rows, 0)
            wider.append(lax.dynamic_update_slice_in_dim(whole, other, (1 - side) * rows, 0))
        parts = wider
    return parts


def pack(parts):
    width = min(part.shape[1] for part in parts)
    return jnp.concatenate(
        [
            part[:, start : start + width]
            for part in parts
            for start in range(0, part.shape[1], width)
        ],
        0,
    )


def gather_all(packed, parts):
    whole = lax.all_gather(packed, "dp", axis=0)
    width = packed.shape[1]
    wide = []
    start = 0
    for part, order in zip(parts, bit_orders()):
        bits = len(order)
        rows = part.shape[0]
        columns = []
        for unused in range(part.shape[1] // width):
            piece = whole[:, start : start + rows].reshape((2,) * bits + (rows, width))
            piece = piece.transpose([bits - 1 - bit for bit in order] + [bits, bits + 1])
            columns.append(piece.reshape(-1, width))
            start += rows
        wide.append(jnp.concatenate(columns, 1).astype(full_type))
    return wide


def body(
    tokens,
    block_ids,
    memory_index,
    memory_keys,
    memory_values,
    attn_gain,
    query_weight,
    key_weight,
    value_weight,
    output_weight,
    position_table,
    memory_gate,
    mlp_gain,
    hidden_weight,
    return_weight,
    grad_output,
):
    share_rows = tokens.shape[0]
    seq_len = block_ids.shape[1]
    head_count, memory_rows, head_width = memory_keys.shape
    picks = memory_index.shape[2]
    inner_width = head_count * head_width
    scale = head_width ** (-0.5)

    offsets = jnp.arange(head_count, dtype=jnp.int32) * memory_rows
    index_rows = memory_index.transpose(1, 0, 2) + offsets[:, None, None]
    found = gather_found(index_rows, interleave(memory_keys, memory_values))
    found = found.reshape(-1, head_width)

    token_full = tokens.astype(full_type)
    normed_rows = rms_scaled(token_full, attn_gain).astype(low_type)
    normed = lax.all_gather(normed_rows, "tensor", axis=0, tiled=True)
    joined = jnp.concatenate([query_weight, key_weight, value_weight], 1)
    projected = dot_rows(normed, joined).astype(low_type)

    query_mask, key_mask = mask_rows(block_ids)
    place = jnp.arange(ring, dtype=jnp.int32)
    place = jnp.where(place < span, place, place - ring)
    ahead = bucket_of(place - tile)
    behind = bucket_of(tile - place)
    level = jnp.arange(32, dtype=jnp.int32)
    ahead_hot = (ahead[:, None] == level).astype(full_type)
    behind_hot = (behind[:, None] == level).astype(full_type)
    scaled_table = position_table * log2_e
    ahead_columns = jnp.dot(ahead_hot, scaled_table, precision=exact_mode).T[:, None, :]
    behind_columns = jnp.dot(behind_hot, scaled_table, precision=exact_mode).T[:, None, :]
    far = jnp.stack([scaled_table[15], scaled_table[31]], 1)
    gates = jax.nn.sigmoid(memory_gate)

    recalled = recall(found, projected, head_count, picks, scale)
    mixed_rows = local_read(
        projected, query_mask, key_mask, recalled, ahead_columns, far, gates, seq_len, scale
    )
    middle = token_full + fold(
        lambda rows: dot_rows(rows, output_weight), lambda k: share_of(mixed_rows, k, share_rows)
    )
    second_rows = rms_scaled(middle, mlp_gain).astype(low_type)
    grad_full = jnp.concatenate(fetch(grad_output), 0)
    second = jnp.concatenate(fetch(second_rows), 0)
    hidden = dot_rows(second, hidden_weight)
    active = jax.nn.gelu(hidden).astype(low_type)
    return_low = dot_outer(active, grad_full).astype(low_type)
    active_delta = dot_inner(grad_full, return_weight)
    gelu_back = jax.vjp(jax.nn.gelu, hidden)[1]
    hidden_delta = gelu_back(active_delta)[0].astype(low_type)
    second_delta = fold(
        lambda rows: dot_inner(rows, hidden_weight),
        lambda k: lax.slice_in_dim(hidden_delta, k * share_rows, (k + 1) * share_rows),
    )
    hidden_low = dot_outer(second, hidden_delta).astype(low_type)
    second_back = jax.vjp(rms_scaled, middle, mlp_gain)[1]
    middle_part, mlp_gain_part = second_back(second_delta)
    middle_delta = grad_output.astype(full_type) + middle_part
    middle_full = in_order(fetch(middle_delta.astype(low_type)))
    mixed_delta = dot_inner(middle_full, output_weight).astype(low_type)
    layer_output = (
        middle
        + fold(
            lambda rows: dot_rows(rows, return_weight),
            lambda k: lax.slice_in_dim(active, k * share_rows, (k + 1) * share_rows),
        )
    ).astype(low_type)

    return_half = return_low.shape[0] // 2
    steps = len(bit_orders()[0])
    output_low = dot_outer(mixed_rows, middle_full).astype(low_type)
    kept, sent = halve_step(
        [
            hidden_low,
            return_low[:return_half],
            jnp.concatenate([return_low[return_half:], output_low], 0),
        ],
        0,
    )
    taken = 0
    waits = (0, 2, 3)
    recall_delta = None
    recall_sums = []
    for head in range(head_count):
        recall_delta, head_sums, kept = recall_back(
            found, projected, mixed_delta, gates, head, kept, recall_delta, head_count, picks, scale
        )
        recall_sums.append(head_sums)
        if head in waits and taken < steps - 1:
            taken += 1
            kept, sent = halve_step(add_low(kept, sent), taken)
    while taken < steps - 1:
        taken += 1
        kept, sent = halve_step(add_low(kept, sent), taken)
    recall_sums = jnp.concatenate(recall_sums, 0)
    half_heads = max(1, head_count // 2)
    deltas = []
    diagonals = []
    local_sums = []
    shards = []
    packed = []
    for start in range(0, head_count, half_heads):
        deltas, diagonal_now, sums_now, kept = local_back(
            projected, query_mask, key_mask, mixed_delta, recall_delta, behind_columns, far, gates,
            seq_len, scale, (start, half_heads), [] if shards else kept, deltas, packed,
        )
        if not shards:
            shards = add_low(kept, sent)
            packed = [pack(shards)]
        diagonals.append(diagonal_now)
        local_sums.append(sums_now)
    hidden_sum, return_sum, mixed_sum = gather_all(packed[0], shards)
    query_delta, key_delta, value_delta = deltas
    diagonals = jnp.concatenate(diagonals, 0)
    local_sums = jnp.concatenate(local_sums, 0)
    recall_gain = jnp.sum(recall_sums[:, :, 0], 1)
    local_gain = jnp.sum(local_sums[:, 0], 1)
    gate_part = gates * (1.0 - gates) * recall_gain - gates * local_gain
    diagonal_sums = jnp.sum(diagonals, 1)
    table_part = jnp.dot(diagonal_sums, behind_hot, precision=exact_mode)
    far_left = jnp.sum(local_sums[:, 8:16], (1, 2))
    far_right = jnp.sum(local_sums[:, 16:24], (1, 2))
    table_part = table_part + far_left[:, None] * (level == 15) + far_right[:, None] * (level == 31)

    project_delta = jnp.concatenate([query_delta, key_delta, value_delta], 1)
    joined_part = dot_outer(normed, project_delta)
    attn_gain_part = jnp.sum(joined_part * joined.astype(full_type), 1) / attn_gain
    model_width = tokens.shape[1]
    small = jnp.concatenate([table_part.reshape(-1), gate_part])
    small = jnp.pad(small, (0, model_width - small.shape[0]))
    extra = jnp.stack([attn_gain_part, mlp_gain_part, small], 1)
    extra = jnp.pad(extra, ((0, 0), (0, 125)))
    joined_low = jnp.concatenate([joined_part, extra], 1).astype(low_type)
    quarter = joined_low.shape[0] // 4
    last = [
        joined_low[: 2 * quarter],
        joined_low[2 * quarter : 3 * quarter],
        joined_low[3 * quarter :],
    ]
    for step in range(steps):
        last = add_low(*halve_step(last, step))
    joined_sum = double_all(last)

    normed_delta = fold(
        lambda rows: dot_inner(rows, joined), lambda k: share_of(project_delta, k, share_rows)
    )
    first_back = jax.vjp(rms_scaled, token_full, attn_gain)[1]
    tokens_grad = (middle_delta + first_back(normed_delta)[0]).astype(low_type)

    joined_grad = jnp.concatenate(joined_sum, 0).astype(full_type)
    gains = sum(fetch(joined_grad[:, 3 * inner_width : 3 * inner_width + 2]))
    small_sum = joined_grad[:, 3 * inner_width + 2]
    table_size = head_count * 32
    return (
        layer_output,
        tokens_grad,
        gains[:, 0],
        joined_grad[:, :inner_width],
        joined_grad[:, inner_width : 2 * inner_width],
        joined_grad[:, 2 * inner_width : 3 * inner_width],
        mixed_sum[return_half:],
        small_sum[:table_size].reshape(head_count, 32).T,
        small_sum[table_size : table_size + head_count],
        gains[:, 1],
        hidden_sum,
        jnp.concatenate([return_sum, mixed_sum[:return_half]], 0),
    )


def solution(mesh):
    def run(*arrays):
        with jax.sharding.use_abstract_mesh(mesh.abstract_mesh):
            return jax.shard_map(
                body,
                mesh=mesh,
                in_specs=(
                    P(("dp", "tensor"), None),
                    P("dp", None),
                    P("dp", "tensor", None),
                    P("tensor", None, None),
                    P("tensor", None, None),
                    P(),
                    P(None, "tensor"),
                    P(None, "tensor"),
                    P(None, "tensor"),
                    P("tensor", None),
                    P(None, "tensor"),
                    P("tensor"),
                    P(),
                    P(None, "tensor"),
                    P("tensor", None),
                    P(("dp", "tensor"), None),
                ),
                out_specs=(
                    P(("dp", "tensor"), None),
                    P(("dp", "tensor"), None),
                    P(),
                    P(None, "tensor"),
                    P(None, "tensor"),
                    P(None, "tensor"),
                    P("tensor", None),
                    P(None, "tensor"),
                    P("tensor"),
                    P(),
                    P(None, "tensor"),
                    P("tensor", None),
                ),
                check_vma=False,
            )(*arrays)

    return run
```

```python
import functools
import math

import jax
import jax.numpy as jnp
from jax import lax
from jax.experimental import pallas as pl
from jax.experimental.pallas import tpu as pltpu
from jax.sharding import PartitionSpec as P

eps_norm = 1e-06
far_steps = (12, 16, 23, 32, 46, 64, 91)
exact_mode = lax.Precision.HIGHEST
low_type = jnp.bfloat16
full_type = jnp.float32
log2_e = math.log2(math.e)
tile = 256
span = 3 * tile
ring = 1024
mask_gap = -(2.0**100)
vmem_most = 60 * 2**20


def bucket_of(relative):
    upper_half = jnp.where(relative > 0, 16, 0).astype(jnp.int32)
    distance = jnp.abs(relative)
    far_bucket = 8 + sum(((distance >= step_size).astype(jnp.int32) for step_size in far_steps))
    return upper_half + jnp.where(distance < 8, distance, far_bucket)


def rms_scaled(rows, gain):
    return rows * lax.rsqrt(jnp.mean(rows * rows, -1, keepdims=True) + eps_norm) * gain


def dot_rows(left, right):
    return jnp.dot(left, right, preferred_element_type=full_type)


def dot_outer(left, right):
    return lax.dot_general(
        left, right, (((0,), (0,)), ((), ())), preferred_element_type=full_type
    )


def dot_inner(left, right):
    return lax.dot_general(
        left, right, (((1,), (1,)), ((), ())), preferred_element_type=full_type
    )


def interleave_kernel(key_ref, value_ref, table_ref):
    rows = key_ref.shape[1]
    row = lax.broadcasted_iota(jnp.int32, (256, 256), 0)
    column = lax.broadcasted_iota(jnp.int32, (256, 256), 1)
    order = jnp.where(column == (row // 2 + (row % 2) * 128), 1.0, 0.0).astype(low_type)
    for part in range(rows // 128):
        both = jnp.concatenate(
            [key_ref[0, pl.ds(part * 128, 128)], value_ref[0, pl.ds(part * 128, 128)]], 0
        )
        table_ref[pl.ds(part * 256, 256), :] = dot_rows(order, both).astype(low_type)


def interleave(memory_keys, memory_values):
    heads, rows, width = memory_keys.shape
    step = min(2048, rows)
    spec = pl.BlockSpec((1, step, width), lambda h, i: (h, i, 0))
    return pl.pallas_call(
        interleave_kernel,
        grid=(heads, rows // step),
        in_specs=[spec, spec],
        out_specs=pl.BlockSpec((2 * step, width), lambda h, i: (h * (rows // step) + i, 0)),
        out_shape=jax.ShapeDtypeStruct((heads * rows * 2, width), low_type),
        cost_estimate=pl.CostEstimate(
            flops=heads * rows * 4 * 256 * width,
            bytes_accessed=heads * rows * width * 8,
            transcendentals=0,
        ),
        name="interleave",
    )(memory_keys, memory_values).reshape(heads, rows, 2, width)


def own_columns(picks):
    shape = (8, 8 * picks * 2)
    lane = lax.broadcasted_iota(jnp.int32, shape, 1)
    row = lax.broadcasted_iota(jnp.int32, shape, 0)
    return jnp.logical_and(lane // (2 * picks) == row, lane % 2 == 0)


def copy_rows(picked, first, table_ref, found_ref, start, count):
    for at in range(0, count, 8):
        rows_now = [
            table_ref[picked[(first + at + j) // 128, (first + at + j) % 128]] for j in range(8)
        ]
        for j in range(8):
            found_ref[start + at + j] = rows_now[j]
        yield


def recall_rows(picks, scale, own, query_ref, query_at, rows_ref, read_ref, read_at, tokens):
    wide = 8 * picks * 2
    groups = range(tokens // 8)
    scores = []
    for g in groups:
        rows = rows_ref[pl.ds(g * wide, wide), :]
        scores.append(dot_inner(query_ref[pl.ds(query_at + g * 8, 8), :], rows))
        yield
    shifted = []
    totals = []
    for g in groups:
        masked = jnp.where(own, scores[g] * (scale * log2_e), -jnp.inf)
        exponent = jnp.exp2(masked - jnp.max(masked, 1, keepdims=True))
        totals.append(jnp.sum(exponent, 1, keepdims=True))
        shifted.append(pltpu.roll(exponent, 1, 1).astype(low_type))
        yield
    for g in groups:
        rows = rows_ref[pl.ds(g * wide, wide), :]
        read_ref[pl.ds(read_at + g * 8, 8), :] = dot_rows(shifted[g], rows) / totals[g]
        yield


def weave(many, many_count, few, few_count):
    done = 0
    for number in range(few_count):
        until = (number + 1) * many_count // few_count
        while done < until:
            next(many)
            done += 1
        next(few)


def gather_kernel(
    picks, scale, index_hbm, table_hbm, now_ref, before_ref, found_ref, late_ref, early_ref,
    table_ref, table_sems, index_a, index_b, index_sems, stage_ref, stage_sems,
):
    step = pl.program_id(0)
    steps = pl.num_programs(0) - 1
    heads = table_sems.shape[0]
    blocks = steps // heads
    chunk = found_ref.shape[0] // 2
    rows = table_ref.shape[0] // heads
    slots = (index_a, index_b)
    part = chunk // 2
    tokens = part // picks
    own = own_columns(picks)
    flat = found_ref.reshape(4 * chunk, 128)

    def index_copy(number, slot):
        return pltpu.make_async_copy(index_hbm.at[number], slots[slot], index_sems.at[slot])

    def table_copy(number):
        where = pl.ds(number * rows, rows)
        return pltpu.make_async_copy(
            table_hbm.at[where], table_ref.at[where], table_sems.at[number]
        )

    def stage_copy(number):
        return pltpu.make_async_copy(
            flat.at[pl.ds(number * 2 * part, 2 * part)], stage_ref.at[number], stage_sems.at[number]
        )

    def reads(number, query_ref, read_ref):
        return recall_rows(
            picks, scale, own, query_ref, (number % 2) * tokens, stage_ref.at[number], read_ref,
            (number % 2) * tokens, tokens,
        )

    @pl.when(step == 0)
    def start_all():
        index_copy(0, 0).start()
        index_copy(1, 1).start()
        for number in range(heads):
            table_copy(number).start()
        stage_copy(2).start()
        stage_copy(3).start()

    @pl.when(jnp.logical_and(step < steps, step % blocks == 0))
    def wait_table():
        table_copy(step // blocks).wait()

    @pl.when(step < steps)
    def work():
        following = jnp.minimum(step + 1, steps - 1)
        for number in range(4):
            slot = number // 2
            if number % 2 == 0:
                index_copy(2 * step + slot, slot).wait()
            finished = (number + 2) % 4
            stage_copy(finished).wait()
            copied = copy_rows(
                slots[slot], (number % 2) * part, table_ref, found_ref, number * part, part
            )
            if number < 2:
                read = reads(finished, before_ref, late_ref)
            else:
                read = reads(finished, now_ref, early_ref)
            weave(copied, part // 8, read, 3 * (tokens // 8))
            stage_copy(number).start()
            if number % 2 == 1:
                index_copy(2 * following + slot, slot).start()

    @pl.when(step == steps)
    def finish():
        for number in (2, 3):
            stage_copy(number).wait()
            for unused in reads(number, before_ref, late_ref):
                pass
        for slot in range(2):
            index_copy(2 * (steps - 1) + slot, slot).wait()


def gather_found(index_rows, table, queries, picks, scale):
    heads, rows, unused, width = table.shape
    tokens = queries.shape[0]
    half = 128
    blocks = tokens // (2 * half)
    steps = heads * blocks
    chunk = half * picks

    def query_spec(shift):
        def place(t):
            at = jnp.clip(t - shift, 0, steps - 1)
            return (2 * (at % blocks) + shift, at // blocks)

        return pl.BlockSpec((half, width), place)

    return pl.pallas_call(
        functools.partial(gather_kernel, picks, scale),
        grid=(steps + 1,),
        in_specs=[
            pl.BlockSpec(memory_space=pl.ANY),
            pl.BlockSpec(memory_space=pl.ANY),
            query_spec(0),
            query_spec(1),
        ],
        out_specs=[
            pl.BlockSpec((2 * chunk, 2, width), lambda t: (jnp.minimum(t, steps - 1), 0, 0)),
            pl.BlockSpec((half, width), lambda t: (jnp.maximum(t - 1, 0), 0)),
            pl.BlockSpec((half, width), lambda t: (jnp.minimum(t, steps - 1), 0)),
        ],
        out_shape=[
            jax.ShapeDtypeStruct((heads * tokens * picks, 2, width), low_type),
            jax.ShapeDtypeStruct((heads * tokens // 2, width), full_type),
            jax.ShapeDtypeStruct((heads * tokens // 2, width), full_type),
        ],
        scratch_shapes=[
            pltpu.VMEM((heads * rows, 2, width), low_type),
            pltpu.SemaphoreType.DMA((heads,)),
            pltpu.SMEM((chunk // 128, 128), jnp.int32),
            pltpu.SMEM((chunk // 128, 128), jnp.int32),
            pltpu.SemaphoreType.DMA((2,)),
            pltpu.VMEM((4, chunk, width), low_type),
            pltpu.SemaphoreType.DMA((4,)),
        ],
        compiler_params=pltpu.CompilerParams(vmem_limit_bytes=vmem_most),
        cost_estimate=pl.CostEstimate(
            flops=0, bytes_accessed=4 * heads * tokens * picks * width * 4, transcendentals=0
        ),
        name="gather_found",
    )(
        index_rows.reshape(-1, chunk // 128, 128), table.reshape(heads * rows, 2, width), queries,
        queries,
    )


def recall_back_kernel(
    picks, scale, gate_ref, found_ref, query_ref, delta_ref, query_delta_ref, sums_ref
):
    tokens = query_ref.shape[0]
    wide = 8 * picks * 2
    own = own_columns(picks)
    gate = gate_ref[0]
    groups = range(tokens // 8)
    both = []
    for g in groups:
        rows = jnp.concatenate(
            [query_ref[pl.ds(g * 8, 8), :], delta_ref[pl.ds(g * 8, 8), :]], 0
        )
        both.append(dot_inner(rows, found_ref[pl.ds(g * wide, wide), :]))
    gained = jnp.zeros((8, 1), full_type)
    for g in groups:
        masked = jnp.where(own, both[g][:8] * (scale * log2_e), -jnp.inf)
        exponent = jnp.exp2(masked - jnp.max(masked, 1, keepdims=True))
        weights = exponent / jnp.sum(exponent, 1, keepdims=True)
        reads = pltpu.roll(both[g][8:], wide - 1, 1)
        expected = jnp.sum(weights * reads, 1, keepdims=True)
        gained = gained + expected
        score_delta = (weights * (reads - expected)).astype(low_type)
        query_delta_ref[pl.ds(g * 8, 8), :] = dot_rows(
            score_delta, found_ref[pl.ds(g * wide, wide), :]
        ) * (scale * gate)

    @pl.when(pl.program_id(0) == 0)
    def clear():
        sums_ref[...] = jnp.zeros(sums_ref.shape, full_type)

    sums_ref[0] += jnp.broadcast_to(gained, (8, 128))


def recall_back(
    found, queries, mixed_delta, gates, head, carried, after, kept, heads, picks, scale
):
    tokens = queries.shape[0]
    width = mixed_delta.shape[1] // heads
    step = min(512, tokens)
    blocks = tokens // step
    rows_spec = pl.BlockSpec((step, width), lambda i: (i, head))
    anywhere = pl.BlockSpec(memory_space=pl.ANY)
    extra = [kept] if kept is not None else []
    first = 4 + len(extra)

    def kernel(gate_ref, found_ref, query_ref, delta_ref, *rest):
        query_delta_ref, sums_ref = rest[len(extra) + len(carried) + len(after) :][:2]
        recall_back_kernel(
            picks, scale, gate_ref, found_ref, query_ref, delta_ref, query_delta_ref, sums_ref
        )

    out = pl.pallas_call(
        kernel,
        grid=(blocks,),
        in_specs=[
            pl.BlockSpec(memory_space=pltpu.SMEM),
            pl.BlockSpec((step * picks * 2, width), lambda i: (head * blocks + i, 0)),
            rows_spec,
            rows_spec,
        ]
        + [anywhere] * (len(extra) + len(carried) + len(after)),
        out_specs=[rows_spec, pl.BlockSpec((1, 8, 128), lambda i: (0, 0, 0))]
        + [anywhere] * len(carried),
        out_shape=[
            jax.ShapeDtypeStruct((tokens, heads * width), full_type),
            jax.ShapeDtypeStruct((1, 8, 128), full_type),
        ]
        + [jax.ShapeDtypeStruct(part.shape, part.dtype) for part in carried],
        input_output_aliases=({4: 0} if extra else {})
        | {first + i: 2 + i for i in range(len(carried))},
        compiler_params=pltpu.CompilerParams(vmem_limit_bytes=vmem_most),
        cost_estimate=pl.CostEstimate(
            flops=0, bytes_accessed=tokens * picks * width * 8, transcendentals=0
        ),
        name="recall_back",
    )(gates[head : head + 1], found, queries, mixed_delta, *extra, *carried, *after)
    return out[0], out[1], list(out[2:])


def band(column_ref):
    wide = jnp.broadcast_to(column_ref[0], (tile, ring))
    return pltpu.roll(wide, 0, 1, stride=1, stride_axis=0)[:, :span]


def local_kernel(
    scale, gate_ref, far_ref, column_ref, query_ref, key_ref, value_ref, query_mask_ref,
    key_mask_ref, early_ref, late_ref, mixed_ref, bias_ref,
):
    head = pl.program_id(0)

    @pl.when(pl.program_id(1) == 0)
    def make_band():
        bias_ref[...] = band(column_ref)

    gate = gate_ref[head]
    count = query_ref.shape[0] // tile
    at = [pl.ds(t * tile, tile) for t in range(count)]
    keys = [jnp.concatenate([key_ref[a, :], key_mask_ref[0, a, :]], 1) for a in at]
    for t in range(count):
        rows = jnp.concatenate([query_ref[at[t], :], query_mask_ref[0, at[t], :]], 1)
        parts = []
        for j in range(count):
            step = j - t
            if step < -1:
                bias = far_ref[head, 0]
            elif step > 1:
                bias = far_ref[head, 1]
            else:
                bias = bias_ref[:, pl.ds((step + 1) * tile, tile)]
            parts.append(dot_inner(rows, keys[j]) * (scale * log2_e) + bias)
        top = jnp.max(functools.reduce(jnp.maximum, parts), 1, keepdims=True)
        parts = [jnp.exp2(part - top) for part in parts]
        total = jnp.sum(functools.reduce(jnp.add, parts), 1, keepdims=True)
        read = sum(dot_rows(parts[j].astype(low_type), value_ref[at[j], :]) for j in range(count))
        half = pl.ds(t * (tile // 2), tile // 2)
        recalled = jnp.concatenate([early_ref[half, :], late_ref[half, :]], 0)
        mixed_ref[at[t], :] = (gate * recalled + ((1.0 - gate) / total) * read).astype(low_type)


def local_read(projected, query_mask, key_mask, early, late, columns, far, gates, seq_len, scale):
    tokens, width = projected.shape
    heads = gates.shape[0]
    width = width // (3 * heads)
    sequences = tokens // seq_len
    half_spec = pl.BlockSpec((seq_len // 2, width), lambda h, s: (h * sequences + s, 0))

    def rows_of(shift):
        return pl.BlockSpec((seq_len, width), lambda h, s: (s, h + shift * heads))

    mask_spec = pl.BlockSpec((1, seq_len, 128), lambda h, s: (s, 0, 0))
    smem = pl.BlockSpec(memory_space=pltpu.SMEM)
    return pl.pallas_call(
        functools.partial(local_kernel, scale),
        grid=(heads, tokens // seq_len),
        in_specs=[
            smem,
            smem,
            pl.BlockSpec((1, 1, ring), lambda h, s: (h, 0, 0)),
            rows_of(0),
            rows_of(1),
            rows_of(2),
            mask_spec,
            mask_spec,
            half_spec,
            half_spec,
        ],
        out_specs=rows_of(0),
        out_shape=jax.ShapeDtypeStruct((tokens, heads * width), low_type),
        scratch_shapes=[pltpu.VMEM((tile, span), full_type)],
        compiler_params=pltpu.CompilerParams(vmem_limit_bytes=vmem_most),
        cost_estimate=pl.CostEstimate(
            flops=0, bytes_accessed=heads * tokens * seq_len * 20, transcendentals=0
        ),
        name="local_read",
    )(gates, far, columns, projected, projected, projected, query_mask, key_mask, early, late)


def local_back_kernel(
    scale, gate_ref, far_ref, column_ref, query_ref, key_ref, value_ref, query_mask_ref,
    key_mask_ref, delta_ref, recall_delta_ref, query_delta_ref, key_delta_ref, value_delta_ref,
    diagonal_ref, sums_ref, bias_ref, near_ref, key_sum_ref, value_sum_ref,
):
    head = pl.program_id(0)
    last = pl.program_id(1) == pl.num_programs(1) - 1

    @pl.when(pl.program_id(1) == 0)
    def make_band():
        bias_ref[...] = band(column_ref)
        near_ref[...] = jnp.zeros(near_ref.shape, full_type)
        sums_ref[...] = jnp.zeros(sums_ref.shape, full_type)

    gate = gate_ref[head]
    count = query_ref.shape[0] // tile
    at = [pl.ds(t * tile, tile) for t in range(count)]
    keys = [jnp.concatenate([key_ref[a, :], key_mask_ref[0, a, :]], 1) for a in at]
    turned = [key_ref[a, :].astype(full_type).T.astype(low_type) for a in at]
    gained = jnp.zeros((1, tile), full_type)
    far_sums = [jnp.zeros((8, tile), full_type) for side in range(2)]
    for t in range(count):
        rows = jnp.concatenate([query_ref[at[t], :], query_mask_ref[0, at[t], :]], 1)
        delta = ((1.0 - gate) * delta_ref[at[t], :].astype(full_type)).astype(low_type)
        parts = []
        for j in range(count):
            step = j - t
            if step < -1:
                bias = far_ref[head, 0]
            elif step > 1:
                bias = far_ref[head, 1]
            else:
                bias = bias_ref[:, pl.ds((1 - step) * tile, tile)]
            parts.append(dot_inner(keys[j], rows) * (scale * log2_e) + bias)
        top = jnp.max(functools.reduce(jnp.maximum, parts), 0, keepdims=True)
        parts = [jnp.exp2(part - top) for part in parts]
        total = jnp.sum(functools.reduce(jnp.add, parts), 0, keepdims=True)
        inverse = 1.0 / total
        parts = [part * inverse for part in parts]
        moves = [dot_inner(value_ref[at[j], :], delta) for j in range(count)]
        expected = jnp.sum(
            functools.reduce(jnp.add, [parts[j] * moves[j] for j in range(count)]),
            0,
            keepdims=True,
        )
        gained = gained + expected
        query_sum = None
        for j in range(count):
            step = j - t
            score_delta = parts[j] * (moves[j] - expected)
            if abs(step) > 1:
                side = 0 if step < 0 else 1
                far_sums[side] = far_sums[side] + jnp.sum(
                    score_delta.reshape(tile // 8, 8, tile), 0
                )
            else:
                near_ref[:, pl.ds((1 - step) * tile, tile)] += score_delta
            low_delta = score_delta.astype(low_type)
            value_part = dot_rows(parts[j].astype(low_type), delta)
            key_part = dot_rows(low_delta, query_ref[at[t], :])
            query_part = dot_rows(turned[j], low_delta)
            if t == 0:
                value_sum_ref[at[j], :] = value_part
                key_sum_ref[at[j], :] = key_part
            else:
                value_sum_ref[at[j], :] += value_part
                key_sum_ref[at[j], :] += key_part
            query_sum = query_part if j == 0 else query_sum + query_part
        query_delta_ref[at[t], :] = (
            query_sum.T * scale + recall_delta_ref[at[t], :]
        ).astype(low_type)
    key_delta_ref[...] = (key_sum_ref[...] * scale).astype(low_type)
    value_delta_ref[...] = value_sum_ref[...].astype(low_type)
    sums_ref[0, 0:1] += gained
    sums_ref[0, 8:16] += far_sums[0]
    sums_ref[0, 16:24] += far_sums[1]

    @pl.when(last)
    def fold_diagonals():
        total = jnp.zeros((8, ring), full_type)
        for g in range(tile // 8):
            part = jnp.concatenate(
                [near_ref[pl.ds(g * 8, 8), :], jnp.zeros((8, ring - span), full_type)], 1
            )
            total = total + (pltpu.roll(part, ring - 8 * g, 1) if g else part)
        row = lax.broadcasted_iota(jnp.int32, (8, ring), 0)
        for bit in (1, 2, 4):
            total = jnp.where((row & bit) != 0, pltpu.roll(total, ring - bit, 1), total)
        diagonal_ref[0] = total


def local_back(
    projected, query_mask, key_mask, mixed_delta, recall_delta, columns, far, gates, seq_len, scale,
    heads_now, carried, kept, after,
):
    tokens = mixed_delta.shape[0]
    heads = gates.shape[0]
    width = mixed_delta.shape[1] // heads
    start, count = heads_now
    anywhere = pl.BlockSpec(memory_space=pl.ANY)
    chosen = slice(start, start + count)

    def rows_of(shift):
        return pl.BlockSpec((seq_len, width), lambda h, s: (s, h + start + shift * heads))

    def kernel(*refs):
        inputs, rest = refs[:10], refs[10 + len(kept) + len(carried) + len(after) :]
        local_back_kernel(scale, *inputs, *rest[:5], *rest[5 + len(carried) :])

    mask_spec = pl.BlockSpec((1, seq_len, 128), lambda h, s: (s, 0, 0))
    smem = pl.BlockSpec(memory_space=pltpu.SMEM)
    rows_shape = jax.ShapeDtypeStruct((tokens, heads * width), low_type)
    first = 10 + len(kept)
    out = pl.pallas_call(
        kernel,
        grid=(count, tokens // seq_len),
        in_specs=[
            smem,
            smem,
            pl.BlockSpec((1, 1, ring), lambda h, s: (h, 0, 0)),
            rows_of(0),
            rows_of(1),
            rows_of(2),
            mask_spec,
            mask_spec,
            rows_of(0),
            rows_of(0),
        ]
        + [anywhere] * (len(kept) + len(carried) + len(after)),
        out_specs=[
            rows_of(0),
            rows_of(0),
            rows_of(0),
            pl.BlockSpec((1, 8, ring), lambda h, s: (h, 0, 0)),
            pl.BlockSpec((1, 24, tile), lambda h, s: (h, 0, 0)),
        ]
        + [anywhere] * len(carried),
        out_shape=[
            rows_shape,
            rows_shape,
            rows_shape,
            jax.ShapeDtypeStruct((count, 8, ring), full_type),
            jax.ShapeDtypeStruct((count, 24, tile), full_type),
        ]
        + [jax.ShapeDtypeStruct(part.shape, part.dtype) for part in carried],
        input_output_aliases={10 + i: i for i in range(len(kept))}
        | {first + i: 5 + i for i in range(len(carried))},
        scratch_shapes=[
            pltpu.VMEM((tile, span), full_type),
            pltpu.VMEM((tile, span), full_type),
            pltpu.VMEM((seq_len, width), full_type),
            pltpu.VMEM((seq_len, width), full_type),
        ],
        compiler_params=pltpu.CompilerParams(vmem_limit_bytes=vmem_most),
        cost_estimate=pl.CostEstimate(
            flops=0, bytes_accessed=count * tokens * seq_len * 40, transcendentals=0
        ),
        name="local_back",
    )(
        gates[chosen], far[chosen], columns[chosen], projected, projected, projected, query_mask,
        key_mask, mixed_delta, recall_delta, *kept, *carried, *after,
    )
    return list(out[:3]), out[3], out[4], list(out[5:])


def mask_rows(block_ids):
    level = jnp.arange(128, dtype=jnp.int32)
    gap = block_ids[:, :, None] - level
    query_mask = jnp.where((gap >= 0) & (gap <= 1), 0.0, mask_gap).astype(low_type)
    key_mask = (gap == 0).astype(low_type)
    return query_mask, key_mask


def fetch(rows):
    group = lax.axis_size("tensor")
    return [rows] + [
        lax.ppermute(rows, "tensor", [((i + k) % group, i) for i in range(group)])
        for k in range(1, group)
    ]


def in_order(shares):
    group = lax.axis_size("tensor")
    rows = shares[0].shape[0]
    whole = jnp.zeros((group * rows,) + shares[0].shape[1:], shares[0].dtype)
    for k in range(group):
        start = ((lax.axis_index("tensor") + k) % group) * rows
        whole = lax.dynamic_update_slice_in_dim(whole, shares[k], start, 0)
    return whole


def share_of(whole, k, rows):
    start = ((lax.axis_index("tensor") + k) % lax.axis_size("tensor")) * rows
    return lax.dynamic_slice_in_dim(whole, start, rows, 0)


def fold(term, piece):
    group = lax.axis_size("tensor")
    sent = [
        lax.ppermute(
            term(piece(k)).astype(low_type), "tensor", [(i, (i + k) % group) for i in range(group)]
        )
        for k in range(1, group)
    ]
    return sum((part.astype(full_type) for part in sent), term(piece(0)))


def bit_orders():
    bits = lax.axis_size("dp").bit_length() - 1
    near = [(0, 1, 2), (1, 2, 0), (2, 0, 1)]
    return [list(head) + list(range(3, bits)) for head in near]


def swap_over(rows, bit):
    return lax.ppermute(rows, "dp", [(i, i ^ (1 << bit)) for i in range(lax.axis_size("dp"))])


def side_of(bit):
    return (lax.axis_index("dp") >> bit) & 1


def halve_step(parts, orders, step):
    kept, sent = [], []
    for part, order in zip(parts, orders):
        half = part.shape[0] // 2
        side = side_of(order[step])
        sent.append(
            swap_over(
                lax.dynamic_slice_in_dim(part, (1 - side) * half, half, 0), order[step]
            )
        )
        kept.append(lax.dynamic_slice_in_dim(part, side * half, half, 0))
    return kept, sent


def add_low(kept, sent):
    return [
        (a.astype(full_type) + b.astype(full_type)).astype(low_type) for a, b in zip(kept, sent)
    ]


def double_all(parts):
    orders = bit_orders()
    for step in reversed(range(len(orders[0]))):
        got = [swap_over(part, order[step]) for part, order in zip(parts, orders)]
        wider = []
        for part, other, order in zip(parts, got, orders):
            rows = part.shape[0]
            side = side_of(order[step])
            whole = jnp.zeros((2 * rows,) + part.shape[1:], part.dtype)
            whole = lax.dynamic_update_slice_in_dim(whole, part, side * rows, 0)
            wider.append(lax.dynamic_update_slice_in_dim(whole, other, (1 - side) * rows, 0))
        parts = wider
    return parts


def pack(parts):
    width = min(part.shape[1] for part in parts)
    return jnp.concatenate(
        [
            part[:, start : start + width]
            for part in parts
            for start in range(0, part.shape[1], width)
        ],
        0,
    )


def gather_all(packed, parts, orders):
    whole = lax.all_gather(packed, "dp", axis=0)
    width = packed.shape[1]
    wide = []
    start = 0
    for part, order in zip(parts, orders):
        bits = len(order)
        rows = part.shape[0]
        columns = []
        for unused in range(part.shape[1] // width):
            piece = whole[:, start : start + rows].reshape((2,) * bits + (rows, width))
            piece = piece.transpose([bits - 1 - bit for bit in order] + [bits, bits + 1])
            columns.append(piece.reshape(-1, width))
            start += rows
        wide.append(jnp.concatenate(columns, 1).astype(full_type))
    return wide


def body(
    tokens,
    block_ids,
    memory_index,
    memory_keys,
    memory_values,
    attn_gain,
    query_weight,
    key_weight,
    value_weight,
    output_weight,
    position_table,
    memory_gate,
    mlp_gain,
    hidden_weight,
    return_weight,
    grad_output,
):
    share_rows = tokens.shape[0]
    seq_len = block_ids.shape[1]
    head_count, memory_rows, head_width = memory_keys.shape
    picks = memory_index.shape[2]
    inner_width = head_count * head_width
    scale = head_width ** (-0.5)

    offsets = jnp.arange(head_count, dtype=jnp.int32) * memory_rows
    index_rows = memory_index.transpose(1, 0, 2) + offsets[:, None, None]
    table = interleave(memory_keys, memory_values)

    token_full = tokens.astype(full_type)
    normed_rows = rms_scaled(token_full, attn_gain).astype(low_type)
    normed = lax.all_gather(normed_rows, "tensor", axis=0, tiled=True)
    joined = jnp.concatenate([query_weight, key_weight, value_weight], 1)
    projected = dot_rows(normed, joined).astype(low_type)
    found, late, early = gather_found(index_rows, table, projected, picks, scale)
    found = found.reshape(-1, head_width)

    query_mask, key_mask = mask_rows(block_ids)
    place = jnp.arange(ring, dtype=jnp.int32)
    place = jnp.where(place < span, place, place - ring)
    ahead = bucket_of(place - tile)
    behind = bucket_of(tile - place)
    level = jnp.arange(32, dtype=jnp.int32)
    ahead_hot = (ahead[:, None] == level).astype(full_type)
    behind_hot = (behind[:, None] == level).astype(full_type)
    scaled_table = position_table * log2_e
    ahead_columns = jnp.dot(ahead_hot, scaled_table, precision=exact_mode).T[:, None, :]
    behind_columns = jnp.dot(behind_hot, scaled_table, precision=exact_mode).T[:, None, :]
    far = jnp.stack([scaled_table[15], scaled_table[31]], 1)
    gates = jax.nn.sigmoid(memory_gate)

    mixed_rows = local_read(
        projected, query_mask, key_mask, early, late, ahead_columns, far, gates, seq_len, scale
    )
    middle = token_full + fold(
        lambda rows: dot_rows(rows, output_weight), lambda k: share_of(mixed_rows, k, share_rows)
    )
    second_rows = rms_scaled(middle, mlp_gain).astype(low_type)
    grad_full = jnp.concatenate(fetch(grad_output), 0)
    second = jnp.concatenate(fetch(second_rows), 0)
    hidden = dot_rows(second, hidden_weight)
    active = jax.nn.gelu(hidden).astype(low_type)
    return_low = dot_outer(active, grad_full).astype(low_type)
    orders = bit_orders()
    steps = len(orders[0])
    return_half = return_low.shape[0] // 2
    return_parts = [return_low[:return_half], return_low[return_half:]]
    for step in range(steps):
        return_parts = add_low(*halve_step(return_parts, orders[1:], step))
    active_delta = dot_inner(grad_full, return_weight)
    gelu_back = jax.vjp(jax.nn.gelu, hidden)[1]
    hidden_delta = gelu_back(active_delta)[0].astype(low_type)
    second_delta = fold(
        lambda rows: dot_inner(rows, hidden_weight),
        lambda k: lax.slice_in_dim(hidden_delta, k * share_rows, (k + 1) * share_rows),
    )
    hidden_low = dot_outer(second, hidden_delta).astype(low_type)
    hidden_half = hidden_low.shape[0] // 2
    hidden_parts = [hidden_low[:hidden_half], hidden_low[hidden_half:]]
    hidden_parts = add_low(*halve_step(hidden_parts, orders[:2], 0))
    kept, sent = halve_step(hidden_parts, orders[:2], 1)
    second_back = jax.vjp(rms_scaled, middle, mlp_gain)[1]
    middle_part, mlp_gain_part = second_back(second_delta)
    middle_delta = grad_output.astype(full_type) + middle_part
    middle_full = in_order(fetch(middle_delta.astype(low_type)))
    mixed_delta = dot_inner(middle_full, output_weight).astype(low_type)
    layer_output = (
        middle
        + fold(
            lambda rows: dot_rows(rows, return_weight),
            lambda k: lax.slice_in_dim(active, k * share_rows, (k + 1) * share_rows),
        )
    ).astype(low_type)

    taken = 1
    shards, packed = [], []
    recall_delta = None
    recall_sums = []
    for head in range(head_count):
        recall_delta, head_sums, kept = recall_back(
            found, projected, mixed_delta, gates, head, kept, packed, recall_delta, head_count,
            picks, scale,
        )
        recall_sums.append(head_sums)
        if taken < steps - 1:
            taken += 1
            kept, sent = halve_step(add_low(kept, sent), orders[:2], taken)
        elif not shards:
            shards = add_low(kept, sent) + return_parts
            packed = [pack(shards)]
            kept = []
    while taken < steps - 1:
        taken += 1
        kept, sent = halve_step(add_low(kept, sent), orders[:2], taken)
    if not shards:
        shards = add_low(kept, sent) + return_parts
        packed = [pack(shards)]
    hidden_low_sum, hidden_high_sum, return_low_sum, return_high_sum = gather_all(
        packed[0], shards, orders[:2] + orders[1:]
    )
    hidden_sum = jnp.concatenate([hidden_low_sum, hidden_high_sum], 0)
    return_sum = jnp.concatenate([return_low_sum, return_high_sum], 0)
    recall_sums = jnp.concatenate(recall_sums, 0)
    half_heads = max(1, head_count // 2)
    deltas = []
    diagonals = []
    local_sums = []
    for start in range(0, head_count, half_heads):
        deltas, diagonal_now, sums_now, unused = local_back(
            projected, query_mask, key_mask, mixed_delta, recall_delta, behind_columns, far, gates,
            seq_len, scale, (start, half_heads), [], deltas, packed,
        )
        diagonals.append(diagonal_now)
        local_sums.append(sums_now)
    query_delta, key_delta, value_delta = deltas
    diagonals = jnp.concatenate(diagonals, 0)
    local_sums = jnp.concatenate(local_sums, 0)
    recall_gain = jnp.sum(recall_sums[:, :, 0], 1)
    local_gain = jnp.sum(local_sums[:, 0], 1)
    gate_part = gates * (1.0 - gates) * recall_gain - gates * local_gain
    diagonal_sums = jnp.sum(diagonals, 1)
    table_part = jnp.dot(diagonal_sums, behind_hot, precision=exact_mode)
    far_left = jnp.sum(local_sums[:, 8:16], (1, 2))
    far_right = jnp.sum(local_sums[:, 16:24], (1, 2))
    table_part = table_part + far_left[:, None] * (level == 15) + far_right[:, None] * (level == 31)

    project_delta = jnp.concatenate([query_delta, key_delta, value_delta], 1)
    joined_part = dot_outer(normed, project_delta)
    attn_gain_part = jnp.sum(joined_part * joined.astype(full_type), 1) / attn_gain
    model_width = tokens.shape[1]
    small = jnp.concatenate([table_part.reshape(-1), gate_part])
    small = jnp.pad(small, (0, model_width - small.shape[0]))
    extra = jnp.stack([attn_gain_part, mlp_gain_part, small], 1)
    extra = jnp.pad(extra, ((0, 0), (0, 125)))
    joined_low = jnp.concatenate([joined_part, extra], 1).astype(low_type)
    joined_half = joined_low.shape[0] // 2
    last = [
        joined_low[:joined_half],
        joined_low[joined_half:],
        dot_outer(mixed_rows, middle_full).astype(low_type),
    ]
    for step in range(steps):
        last = add_low(*halve_step(last, orders, step))
    last, hidden_sum, return_sum = lax.optimization_barrier((last, hidden_sum, return_sum))
    *joined_sum, output_sum = double_all(last)

    normed_delta = fold(
        lambda rows: dot_inner(rows, joined), lambda k: share_of(project_delta, k, share_rows)
    )
    first_back = jax.vjp(rms_scaled, token_full, attn_gain)[1]
    tokens_grad = (middle_delta + first_back(normed_delta)[0]).astype(low_type)

    def joined_columns(start, stop):
        return jnp.concatenate([part[:, start:stop].astype(full_type) for part in joined_sum], 0)

    last_columns = joined_columns(3 * inner_width, 3 * inner_width + 128)
    gains = sum(fetch(last_columns[:, :2].T))
    small_sum = last_columns[:, 2]
    table_size = head_count * 32
    return (
        layer_output,
        tokens_grad,
        gains[0],
        joined_columns(0, inner_width),
        joined_columns(inner_width, 2 * inner_width),
        joined_columns(2 * inner_width, 3 * inner_width),
        output_sum.astype(full_type),
        small_sum[:table_size].reshape(head_count, 32).T,
        small_sum[table_size : table_size + head_count],
        gains[1],
        hidden_sum,
        return_sum,
    )


def solution(mesh):
    def run(*arrays):
        with jax.sharding.use_abstract_mesh(mesh.abstract_mesh):
            return jax.shard_map(
                body,
                mesh=mesh,
                in_specs=(
                    P(("dp", "tensor"), None),
                    P("dp", None),
                    P("dp", "tensor", None),
                    P("tensor", None, None),
                    P("tensor", None, None),
                    P(),
                    P(None, "tensor"),
                    P(None, "tensor"),
                    P(None, "tensor"),
                    P("tensor", None),
                    P(None, "tensor"),
                    P("tensor"),
                    P(),
                    P(None, "tensor"),
                    P("tensor", None),
                    P(("dp", "tensor"), None),
                ),
                out_specs=(
                    P(("dp", "tensor"), None),
                    P(("dp", "tensor"), None),
                    P(),
                    P(None, "tensor"),
                    P(None, "tensor"),
                    P(None, "tensor"),
                    P("tensor", None),
                    P(None, "tensor"),
                    P("tensor"),
                    P(),
                    P(None, "tensor"),
                    P("tensor", None),
                ),
                check_vma=False,
            )(*arrays)

    return run
```

```python
import functools
import math

import jax
import jax.numpy as jnp
from jax import lax
from jax.experimental import pallas as pl
from jax.experimental.pallas import tpu as pltpu
from jax.sharding import PartitionSpec as P

eps_norm = 1e-06
far_steps = (12, 16, 23, 32, 46, 64, 91)
exact_mode = lax.Precision.HIGHEST
low_type = jnp.bfloat16
full_type = jnp.float32
log2_e = math.log2(math.e)
tile = 256
span = 3 * tile
ring = 1024
mask_gap = -(2.0**100)
vmem_most = 60 * 2**20


def bucket_of(relative):
    upper_half = jnp.where(relative > 0, 16, 0).astype(jnp.int32)
    distance = jnp.abs(relative)
    far_bucket = 8 + sum(((distance >= step_size).astype(jnp.int32) for step_size in far_steps))
    return upper_half + jnp.where(distance < 8, distance, far_bucket)


def rms_scaled(rows, gain):
    return rows * lax.rsqrt(jnp.mean(rows * rows, -1, keepdims=True) + eps_norm) * gain


def gelu_pair(rows):
    reach = math.sqrt(2.0 / math.pi)
    square = rows * rows
    turn = jnp.tanh(reach * rows * (1.0 + 0.044715 * square))
    share = 0.5 * (1.0 + turn)
    steep = 0.5 * (1.0 - turn * turn) * reach * (1.0 + 3.0 * 0.044715 * square)
    return (rows * share).astype(low_type), (share + rows * steep).astype(low_type)


def dot_rows(left, right):
    return jnp.dot(left, right, preferred_element_type=full_type)


def dot_outer(left, right):
    return lax.dot_general(
        left, right, (((0,), (0,)), ((), ())), preferred_element_type=full_type
    )


def dot_inner(left, right):
    return lax.dot_general(
        left, right, (((1,), (1,)), ((), ())), preferred_element_type=full_type
    )


def interleave_kernel(key_ref, value_ref, table_ref):
    rows = key_ref.shape[1]
    row = lax.broadcasted_iota(jnp.int32, (256, 256), 0)
    column = lax.broadcasted_iota(jnp.int32, (256, 256), 1)
    order = jnp.where(column == (row // 2 + (row % 2) * 128), 1.0, 0.0).astype(low_type)
    for part in range(rows // 256):
        low, high = pl.ds(part * 256, 128), pl.ds(part * 256 + 128, 128)
        both = jnp.concatenate(
            [
                jnp.concatenate([key_ref[0, low], key_ref[0, high]], 1),
                jnp.concatenate([value_ref[0, low], value_ref[0, high]], 1),
            ],
            0,
        )
        mixed = dot_rows(order, both).astype(low_type)
        table_ref[pl.ds(part * 512, 256), :] = mixed[:, :128]
        table_ref[pl.ds(part * 512 + 256, 256), :] = mixed[:, 128:]


def interleave(memory_keys, memory_values):
    heads, rows, width = memory_keys.shape
    step = min(2048, rows)
    spec = pl.BlockSpec((1, step, width), lambda h, i: (h, i, 0))
    return pl.pallas_call(
        interleave_kernel,
        grid=(heads, rows // step),
        in_specs=[spec, spec],
        out_specs=pl.BlockSpec((2 * step, width), lambda h, i: (h * (rows // step) + i, 0)),
        out_shape=jax.ShapeDtypeStruct((heads * rows * 2, width), low_type),
        cost_estimate=pl.CostEstimate(
            flops=heads * rows * 4 * 256 * width,
            bytes_accessed=heads * rows * width * 8,
            transcendentals=0,
        ),
        name="interleave",
    )(memory_keys, memory_values).reshape(heads, rows, 2, width)


def own_columns(picks):
    shape = (8, 8 * picks * 2)
    lane = lax.broadcasted_iota(jnp.int32, shape, 1)
    row = lax.broadcasted_iota(jnp.int32, shape, 0)
    return jnp.logical_and(lane // (2 * picks) == row, lane % 2 == 0)


def copy_rows(picked, first, table_ref, found_ref, start, count):
    for at in range(0, count, 8):
        rows_now = [
            table_ref[picked[(first + at + j) // 128, (first + at + j) % 128]] for j in range(8)
        ]
        for j in range(8):
            found_ref[start + at + j] = rows_now[j]
        yield


def recall_rows(picks, scale, own, query_ref, query_at, rows_ref, read_ref, read_at, tokens):
    wide = 8 * picks * 2
    groups = range(tokens // 8)
    scores = []
    for g in groups:
        rows = rows_ref[pl.ds(g * wide, wide), :]
        scores.append(dot_inner(query_ref[pl.ds(query_at + g * 8, 8), :], rows))
        yield
    shifted = []
    totals = []
    for g in groups:
        masked = jnp.where(own, scores[g] * (scale * log2_e), -jnp.inf)
        exponent = jnp.exp2(masked - jnp.max(masked, 1, keepdims=True))
        totals.append(jnp.sum(exponent, 1, keepdims=True))
        shifted.append(pltpu.roll(exponent, 1, 1).astype(low_type))
        yield
    for g in groups:
        rows = rows_ref[pl.ds(g * wide, wide), :]
        read_ref[pl.ds(read_at + g * 8, 8), :] = dot_rows(shifted[g], rows) / totals[g]
        yield


def weave(many, many_count, few, few_count):
    done = 0
    for number in range(few_count):
        until = (number + 1) * many_count // few_count
        while done < until:
            next(many)
            done += 1
        next(few)


def gather_kernel(
    picks, scale, index_hbm, table_hbm, now_ref, before_ref, found_ref, late_ref, early_ref,
    table_ref, table_sems, index_a, index_b, index_sems, stage_ref, stage_sems,
):
    step = pl.program_id(0)
    steps = pl.num_programs(0) - 1
    heads = table_sems.shape[0]
    blocks = steps // heads
    chunk = found_ref.shape[0] // 2
    rows = table_ref.shape[0] // heads
    slots = (index_a, index_b)
    part = chunk // 2
    tokens = part // picks
    own = own_columns(picks)
    flat = found_ref.reshape(4 * chunk, 128)

    def index_copy(number, slot):
        return pltpu.make_async_copy(index_hbm.at[number], slots[slot], index_sems.at[slot])

    def table_copy(number):
        where = pl.ds(number * rows, rows)
        return pltpu.make_async_copy(
            table_hbm.at[where], table_ref.at[where], table_sems.at[number]
        )

    def stage_copy(number):
        return pltpu.make_async_copy(
            flat.at[pl.ds(number * 2 * part, 2 * part)], stage_ref.at[number], stage_sems.at[number]
        )

    def reads(number, query_ref, read_ref):
        return recall_rows(
            picks, scale, own, query_ref, (number % 2) * tokens, stage_ref.at[number], read_ref,
            (number % 2) * tokens, tokens,
        )

    @pl.when(step == 0)
    def start_all():
        index_copy(0, 0).start()
        index_copy(1, 1).start()
        for number in range(heads):
            table_copy(number).start()
        stage_copy(2).start()
        stage_copy(3).start()

    @pl.when(jnp.logical_and(step < steps, step % blocks == 0))
    def wait_table():
        table_copy(step // blocks).wait()

    @pl.when(step < steps)
    def work():
        following = jnp.minimum(step + 1, steps - 1)
        for number in range(4):
            slot = number // 2
            if number % 2 == 0:
                index_copy(2 * step + slot, slot).wait()
            finished = (number + 2) % 4
            stage_copy(finished).wait()
            copied = copy_rows(
                slots[slot], (number % 2) * part, table_ref, found_ref, number * part, part
            )
            if number < 2:
                read = reads(finished, before_ref, late_ref)
            else:
                read = reads(finished, now_ref, early_ref)
            weave(copied, part // 8, read, 3 * (tokens // 8))
            stage_copy(number).start()
            if number % 2 == 1:
                index_copy(2 * following + slot, slot).start()

    @pl.when(step == steps)
    def finish():
        for number in (2, 3):
            stage_copy(number).wait()
            for unused in reads(number, before_ref, late_ref):
                pass
        for slot in range(2):
            index_copy(2 * (steps - 1) + slot, slot).wait()


def gather_found(index_rows, table, queries, picks, scale):
    heads, rows, unused, width = table.shape
    tokens = queries.shape[0]
    half = 128
    blocks = tokens // (2 * half)
    steps = heads * blocks
    chunk = half * picks

    def query_spec(shift):
        def place(t):
            at = jnp.clip(t - shift, 0, steps - 1)
            return (2 * (at % blocks) + shift, at // blocks)

        return pl.BlockSpec((half, width), place)

    return pl.pallas_call(
        functools.partial(gather_kernel, picks, scale),
        grid=(steps + 1,),
        in_specs=[
            pl.BlockSpec(memory_space=pl.ANY),
            pl.BlockSpec(memory_space=pl.ANY),
            query_spec(0),
            query_spec(1),
        ],
        out_specs=[
            pl.BlockSpec((2 * chunk, 2, width), lambda t: (jnp.minimum(t, steps - 1), 0, 0)),
            pl.BlockSpec((half, width), lambda t: (jnp.maximum(t - 1, 0), 0)),
            pl.BlockSpec((half, width), lambda t: (jnp.minimum(t, steps - 1), 0)),
        ],
        out_shape=[
            jax.ShapeDtypeStruct((heads * tokens * picks, 2, width), low_type),
            jax.ShapeDtypeStruct((heads * tokens // 2, width), full_type),
            jax.ShapeDtypeStruct((heads * tokens // 2, width), full_type),
        ],
        scratch_shapes=[
            pltpu.VMEM((heads * rows, 2, width), low_type),
            pltpu.SemaphoreType.DMA((heads,)),
            pltpu.SMEM((chunk // 128, 128), jnp.int32),
            pltpu.SMEM((chunk // 128, 128), jnp.int32),
            pltpu.SemaphoreType.DMA((2,)),
            pltpu.VMEM((4, chunk, width), low_type),
            pltpu.SemaphoreType.DMA((4,)),
        ],
        compiler_params=pltpu.CompilerParams(vmem_limit_bytes=vmem_most),
        cost_estimate=pl.CostEstimate(
            flops=0, bytes_accessed=4 * heads * tokens * picks * width * 4, transcendentals=0
        ),
        name="gather_found",
    )(
        index_rows.reshape(-1, chunk // 128, 128), table.reshape(heads * rows, 2, width), queries,
        queries,
    )


def recall_back_kernel(
    picks, scale, gate_ref, found_ref, query_ref, delta_ref, query_delta_ref, sums_ref
):
    tokens = query_ref.shape[0]
    wide = 8 * picks * 2
    own = own_columns(picks)
    gate = gate_ref[0]
    groups = range(tokens // 8)
    both = []
    for g in groups:
        rows = jnp.concatenate(
            [query_ref[pl.ds(g * 8, 8), :], delta_ref[pl.ds(g * 8, 8), :]], 0
        )
        both.append(dot_inner(rows, found_ref[pl.ds(g * wide, wide), :]))
    gained = jnp.zeros((8, 1), full_type)
    for g in groups:
        masked = jnp.where(own, both[g][:8] * (scale * log2_e), -jnp.inf)
        exponent = jnp.exp2(masked - jnp.max(masked, 1, keepdims=True))
        weights = exponent / jnp.sum(exponent, 1, keepdims=True)
        reads = pltpu.roll(both[g][8:], wide - 1, 1)
        expected = jnp.sum(weights * reads, 1, keepdims=True)
        gained = gained + expected
        score_delta = (weights * (reads - expected)).astype(low_type)
        query_delta_ref[pl.ds(g * 8, 8), :] = dot_rows(
            score_delta, found_ref[pl.ds(g * wide, wide), :]
        ) * (scale * gate)

    @pl.when(pl.program_id(0) == 0)
    def clear():
        sums_ref[...] = jnp.zeros(sums_ref.shape, full_type)

    sums_ref[0] += jnp.broadcast_to(gained, (8, 128))


def recall_back(
    found, queries, mixed_delta, gates, head, heads_now, carried, after, kept, picks, scale
):
    tokens = queries.shape[0]
    width = mixed_delta.shape[1] // gates.shape[0]
    start, count = heads_now
    step = min(512, tokens)
    blocks = tokens // step
    rows_spec = pl.BlockSpec((step, width), lambda i: (i, head))
    out_spec = pl.BlockSpec((step, width), lambda i: (i, head - start))
    anywhere = pl.BlockSpec(memory_space=pl.ANY)
    extra = [kept] if kept is not None else []
    first = 4 + len(extra)

    def kernel(gate_ref, found_ref, query_ref, delta_ref, *rest):
        query_delta_ref, sums_ref = rest[len(extra) + len(carried) + len(after) :][:2]
        recall_back_kernel(
            picks, scale, gate_ref, found_ref, query_ref, delta_ref, query_delta_ref, sums_ref
        )

    out = pl.pallas_call(
        kernel,
        grid=(blocks,),
        in_specs=[
            pl.BlockSpec(memory_space=pltpu.SMEM),
            pl.BlockSpec((step * picks * 2, width), lambda i: (head * blocks + i, 0)),
            rows_spec,
            rows_spec,
        ]
        + [anywhere] * (len(extra) + len(carried) + len(after)),
        out_specs=[out_spec, pl.BlockSpec((1, 8, 128), lambda i: (0, 0, 0))]
        + [anywhere] * len(carried),
        out_shape=[
            jax.ShapeDtypeStruct((tokens, count * width), full_type),
            jax.ShapeDtypeStruct((1, 8, 128), full_type),
        ]
        + [jax.ShapeDtypeStruct(part.shape, part.dtype) for part in carried],
        input_output_aliases=({4: 0} if extra else {})
        | {first + i: 2 + i for i in range(len(carried))},
        compiler_params=pltpu.CompilerParams(vmem_limit_bytes=vmem_most),
        cost_estimate=pl.CostEstimate(
            flops=0, bytes_accessed=tokens * picks * width * 8, transcendentals=0
        ),
        name="recall_back",
    )(gates[head : head + 1], found, queries, mixed_delta, *extra, *carried, *after)
    return out[0], out[1], list(out[2:])


def band(column_ref):
    wide = jnp.broadcast_to(column_ref[0], (tile, ring))
    return pltpu.roll(wide, 0, 1, stride=1, stride_axis=0)[:, :span]


def local_kernel(
    scale, gate_ref, far_ref, column_ref, query_ref, key_ref, value_ref, query_mask_ref,
    key_mask_ref, early_ref, late_ref, mixed_ref, bias_ref,
):
    head = pl.program_id(0)

    @pl.when(pl.program_id(1) == 0)
    def make_band():
        bias_ref[...] = band(column_ref)

    gate = gate_ref[head]
    count = query_ref.shape[0] // tile
    at = [pl.ds(t * tile, tile) for t in range(count)]
    keys = [jnp.concatenate([key_ref[a, :], key_mask_ref[0, a, :]], 1) for a in at]
    for t in range(count):
        rows = jnp.concatenate([query_ref[at[t], :], query_mask_ref[0, at[t], :]], 1)
        parts = []
        for j in range(count):
            step = j - t
            if step < -1:
                bias = far_ref[head, 0]
            elif step > 1:
                bias = far_ref[head, 1]
            else:
                bias = bias_ref[:, pl.ds((step + 1) * tile, tile)]
            parts.append(dot_inner(rows, keys[j]) * (scale * log2_e) + bias)
        top = jnp.max(functools.reduce(jnp.maximum, parts), 1, keepdims=True)
        parts = [jnp.exp2(part - top) for part in parts]
        total = jnp.sum(functools.reduce(jnp.add, parts), 1, keepdims=True)
        read = sum(dot_rows(parts[j].astype(low_type), value_ref[at[j], :]) for j in range(count))
        half = pl.ds(t * (tile // 2), tile // 2)
        recalled = jnp.concatenate([early_ref[half, :], late_ref[half, :]], 0)
        mixed_ref[at[t], :] = (gate * recalled + ((1.0 - gate) / total) * read).astype(low_type)


def local_read(projected, query_mask, key_mask, early, late, columns, far, gates, seq_len, scale):
    tokens, width = projected.shape
    heads = gates.shape[0]
    width = width // (3 * heads)
    sequences = tokens // seq_len
    half_spec = pl.BlockSpec((seq_len // 2, width), lambda h, s: (h * sequences + s, 0))

    def rows_of(shift):
        return pl.BlockSpec((seq_len, width), lambda h, s: (s, h + shift * heads))

    mask_spec = pl.BlockSpec((1, seq_len, 128), lambda h, s: (s, 0, 0))
    smem = pl.BlockSpec(memory_space=pltpu.SMEM)
    return pl.pallas_call(
        functools.partial(local_kernel, scale),
        grid=(heads, tokens // seq_len),
        in_specs=[
            smem,
            smem,
            pl.BlockSpec((1, 1, ring), lambda h, s: (h, 0, 0)),
            rows_of(0),
            rows_of(1),
            rows_of(2),
            mask_spec,
            mask_spec,
            half_spec,
            half_spec,
        ],
        out_specs=rows_of(0),
        out_shape=jax.ShapeDtypeStruct((tokens, heads * width), low_type),
        scratch_shapes=[pltpu.VMEM((tile, span), full_type)],
        compiler_params=pltpu.CompilerParams(vmem_limit_bytes=vmem_most),
        cost_estimate=pl.CostEstimate(
            flops=0, bytes_accessed=heads * tokens * seq_len * 20, transcendentals=0
        ),
        name="local_read",
    )(gates, far, columns, projected, projected, projected, query_mask, key_mask, early, late)


def local_back_kernel(
    scale, gate_ref, far_ref, column_ref, query_ref, key_ref, value_ref, query_mask_ref,
    key_mask_ref, delta_ref, recall_delta_ref, query_delta_ref, key_delta_ref, value_delta_ref,
    diagonal_ref, sums_ref, bias_ref, near_ref, key_sum_ref, value_sum_ref,
):
    head = pl.program_id(0)
    last = pl.program_id(1) == pl.num_programs(1) - 1

    @pl.when(pl.program_id(1) == 0)
    def make_band():
        bias_ref[...] = band(column_ref)
        near_ref[...] = jnp.zeros(near_ref.shape, full_type)
        sums_ref[...] = jnp.zeros(sums_ref.shape, full_type)

    gate = gate_ref[head]
    count = query_ref.shape[0] // tile
    at = [pl.ds(t * tile, tile) for t in range(count)]
    keys = [jnp.concatenate([key_ref[a, :], key_mask_ref[0, a, :]], 1) for a in at]
    turned = [key_ref[a, :].astype(full_type).T.astype(low_type) for a in at]
    gained = jnp.zeros((1, tile), full_type)
    far_sums = [jnp.zeros((8, tile), full_type) for side in range(2)]
    for t in range(count):
        rows = jnp.concatenate([query_ref[at[t], :], query_mask_ref[0, at[t], :]], 1)
        delta = ((1.0 - gate) * delta_ref[at[t], :].astype(full_type)).astype(low_type)
        parts = []
        for j in range(count):
            step = j - t
            if step < -1:
                bias = far_ref[head, 0]
            elif step > 1:
                bias = far_ref[head, 1]
            else:
                bias = bias_ref[:, pl.ds((1 - step) * tile, tile)]
            parts.append(dot_inner(keys[j], rows) * (scale * log2_e) + bias)
        top = jnp.max(functools.reduce(jnp.maximum, parts), 0, keepdims=True)
        parts = [jnp.exp2(part - top) for part in parts]
        total = jnp.sum(functools.reduce(jnp.add, parts), 0, keepdims=True)
        inverse = 1.0 / total
        parts = [part * inverse for part in parts]
        moves = [dot_inner(value_ref[at[j], :], delta) for j in range(count)]
        expected = jnp.sum(
            functools.reduce(jnp.add, [parts[j] * moves[j] for j in range(count)]),
            0,
            keepdims=True,
        )
        gained = gained + expected
        query_sum = None
        for j in range(count):
            step = j - t
            score_delta = parts[j] * (moves[j] - expected)
            if abs(step) > 1:
                side = 0 if step < 0 else 1
                far_sums[side] = far_sums[side] + jnp.sum(
                    score_delta.reshape(tile // 8, 8, tile), 0
                )
            else:
                near_ref[:, pl.ds((1 - step) * tile, tile)] += score_delta
            low_delta = score_delta.astype(low_type)
            value_part = dot_rows(parts[j].astype(low_type), delta)
            key_part = dot_rows(low_delta, query_ref[at[t], :])
            query_part = dot_rows(turned[j], low_delta)
            if t == 0:
                value_sum_ref[at[j], :] = value_part
                key_sum_ref[at[j], :] = key_part
            else:
                value_sum_ref[at[j], :] += value_part
                key_sum_ref[at[j], :] += key_part
            query_sum = query_part if j == 0 else query_sum + query_part
        query_delta_ref[at[t], :] = (
            query_sum.T * scale + recall_delta_ref[at[t], :]
        ).astype(low_type)
    key_delta_ref[...] = (key_sum_ref[...] * scale).astype(low_type)
    value_delta_ref[...] = value_sum_ref[...].astype(low_type)
    sums_ref[0, 0:1] += gained
    sums_ref[0, 8:16] += far_sums[0]
    sums_ref[0, 16:24] += far_sums[1]

    @pl.when(last)
    def fold_diagonals():
        total = jnp.zeros((8, ring), full_type)
        for g in range(tile // 8):
            part = jnp.concatenate(
                [near_ref[pl.ds(g * 8, 8), :], jnp.zeros((8, ring - span), full_type)], 1
            )
            total = total + (pltpu.roll(part, ring - 8 * g, 1) if g else part)
        row = lax.broadcasted_iota(jnp.int32, (8, ring), 0)
        for bit in (1, 2, 4):
            total = jnp.where((row & bit) != 0, pltpu.roll(total, ring - bit, 1), total)
        diagonal_ref[0] = total


def local_back(
    projected, query_mask, key_mask, mixed_delta, recall_delta, columns, far, gates, seq_len, scale,
    heads_now, carried, after,
):
    tokens = mixed_delta.shape[0]
    heads = gates.shape[0]
    width = mixed_delta.shape[1] // heads
    start, count = heads_now
    anywhere = pl.BlockSpec(memory_space=pl.ANY)
    chosen = slice(start, start + count)

    def rows_of(shift):
        return pl.BlockSpec((seq_len, width), lambda h, s: (s, h + start + shift * heads))

    own_spec = pl.BlockSpec((seq_len, width), lambda h, s: (s, h))

    def kernel(*refs):
        inputs, rest = refs[:10], refs[10 + len(carried) + len(after) :]
        local_back_kernel(scale, *inputs, *rest[:5], *rest[5 + len(carried) :])

    mask_spec = pl.BlockSpec((1, seq_len, 128), lambda h, s: (s, 0, 0))
    smem = pl.BlockSpec(memory_space=pltpu.SMEM)
    rows_shape = jax.ShapeDtypeStruct((tokens, count * width), low_type)
    out = pl.pallas_call(
        kernel,
        grid=(count, tokens // seq_len),
        in_specs=[
            smem,
            smem,
            pl.BlockSpec((1, 1, ring), lambda h, s: (h, 0, 0)),
            rows_of(0),
            rows_of(1),
            rows_of(2),
            mask_spec,
            mask_spec,
            rows_of(0),
            own_spec,
        ]
        + [anywhere] * (len(carried) + len(after)),
        out_specs=[
            own_spec,
            own_spec,
            own_spec,
            pl.BlockSpec((1, 8, ring), lambda h, s: (h, 0, 0)),
            pl.BlockSpec((1, 24, tile), lambda h, s: (h, 0, 0)),
        ]
        + [anywhere] * len(carried),
        out_shape=[
            rows_shape,
            rows_shape,
            rows_shape,
            jax.ShapeDtypeStruct((count, 8, ring), full_type),
            jax.ShapeDtypeStruct((count, 24, tile), full_type),
        ]
        + [jax.ShapeDtypeStruct(part.shape, part.dtype) for part in carried],
        input_output_aliases={10 + i: 5 + i for i in range(len(carried))},
        scratch_shapes=[
            pltpu.VMEM((tile, span), full_type),
            pltpu.VMEM((tile, span), full_type),
            pltpu.VMEM((seq_len, width), full_type),
            pltpu.VMEM((seq_len, width), full_type),
        ],
        compiler_params=pltpu.CompilerParams(vmem_limit_bytes=vmem_most),
        cost_estimate=pl.CostEstimate(
            flops=0, bytes_accessed=count * tokens * seq_len * 40, transcendentals=0
        ),
        name="local_back",
    )(
        gates[chosen], far[chosen], columns[chosen], projected, projected, projected, query_mask,
        key_mask, mixed_delta, recall_delta, *carried, *after,
    )
    return list(out[:3]), out[3], out[4], list(out[5:])


def mask_rows(block_ids):
    level = jnp.arange(128, dtype=jnp.int32)
    gap = block_ids[:, :, None] - level
    query_mask = jnp.where((gap >= 0) & (gap <= 1), 0.0, mask_gap).astype(low_type)
    key_mask = (gap == 0).astype(low_type)
    return query_mask, key_mask


def fetch(rows):
    group = lax.axis_size("tensor")
    return [rows] + [
        lax.ppermute(rows, "tensor", [((i + k) % group, i) for i in range(group)])
        for k in range(1, group)
    ]


def in_order(shares):
    group = lax.axis_size("tensor")
    rows = shares[0].shape[0]
    whole = jnp.zeros((group * rows,) + shares[0].shape[1:], shares[0].dtype)
    for k in range(group):
        start = ((lax.axis_index("tensor") + k) % group) * rows
        whole = lax.dynamic_update_slice_in_dim(whole, shares[k], start, 0)
    return whole


def share_of(whole, k, rows):
    start = ((lax.axis_index("tensor") + k) % lax.axis_size("tensor")) * rows
    return lax.dynamic_slice_in_dim(whole, start, rows, 0)


def fold(term, piece):
    group = lax.axis_size("tensor")
    sent = [
        lax.ppermute(
            term(piece(k)).astype(low_type), "tensor", [(i, (i + k) % group) for i in range(group)]
        )
        for k in range(1, group)
    ]
    return sum((part.astype(full_type) for part in sent), term(piece(0)))


def bit_orders():
    bits = lax.axis_size("dp").bit_length() - 1
    near = [(0, 1, 2), (1, 2, 0), (2, 0, 1)]
    return [list(head) + list(range(3, bits)) for head in near]


def swap_over(rows, bit):
    return lax.ppermute(rows, "dp", [(i, i ^ (1 << bit)) for i in range(lax.axis_size("dp"))])


def side_of(bit):
    return (lax.axis_index("dp") >> bit) & 1


def halve_step(parts, orders, step):
    kept, sent = [], []
    for part, order in zip(parts, orders):
        half = part.shape[0] // 2
        side = side_of(order[step])
        sent.append(
            swap_over(
                lax.dynamic_slice_in_dim(part, (1 - side) * half, half, 0), order[step]
            )
        )
        kept.append(lax.dynamic_slice_in_dim(part, side * half, half, 0))
    return kept, sent


def add_low(kept, sent):
    return [
        (a.astype(full_type) + b.astype(full_type)).astype(low_type) for a, b in zip(kept, sent)
    ]


def double_all(parts, beside):
    orders = bit_orders()
    for step in reversed(range(len(orders[0]))):
        got = [swap_over(part, order[step]) for part, order in zip(parts, orders)]
        if step == 1:
            got[2], beside = lax.optimization_barrier((got[2], beside))
        wider = []
        for part, other, order in zip(parts, got, orders):
            rows = part.shape[0]
            side = side_of(order[step])
            whole = jnp.zeros((2 * rows,) + part.shape[1:], part.dtype)
            whole = lax.dynamic_update_slice_in_dim(whole, part, side * rows, 0)
            wider.append(lax.dynamic_update_slice_in_dim(whole, other, (1 - side) * rows, 0))
        parts = wider
    return parts, beside


def pack(parts):
    width = min(part.shape[1] for part in parts)
    return jnp.concatenate(
        [
            part[:, start : start + width]
            for part in parts
            for start in range(0, part.shape[1], width)
        ],
        0,
    )


def gather_all(packed, parts, orders):
    whole = lax.all_gather(packed, "dp", axis=0)
    width = packed.shape[1]
    wide = []
    start = 0
    for part, order in zip(parts, orders):
        bits = len(order)
        rows = part.shape[0]
        columns = []
        for unused in range(part.shape[1] // width):
            piece = whole[:, start : start + rows].reshape((2,) * bits + (rows, width))
            piece = piece.transpose([bits - 1 - bit for bit in order] + [bits, bits + 1])
            columns.append(piece.reshape(-1, width))
            start += rows
        wide.append(jnp.concatenate(columns, 1).astype(full_type))
    return wide


def body(
    tokens,
    block_ids,
    memory_index,
    memory_keys,
    memory_values,
    attn_gain,
    query_weight,
    key_weight,
    value_weight,
    output_weight,
    position_table,
    memory_gate,
    mlp_gain,
    hidden_weight,
    return_weight,
    grad_output,
):
    share_rows = tokens.shape[0]
    seq_len = block_ids.shape[1]
    head_count, memory_rows, head_width = memory_keys.shape
    picks = memory_index.shape[2]
    inner_width = head_count * head_width
    scale = head_width ** (-0.5)

    offsets = jnp.arange(head_count, dtype=jnp.int32) * memory_rows
    index_rows = memory_index.transpose(1, 0, 2) + offsets[:, None, None]
    table = interleave(memory_keys, memory_values)

    token_full = tokens.astype(full_type)
    normed_rows = rms_scaled(token_full, attn_gain).astype(low_type)
    normed = lax.all_gather(normed_rows, "tensor", axis=0, tiled=True)
    joined = jnp.concatenate([query_weight, key_weight, value_weight], 1)
    projected = dot_rows(normed, joined).astype(low_type)
    found, late, early = gather_found(index_rows, table, projected, picks, scale)
    found = found.reshape(-1, head_width)

    query_mask, key_mask = mask_rows(block_ids)
    place = jnp.arange(ring, dtype=jnp.int32)
    place = jnp.where(place < span, place, place - ring)
    ahead = bucket_of(place - tile)
    behind = bucket_of(tile - place)
    level = jnp.arange(32, dtype=jnp.int32)
    ahead_hot = (ahead[:, None] == level).astype(full_type)
    behind_hot = (behind[:, None] == level).astype(full_type)
    scaled_table = position_table * log2_e
    ahead_columns = jnp.dot(ahead_hot, scaled_table, precision=exact_mode).T[:, None, :]
    behind_columns = jnp.dot(behind_hot, scaled_table, precision=exact_mode).T[:, None, :]
    far = jnp.stack([scaled_table[15], scaled_table[31]], 1)
    gates = jax.nn.sigmoid(memory_gate)

    mixed_rows = local_read(
        projected, query_mask, key_mask, early, late, ahead_columns, far, gates, seq_len, scale
    )
    middle = token_full + fold(
        lambda rows: dot_rows(rows, output_weight), lambda k: share_of(mixed_rows, k, share_rows)
    )
    second_rows = rms_scaled(middle, mlp_gain).astype(low_type)
    grad_full = jnp.concatenate(fetch(grad_output), 0)
    second = jnp.concatenate(fetch(second_rows), 0)
    active, slope = gelu_pair(dot_rows(second, hidden_weight))
    slope = lax.optimization_barrier(slope)
    orders = bit_orders()
    steps = len(orders[0])

    return_low = dot_outer(active, grad_full).astype(low_type)
    return_half = return_low.shape[0] // 2
    kept_back, sent_back = halve_step(
        [return_low[:return_half], return_low[return_half:]], orders[1:], 0
    )
    active_delta = dot_inner(grad_full, return_weight)
    hidden_delta = (active_delta * slope.astype(full_type)).astype(low_type)
    second_delta = fold(
        lambda rows: dot_inner(rows, hidden_weight),
        lambda k: lax.slice_in_dim(hidden_delta, k * share_rows, (k + 1) * share_rows),
    )
    hidden_half = hidden_delta.shape[1] // 2
    hidden_parts = [
        dot_outer(second, hidden_delta[:, :hidden_half]).astype(low_type),
        dot_outer(second, hidden_delta[:, hidden_half:]).astype(low_type),
    ]
    kept, sent = halve_step(hidden_parts, orders[:2], 0)

    kept_back, kept = lax.optimization_barrier((kept_back, kept))
    kept_back, sent_back = halve_step(add_low(kept_back, sent_back), orders[1:], 1)

    second_back = jax.vjp(rms_scaled, middle, mlp_gain)[1]
    middle_part, mlp_gain_part = second_back(second_delta)
    middle_delta = grad_output.astype(full_type) + middle_part
    middle_low = middle_delta.astype(low_type)
    kept, kept_back, middle_low = lax.optimization_barrier((kept, kept_back, middle_low))
    kept, sent = halve_step(add_low(kept, sent), orders[:2], 1)
    kept_back, sent_back = halve_step(add_low(kept_back, sent_back), orders[1:], 2)
    middle_full = in_order(fetch(middle_low))
    mixed_delta = dot_inner(middle_full, output_weight).astype(low_type)
    kept, kept_back, mixed_delta = lax.optimization_barrier((kept, kept_back, mixed_delta))
    kept, sent = halve_step(add_low(kept, sent), orders[:2], 2)
    kept_back, sent_back = halve_step(add_low(kept_back, sent_back), orders[1:], 3)
    taken = 2
    for step in range(4, steps):
        kept_back, sent_back = halve_step(add_low(kept_back, sent_back), orders[1:], step)
    layer_output = (
        middle
        + fold(
            lambda rows: dot_rows(rows, return_weight),
            lambda k: lax.slice_in_dim(active, k * share_rows, (k + 1) * share_rows),
        )
    ).astype(low_type)

    shards, packed = [], []
    half_heads = max(1, head_count // 2)
    recall_gain, local_gain, diagonals, far_left, far_right = [], [], [], [], []
    attn_gain_part = jnp.zeros_like(attn_gain)
    joined_parts = []
    early_kept, early_sent, early_taken = [], [], 0
    early_shards = []
    normed_terms = []

    def early_step(parts):
        if early_taken + 1 < steps:
            return *halve_step(add_low(parts, early_sent), orders, early_taken + 1), early_taken + 1
        return parts, early_sent, early_taken

    for start in range(0, head_count, half_heads):
        recall_delta = None
        for head in range(start, start + half_heads):
            count_kept = len(kept)
            recall_delta, head_sums, passed = recall_back(
                found, projected, mixed_delta, gates, head, (start, half_heads), kept + early_kept,
                packed, recall_delta, picks, scale,
            )
            recall_gain.append(jnp.sum(head_sums[:, :, 0], 1))
            if early_kept:
                early_kept, early_sent, early_taken = early_step(passed[count_kept:])
            if shards:
                continue
            kept = passed[:count_kept]
            if taken < steps - 1:
                taken += 1
                kept, sent = halve_step(add_low(kept, sent), orders[:2], taken)
            else:
                shards = add_low(kept, sent) + add_low(kept_back, sent_back)
                packed = [pack(shards)]
                kept = []
        deltas, diagonal_now, local_sums, passed = local_back(
            projected, query_mask, key_mask, mixed_delta, recall_delta, behind_columns, far, gates,
            seq_len, scale, (start, half_heads), early_kept, packed,
        )
        diagonals.append(diagonal_now)
        local_gain.append(jnp.sum(local_sums[:, 0], 1))
        far_left.append(jnp.sum(local_sums[:, 8:16], (1, 2)))
        far_right.append(jnp.sum(local_sums[:, 16:24], (1, 2)))
        if early_kept:
            early_kept = passed
            while early_taken + 1 < steps:
                early_kept, early_sent, early_taken = early_step(early_kept)
            early_shards = add_low(early_kept, early_sent)
            early_kept = []
        columns = slice(start * head_width, (start + half_heads) * head_width)
        weights_now = jnp.concatenate(
            [query_weight[:, columns], key_weight[:, columns], value_weight[:, columns]], 1
        )
        project_delta = jnp.concatenate(deltas, 1)
        joined_part = dot_outer(normed, project_delta)
        attn_gain_part += jnp.sum(joined_part * weights_now.astype(full_type), 1) / attn_gain
        normed_terms.append((project_delta, weights_now))
        if start + half_heads < head_count:
            joined_low = joined_part.astype(low_type)
            joined_half = joined_low.shape[0] // 2
            early_kept, early_sent = halve_step(
                [joined_low[:joined_half], joined_low[joined_half:]], orders, 0
            )
    while taken < steps - 1:
        taken += 1
        kept, sent = halve_step(add_low(kept, sent), orders[:2], taken)
    if not shards:
        shards = add_low(kept, sent) + add_low(kept_back, sent_back)
        packed = [pack(shards)]
    hidden_low_sum, hidden_high_sum, return_low_sum, return_high_sum = gather_all(
        packed[0], shards, orders[:2] + orders[1:]
    )
    hidden_sum = jnp.concatenate([hidden_low_sum, hidden_high_sum], 1)
    return_sum = jnp.concatenate([return_low_sum, return_high_sum], 0)
    gate_part = gates * (1.0 - gates) * jnp.concatenate(recall_gain)
    gate_part = gate_part - gates * jnp.concatenate(local_gain)
    table_part = jnp.dot(
        jnp.sum(jnp.concatenate(diagonals, 0), 1), behind_hot, precision=exact_mode
    )
    table_part = (
        table_part
        + jnp.concatenate(far_left)[:, None] * (level == 15)
        + jnp.concatenate(far_right)[:, None] * (level == 31)
    )
    model_width = tokens.shape[1]
    small = jnp.concatenate([table_part.reshape(-1), gate_part])
    small = jnp.pad(small, (0, model_width - small.shape[0]))
    extra = jnp.stack([attn_gain_part, mlp_gain_part, small], 1)
    extra = jnp.pad(extra, ((0, 0), (0, 125)))
    joined_low = jnp.concatenate([joined_part, extra], 1).astype(low_type)
    joined_half = joined_low.shape[0] // 2
    last = [
        joined_low[:joined_half],
        joined_low[joined_half:],
        dot_outer(mixed_rows, middle_full).astype(low_type),
    ]
    for step in range(steps):
        last = add_low(*halve_step(last, orders, step))
    if early_shards:
        last[:2] = [jnp.concatenate(pair, 1) for pair in zip(early_shards, last[:2])]
    last, (hidden_sum, return_sum) = double_all(last, (hidden_sum, return_sum))
    *joined_sum, output_sum = last

    def normed_term(k):
        terms = [
            dot_inner(share_of(delta, k, share_rows), weights) for delta, weights in normed_terms
        ]
        return functools.reduce(jnp.add, terms)

    normed_delta = fold(lambda term: term, normed_term)
    first_back = jax.vjp(rms_scaled, token_full, attn_gain)[1]
    tokens_grad = (middle_delta + first_back(normed_delta)[0]).astype(low_type)

    def joined_columns(start, stop):
        return jnp.concatenate([part[:, start:stop].astype(full_type) for part in joined_sum], 0)

    last_columns = joined_columns(3 * inner_width, 3 * inner_width + 128)
    gains = sum(fetch(last_columns[:, :2].T))
    small_sum = last_columns[:, 2]
    table_size = head_count * 32
    half_width = half_heads * head_width

    def weight_grad(which):
        blocks = [
            joined_columns(3 * first + which * half_width, 3 * first + (which + 1) * half_width)
            for first in range(0, inner_width, half_width)
        ]
        return jnp.concatenate(blocks, 1)

    return (
        layer_output,
        tokens_grad,
        gains[0],
        weight_grad(0),
        weight_grad(1),
        weight_grad(2),
        output_sum.astype(full_type),
        small_sum[:table_size].reshape(head_count, 32).T,
        small_sum[table_size : table_size + head_count],
        gains[1],
        hidden_sum,
        return_sum,
    )


def solution(mesh):
    def run(*arrays):
        with jax.sharding.use_abstract_mesh(mesh.abstract_mesh):
            return jax.shard_map(
                body,
                mesh=mesh,
                in_specs=(
                    P(("dp", "tensor"), None),
                    P("dp", None),
                    P("dp", "tensor", None),
                    P("tensor", None, None),
                    P("tensor", None, None),
                    P(),
                    P(None, "tensor"),
                    P(None, "tensor"),
                    P(None, "tensor"),
                    P("tensor", None),
                    P(None, "tensor"),
                    P("tensor"),
                    P(),
                    P(None, "tensor"),
                    P("tensor", None),
                    P(("dp", "tensor"), None),
                ),
                out_specs=(
                    P(("dp", "tensor"), None),
                    P(("dp", "tensor"), None),
                    P(),
                    P(None, "tensor"),
                    P(None, "tensor"),
                    P(None, "tensor"),
                    P("tensor", None),
                    P(None, "tensor"),
                    P("tensor"),
                    P(),
                    P(None, "tensor"),
                    P("tensor", None),
                ),
                check_vma=False,
            )(*arrays)

    return run
```

```python
import functools
import math

import jax
import jax.numpy as jnp
from jax import lax
from jax.experimental import pallas as pl
from jax.experimental.pallas import tpu as pltpu
from jax.sharding import PartitionSpec as P

eps_norm = 1e-06
far_steps = (12, 16, 23, 32, 46, 64, 91)
exact_mode = lax.Precision.HIGHEST
low_type = jnp.bfloat16
full_type = jnp.float32
log2_e = math.log2(math.e)
tile = 256
span = 3 * tile
ring = 1024
mask_gap = -(2.0**100)
vmem_most = 60 * 2**20


def bucket_of(relative):
    upper_half = jnp.where(relative > 0, 16, 0).astype(jnp.int32)
    distance = jnp.abs(relative)
    far_bucket = 8 + sum(((distance >= step_size).astype(jnp.int32) for step_size in far_steps))
    return upper_half + jnp.where(distance < 8, distance, far_bucket)


def rms_scaled(rows, gain):
    return rows * lax.rsqrt(jnp.mean(rows * rows, -1, keepdims=True) + eps_norm) * gain


def gelu_pair(rows):
    reach = math.sqrt(2.0 / math.pi)
    square = rows * rows
    turn = jnp.tanh(reach * rows * (1.0 + 0.044715 * square))
    share = 0.5 * (1.0 + turn)
    steep = 0.5 * (1.0 - turn * turn) * reach * (1.0 + 3.0 * 0.044715 * square)
    return (rows * share).astype(low_type), (share + rows * steep).astype(low_type)


def dot_rows(left, right):
    return jnp.dot(left, right, preferred_element_type=full_type)


def dot_outer(left, right):
    return lax.dot_general(
        left, right, (((0,), (0,)), ((), ())), preferred_element_type=full_type
    )


def dot_inner(left, right):
    return lax.dot_general(
        left, right, (((1,), (1,)), ((), ())), preferred_element_type=full_type
    )


def interleave_kernel(key_ref, value_ref, table_ref):
    rows = key_ref.shape[1]
    row = lax.broadcasted_iota(jnp.int32, (256, 256), 0)
    column = lax.broadcasted_iota(jnp.int32, (256, 256), 1)
    order = jnp.where(column == (row // 2 + (row % 2) * 128), 1.0, 0.0).astype(low_type)
    for part in range(rows // 256):
        low, high = pl.ds(part * 256, 128), pl.ds(part * 256 + 128, 128)
        both = jnp.concatenate(
            [
                jnp.concatenate([key_ref[0, low], key_ref[0, high]], 1),
                jnp.concatenate([value_ref[0, low], value_ref[0, high]], 1),
            ],
            0,
        )
        mixed = dot_rows(order, both).astype(low_type)
        table_ref[pl.ds(part * 512, 256), :] = mixed[:, :128]
        table_ref[pl.ds(part * 512 + 256, 256), :] = mixed[:, 128:]


def interleave(memory_keys, memory_values):
    heads, rows, width = memory_keys.shape
    step = min(8192, rows)
    spec = pl.BlockSpec((1, step, width), lambda h, i: (h, i, 0))
    return pl.pallas_call(
        interleave_kernel,
        grid=(heads, rows // step),
        in_specs=[spec, spec],
        out_specs=pl.BlockSpec((2 * step, width), lambda h, i: (h * (rows // step) + i, 0)),
        out_shape=jax.ShapeDtypeStruct((heads * rows * 2, width), low_type),
        compiler_params=pltpu.CompilerParams(vmem_limit_bytes=vmem_most),
        cost_estimate=pl.CostEstimate(
            flops=heads * rows * 4 * 256 * width,
            bytes_accessed=heads * rows * width * 8,
            transcendentals=0,
        ),
        name="interleave",
    )(memory_keys, memory_values).reshape(heads, rows, 2, width)


def own_columns(picks):
    shape = (8, 8 * picks * 2)
    lane = lax.broadcasted_iota(jnp.int32, shape, 1)
    row = lax.broadcasted_iota(jnp.int32, shape, 0)
    return jnp.logical_and(lane // (2 * picks) == row, lane % 2 == 0)


def copy_rows(picked, first, table_ref, found_ref, start, count):
    for at in range(0, count, 8):
        rows_now = [
            table_ref[picked[(first + at + j) // 128, (first + at + j) % 128]] for j in range(8)
        ]
        for j in range(8):
            found_ref[start + at + j] = rows_now[j]
        yield


def recall_rows(picks, scale, own, query_ref, query_at, rows_ref, read_ref, read_at, tokens):
    wide = 8 * picks * 2
    groups = range(tokens // 8)
    scores = []
    for g in groups:
        rows = rows_ref[pl.ds(g * wide, wide), :]
        scores.append(dot_inner(query_ref[pl.ds(query_at + g * 8, 8), :], rows))
        yield
    shifted = []
    totals = []
    for g in groups:
        masked = jnp.where(own, scores[g] * (scale * log2_e), -jnp.inf)
        exponent = jnp.exp2(masked - jnp.max(masked, 1, keepdims=True))
        totals.append(jnp.sum(exponent, 1, keepdims=True))
        shifted.append(pltpu.roll(exponent, 1, 1).astype(low_type))
        yield
    for g in groups:
        rows = rows_ref[pl.ds(g * wide, wide), :]
        read_ref[pl.ds(read_at + g * 8, 8), :] = dot_rows(shifted[g], rows) / totals[g]
        yield


def weave(many, many_count, few, few_count):
    done = 0
    for number in range(few_count):
        until = (number + 1) * many_count // few_count
        while done < until:
            next(many)
            done += 1
        next(few)


def gather_kernel(
    picks, scale, index_hbm, table_hbm, now_ref, before_ref, found_ref, late_ref, early_ref,
    table_ref, table_sems, index_a, index_b, index_sems, stage_ref, stage_sems,
):
    step = pl.program_id(0)
    steps = pl.num_programs(0) - 1
    heads = table_sems.shape[0]
    blocks = steps // heads
    chunk = found_ref.shape[0] // 2
    rows = table_ref.shape[0] // heads
    slots = (index_a, index_b)
    part = chunk // 2
    tokens = part // picks
    own = own_columns(picks)
    flat = found_ref.reshape(4 * chunk, 128)

    def index_copy(number, slot):
        return pltpu.make_async_copy(index_hbm.at[number], slots[slot], index_sems.at[slot])

    def table_copy(number):
        where = pl.ds(number * rows, rows)
        return pltpu.make_async_copy(
            table_hbm.at[where], table_ref.at[where], table_sems.at[number]
        )

    def stage_copy(number):
        return pltpu.make_async_copy(
            flat.at[pl.ds(number * 2 * part, 2 * part)], stage_ref.at[number], stage_sems.at[number]
        )

    def reads(number, query_ref, read_ref):
        return recall_rows(
            picks, scale, own, query_ref, (number % 2) * tokens, stage_ref.at[number], read_ref,
            (number % 2) * tokens, tokens,
        )

    @pl.when(step == 0)
    def start_all():
        index_copy(0, 0).start()
        index_copy(1, 1).start()
        for number in range(heads):
            table_copy(number).start()
        stage_copy(2).start()
        stage_copy(3).start()

    @pl.when(jnp.logical_and(step < steps, step % blocks == 0))
    def wait_table():
        table_copy(step // blocks).wait()

    @pl.when(step < steps)
    def work():
        following = jnp.minimum(step + 1, steps - 1)
        for number in range(4):
            slot = number // 2
            if number % 2 == 0:
                index_copy(2 * step + slot, slot).wait()
            finished = (number + 2) % 4
            stage_copy(finished).wait()
            copied = copy_rows(
                slots[slot], (number % 2) * part, table_ref, found_ref, number * part, part
            )
            if number < 2:
                read = reads(finished, before_ref, late_ref)
            else:
                read = reads(finished, now_ref, early_ref)
            weave(copied, part // 8, read, 3 * (tokens // 8))
            stage_copy(number).start()
            if number % 2 == 1:
                index_copy(2 * following + slot, slot).start()

    @pl.when(step == steps)
    def finish():
        for number in (2, 3):
            stage_copy(number).wait()
            for unused in reads(number, before_ref, late_ref):
                pass
        for slot in range(2):
            index_copy(2 * (steps - 1) + slot, slot).wait()


def gather_found(index_rows, table, queries, picks, scale):
    heads, rows, unused, width = table.shape
    tokens = queries.shape[0]
    half = 128
    blocks = tokens // (2 * half)
    steps = heads * blocks
    chunk = half * picks

    def query_spec(shift):
        def place(t):
            at = jnp.clip(t - shift, 0, steps - 1)
            return (2 * (at % blocks) + shift, at // blocks)

        return pl.BlockSpec((half, width), place)

    return pl.pallas_call(
        functools.partial(gather_kernel, picks, scale),
        grid=(steps + 1,),
        in_specs=[
            pl.BlockSpec(memory_space=pl.ANY),
            pl.BlockSpec(memory_space=pl.ANY),
            query_spec(0),
            query_spec(1),
        ],
        out_specs=[
            pl.BlockSpec((2 * chunk, 2, width), lambda t: (jnp.minimum(t, steps - 1), 0, 0)),
            pl.BlockSpec((half, width), lambda t: (jnp.maximum(t - 1, 0), 0)),
            pl.BlockSpec((half, width), lambda t: (jnp.minimum(t, steps - 1), 0)),
        ],
        out_shape=[
            jax.ShapeDtypeStruct((heads * tokens * picks, 2, width), low_type),
            jax.ShapeDtypeStruct((heads * tokens // 2, width), full_type),
            jax.ShapeDtypeStruct((heads * tokens // 2, width), full_type),
        ],
        scratch_shapes=[
            pltpu.VMEM((heads * rows, 2, width), low_type),
            pltpu.SemaphoreType.DMA((heads,)),
            pltpu.SMEM((chunk // 128, 128), jnp.int32),
            pltpu.SMEM((chunk // 128, 128), jnp.int32),
            pltpu.SemaphoreType.DMA((2,)),
            pltpu.VMEM((4, chunk, width), low_type),
            pltpu.SemaphoreType.DMA((4,)),
        ],
        compiler_params=pltpu.CompilerParams(vmem_limit_bytes=vmem_most),
        cost_estimate=pl.CostEstimate(
            flops=0, bytes_accessed=4 * heads * tokens * picks * width * 4, transcendentals=0
        ),
        name="gather_found",
    )(
        index_rows.reshape(-1, chunk // 128, 128), table.reshape(heads * rows, 2, width), queries,
        queries,
    )


def recall_back_kernel(
    picks, scale, gate_ref, found_ref, query_ref, delta_ref, query_delta_ref, sums_ref
):
    tokens = query_ref.shape[0]
    wide = 8 * picks * 2
    own = own_columns(picks)
    gate = gate_ref[0]
    groups = range(tokens // 8)
    both = []
    for g in groups:
        rows = jnp.concatenate(
            [query_ref[pl.ds(g * 8, 8), :], delta_ref[pl.ds(g * 8, 8), :]], 0
        )
        both.append(dot_inner(rows, found_ref[pl.ds(g * wide, wide), :]))
    gained = jnp.zeros((8, 1), full_type)
    for g in groups:
        masked = jnp.where(own, both[g][:8] * (scale * log2_e), -jnp.inf)
        exponent = jnp.exp2(masked - jnp.max(masked, 1, keepdims=True))
        weights = exponent / jnp.sum(exponent, 1, keepdims=True)
        reads = pltpu.roll(both[g][8:], wide - 1, 1)
        expected = jnp.sum(weights * reads, 1, keepdims=True)
        gained = gained + expected
        score_delta = (weights * (reads - expected)).astype(low_type)
        query_delta_ref[pl.ds(g * 8, 8), :] = dot_rows(
            score_delta, found_ref[pl.ds(g * wide, wide), :]
        ) * (scale * gate)

    @pl.when(pl.program_id(0) == 0)
    def clear():
        sums_ref[...] = jnp.zeros(sums_ref.shape, full_type)

    sums_ref[0] += jnp.broadcast_to(gained, (8, 128))


def recall_back(
    found, queries, mixed_delta, gates, head, carried, after, kept, heads, picks, scale
):
    tokens = queries.shape[0]
    width = mixed_delta.shape[1] // heads
    step = min(512, tokens)
    blocks = tokens // step
    rows_spec = pl.BlockSpec((step, width), lambda i: (i, head))
    anywhere = pl.BlockSpec(memory_space=pl.ANY)
    extra = [kept] if kept is not None else []
    first = 4 + len(extra)

    def kernel(gate_ref, found_ref, query_ref, delta_ref, *rest):
        query_delta_ref, sums_ref = rest[len(extra) + len(carried) + len(after) :][:2]
        recall_back_kernel(
            picks, scale, gate_ref, found_ref, query_ref, delta_ref, query_delta_ref, sums_ref
        )

    out = pl.pallas_call(
        kernel,
        grid=(blocks,),
        in_specs=[
            pl.BlockSpec(memory_space=pltpu.SMEM),
            pl.BlockSpec((step * picks * 2, width), lambda i: (head * blocks + i, 0)),
            rows_spec,
            rows_spec,
        ]
        + [anywhere] * (len(extra) + len(carried) + len(after)),
        out_specs=[rows_spec, pl.BlockSpec((1, 8, 128), lambda i: (0, 0, 0))]
        + [anywhere] * len(carried),
        out_shape=[
            jax.ShapeDtypeStruct((tokens, heads * width), full_type),
            jax.ShapeDtypeStruct((1, 8, 128), full_type),
        ]
        + [jax.ShapeDtypeStruct(part.shape, part.dtype) for part in carried],
        input_output_aliases=({4: 0} if extra else {})
        | {first + i: 2 + i for i in range(len(carried))},
        compiler_params=pltpu.CompilerParams(vmem_limit_bytes=vmem_most),
        cost_estimate=pl.CostEstimate(
            flops=0, bytes_accessed=tokens * picks * width * 8, transcendentals=0
        ),
        name="recall_back",
    )(gates[head : head + 1], found, queries, mixed_delta, *extra, *carried, *after)
    return out[0], out[1], list(out[2:])


def band(column_ref):
    wide = jnp.broadcast_to(column_ref[0], (tile, ring))
    return pltpu.roll(wide, 0, 1, stride=1, stride_axis=0)[:, :span]


def local_kernel(
    scale, gate_ref, far_ref, column_ref, query_ref, key_ref, value_ref, query_mask_ref,
    key_mask_ref, early_ref, late_ref, mixed_ref, bias_ref,
):
    head = pl.program_id(0)

    @pl.when(pl.program_id(1) == 0)
    def make_band():
        bias_ref[...] = band(column_ref)

    gate = gate_ref[head]
    count = query_ref.shape[0] // tile
    at = [pl.ds(t * tile, tile) for t in range(count)]
    keys = [jnp.concatenate([key_ref[a, :], key_mask_ref[0, a, :]], 1) for a in at]
    for t in range(count):
        rows = jnp.concatenate([query_ref[at[t], :], query_mask_ref[0, at[t], :]], 1)
        parts = []
        for j in range(count):
            step = j - t
            if step < -1:
                bias = far_ref[head, 0]
            elif step > 1:
                bias = far_ref[head, 1]
            else:
                bias = bias_ref[:, pl.ds((step + 1) * tile, tile)]
            parts.append(dot_inner(rows, keys[j]) * (scale * log2_e) + bias)
        top = jnp.max(functools.reduce(jnp.maximum, parts), 1, keepdims=True)
        parts = [jnp.exp2(part - top) for part in parts]
        total = jnp.sum(functools.reduce(jnp.add, parts), 1, keepdims=True)
        read = sum(dot_rows(parts[j].astype(low_type), value_ref[at[j], :]) for j in range(count))
        half = pl.ds(t * (tile // 2), tile // 2)
        recalled = jnp.concatenate([early_ref[half, :], late_ref[half, :]], 0)
        mixed_ref[at[t], :] = (gate * recalled + ((1.0 - gate) / total) * read).astype(low_type)


def local_read(projected, query_mask, key_mask, early, late, columns, far, gates, seq_len, scale):
    tokens, width = projected.shape
    heads = gates.shape[0]
    width = width // (3 * heads)
    sequences = tokens // seq_len
    half_spec = pl.BlockSpec((seq_len // 2, width), lambda h, s: (h * sequences + s, 0))

    def rows_of(shift):
        return pl.BlockSpec((seq_len, width), lambda h, s: (s, h + shift * heads))

    mask_spec = pl.BlockSpec((1, seq_len, 128), lambda h, s: (s, 0, 0))
    smem = pl.BlockSpec(memory_space=pltpu.SMEM)
    return pl.pallas_call(
        functools.partial(local_kernel, scale),
        grid=(heads, tokens // seq_len),
        in_specs=[
            smem,
            smem,
            pl.BlockSpec((1, 1, ring), lambda h, s: (h, 0, 0)),
            rows_of(0),
            rows_of(1),
            rows_of(2),
            mask_spec,
            mask_spec,
            half_spec,
            half_spec,
        ],
        out_specs=rows_of(0),
        out_shape=jax.ShapeDtypeStruct((tokens, heads * width), low_type),
        scratch_shapes=[pltpu.VMEM((tile, span), full_type)],
        compiler_params=pltpu.CompilerParams(vmem_limit_bytes=vmem_most),
        cost_estimate=pl.CostEstimate(
            flops=0, bytes_accessed=heads * tokens * seq_len * 20, transcendentals=0
        ),
        name="local_read",
    )(gates, far, columns, projected, projected, projected, query_mask, key_mask, early, late)


def local_back_kernel(
    scale, gate_ref, far_ref, column_ref, query_ref, key_ref, value_ref, query_mask_ref,
    key_mask_ref, delta_ref, recall_delta_ref, query_delta_ref, key_delta_ref, value_delta_ref,
    diagonal_ref, sums_ref, bias_ref, near_ref, key_sum_ref, value_sum_ref,
):
    head = pl.program_id(0)
    last = pl.program_id(1) == pl.num_programs(1) - 1

    @pl.when(pl.program_id(1) == 0)
    def make_band():
        bias_ref[...] = band(column_ref)
        near_ref[...] = jnp.zeros(near_ref.shape, full_type)
        sums_ref[...] = jnp.zeros(sums_ref.shape, full_type)

    gate = gate_ref[head]
    count = query_ref.shape[0] // tile
    at = [pl.ds(t * tile, tile) for t in range(count)]
    keys = [jnp.concatenate([key_ref[a, :], key_mask_ref[0, a, :]], 1) for a in at]
    turned = [key_ref[a, :].astype(full_type).T.astype(low_type) for a in at]
    gained = jnp.zeros((1, tile), full_type)
    far_sums = [jnp.zeros((8, tile), full_type) for side in range(2)]
    for t in range(count):
        rows = jnp.concatenate([query_ref[at[t], :], query_mask_ref[0, at[t], :]], 1)
        delta = ((1.0 - gate) * delta_ref[at[t], :].astype(full_type)).astype(low_type)
        parts = []
        for j in range(count):
            step = j - t
            if step < -1:
                bias = far_ref[head, 0]
            elif step > 1:
                bias = far_ref[head, 1]
            else:
                bias = bias_ref[:, pl.ds((1 - step) * tile, tile)]
            parts.append(dot_inner(keys[j], rows) * (scale * log2_e) + bias)
        top = jnp.max(functools.reduce(jnp.maximum, parts), 0, keepdims=True)
        parts = [jnp.exp2(part - top) for part in parts]
        total = jnp.sum(functools.reduce(jnp.add, parts), 0, keepdims=True)
        inverse = 1.0 / total
        parts = [part * inverse for part in parts]
        moves = [dot_inner(value_ref[at[j], :], delta) for j in range(count)]
        expected = jnp.sum(
            functools.reduce(jnp.add, [parts[j] * moves[j] for j in range(count)]),
            0,
            keepdims=True,
        )
        gained = gained + expected
        query_sum = None
        for j in range(count):
            step = j - t
            score_delta = parts[j] * (moves[j] - expected)
            if abs(step) > 1:
                side = 0 if step < 0 else 1
                far_sums[side] = far_sums[side] + jnp.sum(
                    score_delta.reshape(tile // 8, 8, tile), 0
                )
            else:
                near_ref[:, pl.ds((1 - step) * tile, tile)] += score_delta
            low_delta = score_delta.astype(low_type)
            value_part = dot_rows(parts[j].astype(low_type), delta)
            key_part = dot_rows(low_delta, query_ref[at[t], :])
            query_part = dot_rows(turned[j], low_delta)
            if t == 0:
                value_sum_ref[at[j], :] = value_part
                key_sum_ref[at[j], :] = key_part
            else:
                value_sum_ref[at[j], :] += value_part
                key_sum_ref[at[j], :] += key_part
            query_sum = query_part if j == 0 else query_sum + query_part
        query_delta_ref[at[t], :] = (
            query_sum.T * scale + recall_delta_ref[at[t], :]
        ).astype(low_type)
    key_delta_ref[...] = (key_sum_ref[...] * scale).astype(low_type)
    value_delta_ref[...] = value_sum_ref[...].astype(low_type)
    sums_ref[0, 0:1] += gained
    sums_ref[0, 8:16] += far_sums[0]
    sums_ref[0, 16:24] += far_sums[1]

    @pl.when(last)
    def fold_diagonals():
        total = jnp.zeros((8, ring), full_type)
        for g in range(tile // 8):
            part = jnp.concatenate(
                [near_ref[pl.ds(g * 8, 8), :], jnp.zeros((8, ring - span), full_type)], 1
            )
            total = total + (pltpu.roll(part, ring - 8 * g, 1) if g else part)
        row = lax.broadcasted_iota(jnp.int32, (8, ring), 0)
        for bit in (1, 2, 4):
            total = jnp.where((row & bit) != 0, pltpu.roll(total, ring - bit, 1), total)
        diagonal_ref[0] = total


def local_back(
    projected, query_mask, key_mask, mixed_delta, recall_delta, columns, far, gates, seq_len, scale,
    heads_now, carried, kept, after,
):
    tokens = mixed_delta.shape[0]
    heads = gates.shape[0]
    width = mixed_delta.shape[1] // heads
    start, count = heads_now
    anywhere = pl.BlockSpec(memory_space=pl.ANY)
    chosen = slice(start, start + count)

    def rows_of(shift):
        return pl.BlockSpec((seq_len, width), lambda h, s: (s, h + start + shift * heads))

    def kernel(*refs):
        inputs, rest = refs[:10], refs[10 + len(kept) + len(carried) + len(after) :]
        local_back_kernel(scale, *inputs, *rest[:5], *rest[5 + len(carried) :])

    mask_spec = pl.BlockSpec((1, seq_len, 128), lambda h, s: (s, 0, 0))
    smem = pl.BlockSpec(memory_space=pltpu.SMEM)
    rows_shape = jax.ShapeDtypeStruct((tokens, heads * width), low_type)
    first = 10 + len(kept)
    out = pl.pallas_call(
        kernel,
        grid=(count, tokens // seq_len),
        in_specs=[
            smem,
            smem,
            pl.BlockSpec((1, 1, ring), lambda h, s: (h, 0, 0)),
            rows_of(0),
            rows_of(1),
            rows_of(2),
            mask_spec,
            mask_spec,
            rows_of(0),
            rows_of(0),
        ]
        + [anywhere] * (len(kept) + len(carried) + len(after)),
        out_specs=[
            rows_of(0),
            rows_of(0),
            rows_of(0),
            pl.BlockSpec((1, 8, ring), lambda h, s: (h, 0, 0)),
            pl.BlockSpec((1, 24, tile), lambda h, s: (h, 0, 0)),
        ]
        + [anywhere] * len(carried),
        out_shape=[
            rows_shape,
            rows_shape,
            rows_shape,
            jax.ShapeDtypeStruct((count, 8, ring), full_type),
            jax.ShapeDtypeStruct((count, 24, tile), full_type),
        ]
        + [jax.ShapeDtypeStruct(part.shape, part.dtype) for part in carried],
        input_output_aliases={10 + i: i for i in range(len(kept))}
        | {first + i: 5 + i for i in range(len(carried))},
        scratch_shapes=[
            pltpu.VMEM((tile, span), full_type),
            pltpu.VMEM((tile, span), full_type),
            pltpu.VMEM((seq_len, width), full_type),
            pltpu.VMEM((seq_len, width), full_type),
        ],
        compiler_params=pltpu.CompilerParams(vmem_limit_bytes=vmem_most),
        cost_estimate=pl.CostEstimate(
            flops=0, bytes_accessed=count * tokens * seq_len * 40, transcendentals=0
        ),
        name="local_back",
    )(
        gates[chosen], far[chosen], columns[chosen], projected, projected, projected, query_mask,
        key_mask, mixed_delta, recall_delta, *kept, *carried, *after,
    )
    return list(out[:3]), out[3], out[4], list(out[5:])


def mask_rows(block_ids):
    level = jnp.arange(128, dtype=jnp.int32)
    gap = block_ids[:, :, None] - level
    query_mask = jnp.where((gap >= 0) & (gap <= 1), 0.0, mask_gap).astype(low_type)
    key_mask = (gap == 0).astype(low_type)
    return query_mask, key_mask


def fetch(rows):
    group = lax.axis_size("tensor")
    return [rows] + [
        lax.ppermute(rows, "tensor", [((i + k) % group, i) for i in range(group)])
        for k in range(1, group)
    ]


def in_order(shares):
    group = lax.axis_size("tensor")
    rows = shares[0].shape[0]
    whole = jnp.zeros((group * rows,) + shares[0].shape[1:], shares[0].dtype)
    for k in range(group):
        start = ((lax.axis_index("tensor") + k) % group) * rows
        whole = lax.dynamic_update_slice_in_dim(whole, shares[k], start, 0)
    return whole


def share_of(whole, k, rows):
    start = ((lax.axis_index("tensor") + k) % lax.axis_size("tensor")) * rows
    return lax.dynamic_slice_in_dim(whole, start, rows, 0)


def fold(term, piece):
    group = lax.axis_size("tensor")
    sent = [
        lax.ppermute(
            term(piece(k)).astype(low_type), "tensor", [(i, (i + k) % group) for i in range(group)]
        )
        for k in range(1, group)
    ]
    return sum((part.astype(full_type) for part in sent), term(piece(0)))


def bit_orders():
    bits = lax.axis_size("dp").bit_length() - 1
    near = [(0, 1, 2), (1, 2, 0), (2, 0, 1)]
    return [list(head) + list(range(3, bits)) for head in near]


def swap_over(rows, bit):
    return lax.ppermute(rows, "dp", [(i, i ^ (1 << bit)) for i in range(lax.axis_size("dp"))])


def side_of(bit):
    return (lax.axis_index("dp") >> bit) & 1


def halve_step(parts, orders, step):
    kept, sent = [], []
    for part, order in zip(parts, orders):
        half = part.shape[0] // 2
        side = side_of(order[step])
        sent.append(
            swap_over(
                lax.dynamic_slice_in_dim(part, (1 - side) * half, half, 0), order[step]
            )
        )
        kept.append(lax.dynamic_slice_in_dim(part, side * half, half, 0))
    return kept, sent


def add_low(kept, sent):
    return [
        (a.astype(full_type) + b.astype(full_type)).astype(low_type) for a, b in zip(kept, sent)
    ]


def double_all(parts, beside):
    orders = bit_orders()
    for step in reversed(range(len(orders[0]))):
        got = [swap_over(part, order[step]) for part, order in zip(parts, orders)]
        if step == 1:
            got[2], beside = lax.optimization_barrier((got[2], beside))
        wider = []
        for part, other, order in zip(parts, got, orders):
            rows = part.shape[0]
            side = side_of(order[step])
            whole = jnp.zeros((2 * rows,) + part.shape[1:], part.dtype)
            whole = lax.dynamic_update_slice_in_dim(whole, part, side * rows, 0)
            wider.append(lax.dynamic_update_slice_in_dim(whole, other, (1 - side) * rows, 0))
        parts = wider
    return parts, beside


def pack(parts):
    width = min(part.shape[1] for part in parts)
    return jnp.concatenate(
        [
            part[:, start : start + width]
            for part in parts
            for start in range(0, part.shape[1], width)
        ],
        0,
    )


def gather_all(packed, parts, orders):
    whole = lax.all_gather(packed, "dp", axis=0)
    width = packed.shape[1]
    wide = []
    start = 0
    for part, order in zip(parts, orders):
        bits = len(order)
        rows = part.shape[0]
        columns = []
        for unused in range(part.shape[1] // width):
            piece = whole[:, start : start + rows].reshape((2,) * bits + (rows, width))
            piece = piece.transpose([bits - 1 - bit for bit in order] + [bits, bits + 1])
            columns.append(piece.reshape(-1, width))
            start += rows
        wide.append(jnp.concatenate(columns, 1).astype(full_type))
    return wide


def body(
    tokens,
    block_ids,
    memory_index,
    memory_keys,
    memory_values,
    attn_gain,
    query_weight,
    key_weight,
    value_weight,
    output_weight,
    position_table,
    memory_gate,
    mlp_gain,
    hidden_weight,
    return_weight,
    grad_output,
):
    share_rows = tokens.shape[0]
    seq_len = block_ids.shape[1]
    head_count, memory_rows, head_width = memory_keys.shape
    picks = memory_index.shape[2]
    inner_width = head_count * head_width
    scale = head_width ** (-0.5)

    offsets = jnp.arange(head_count, dtype=jnp.int32) * memory_rows
    index_rows = memory_index.transpose(1, 0, 2) + offsets[:, None, None]
    table = interleave(memory_keys, memory_values)

    token_full = tokens.astype(full_type)
    normed_rows = rms_scaled(token_full, attn_gain).astype(low_type)
    normed = lax.all_gather(normed_rows, "tensor", axis=0, tiled=True)
    joined = jnp.concatenate([query_weight, key_weight, value_weight], 1)
    projected = dot_rows(normed, joined).astype(low_type)
    found, late, early = gather_found(index_rows, table, projected, picks, scale)
    found = found.reshape(-1, head_width)

    query_mask, key_mask = mask_rows(block_ids)
    place = jnp.arange(ring, dtype=jnp.int32)
    place = jnp.where(place < span, place, place - ring)
    ahead = bucket_of(place - tile)
    behind = bucket_of(tile - place)
    level = jnp.arange(32, dtype=jnp.int32)
    ahead_hot = (ahead[:, None] == level).astype(full_type)
    behind_hot = (behind[:, None] == level).astype(full_type)
    scaled_table = position_table * log2_e
    ahead_columns = jnp.dot(ahead_hot, scaled_table, precision=exact_mode).T[:, None, :]
    behind_columns = jnp.dot(behind_hot, scaled_table, precision=exact_mode).T[:, None, :]
    far = jnp.stack([scaled_table[15], scaled_table[31]], 1)
    gates = jax.nn.sigmoid(memory_gate)

    mixed_rows = local_read(
        projected, query_mask, key_mask, early, late, ahead_columns, far, gates, seq_len, scale
    )
    middle = token_full + fold(
        lambda rows: dot_rows(rows, output_weight), lambda k: share_of(mixed_rows, k, share_rows)
    )
    second_rows = rms_scaled(middle, mlp_gain).astype(low_type)
    grad_full = jnp.concatenate(fetch(grad_output), 0)
    second = jnp.concatenate(fetch(second_rows), 0)
    active, slope = gelu_pair(dot_rows(second, hidden_weight))
    slope = lax.optimization_barrier(slope)
    orders = bit_orders()
    steps = len(orders[0])

    return_low = dot_outer(active, grad_full).astype(low_type)
    return_half = return_low.shape[0] // 2
    kept_back, sent_back = halve_step(
        [return_low[:return_half], return_low[return_half:]], orders[1:], 0
    )
    active_delta = dot_inner(grad_full, return_weight)
    hidden_delta = (active_delta * slope.astype(full_type)).astype(low_type)
    second_delta = fold(
        lambda rows: dot_inner(rows, hidden_weight),
        lambda k: lax.slice_in_dim(hidden_delta, k * share_rows, (k + 1) * share_rows),
    )
    hidden_half = hidden_delta.shape[1] // 2
    hidden_parts = [
        dot_outer(second, hidden_delta[:, :hidden_half]).astype(low_type),
        dot_outer(second, hidden_delta[:, hidden_half:]).astype(low_type),
    ]
    kept, sent = halve_step(hidden_parts, orders[:2], 0)

    kept_back, kept = lax.optimization_barrier((kept_back, kept))
    kept_back, sent_back = halve_step(add_low(kept_back, sent_back), orders[1:], 1)

    second_back = jax.vjp(rms_scaled, middle, mlp_gain)[1]
    middle_part, mlp_gain_part = second_back(second_delta)
    middle_delta = grad_output.astype(full_type) + middle_part
    middle_low = middle_delta.astype(low_type)
    kept, kept_back, middle_low = lax.optimization_barrier((kept, kept_back, middle_low))
    kept, sent = halve_step(add_low(kept, sent), orders[:2], 1)
    kept_back, sent_back = halve_step(add_low(kept_back, sent_back), orders[1:], 2)
    middle_full = in_order(fetch(middle_low))
    mixed_delta = dot_inner(middle_full, output_weight).astype(low_type)
    kept, kept_back, mixed_delta = lax.optimization_barrier((kept, kept_back, mixed_delta))
    kept, sent = halve_step(add_low(kept, sent), orders[:2], 2)
    kept_back, sent_back = halve_step(add_low(kept_back, sent_back), orders[1:], 3)
    taken = 2
    for step in range(4, steps):
        kept_back, sent_back = halve_step(add_low(kept_back, sent_back), orders[1:], step)
    layer_output = (
        middle
        + fold(
            lambda rows: dot_rows(rows, return_weight),
            lambda k: lax.slice_in_dim(active, k * share_rows, (k + 1) * share_rows),
        )
    ).astype(low_type)

    shards, packed = [], []
    recall_delta = None
    recall_sums = []
    for head in range(head_count):
        recall_delta, head_sums, kept = recall_back(
            found, projected, mixed_delta, gates, head, kept, packed, recall_delta, head_count,
            picks, scale,
        )
        recall_sums.append(head_sums)
        if taken < steps - 1:
            taken += 1
            kept, sent = halve_step(add_low(kept, sent), orders[:2], taken)
        elif not shards:
            shards = add_low(kept, sent) + add_low(kept_back, sent_back)
            packed = [pack(shards)]
            kept = []
    while taken < steps - 1:
        taken += 1
        kept, sent = halve_step(add_low(kept, sent), orders[:2], taken)
    if not shards:
        shards = add_low(kept, sent) + add_low(kept_back, sent_back)
        packed = [pack(shards)]
    hidden_low_sum, hidden_high_sum, return_low_sum, return_high_sum = gather_all(
        packed[0], shards, orders[:2] + orders[1:]
    )
    hidden_sum = jnp.concatenate([hidden_low_sum, hidden_high_sum], 1)
    return_sum = jnp.concatenate([return_low_sum, return_high_sum], 0)
    recall_sums = jnp.concatenate(recall_sums, 0)
    half_heads = max(1, head_count // 2)
    deltas = []
    diagonals = []
    local_sums = []
    for start in range(0, head_count, half_heads):
        deltas, diagonal_now, sums_now, unused = local_back(
            projected, query_mask, key_mask, mixed_delta, recall_delta, behind_columns, far, gates,
            seq_len, scale, (start, half_heads), [], deltas, packed,
        )
        diagonals.append(diagonal_now)
        local_sums.append(sums_now)
    query_delta, key_delta, value_delta = deltas
    diagonals = jnp.concatenate(diagonals, 0)
    local_sums = jnp.concatenate(local_sums, 0)
    recall_gain = jnp.sum(recall_sums[:, :, 0], 1)
    local_gain = jnp.sum(local_sums[:, 0], 1)
    gate_part = gates * (1.0 - gates) * recall_gain - gates * local_gain
    diagonal_sums = jnp.sum(diagonals, 1)
    table_part = jnp.dot(diagonal_sums, behind_hot, precision=exact_mode)
    far_left = jnp.sum(local_sums[:, 8:16], (1, 2))
    far_right = jnp.sum(local_sums[:, 16:24], (1, 2))
    table_part = table_part + far_left[:, None] * (level == 15) + far_right[:, None] * (level == 31)

    project_delta = jnp.concatenate([query_delta, key_delta, value_delta], 1)
    joined_part = dot_outer(normed, project_delta)
    attn_gain_part = jnp.sum(joined_part * joined.astype(full_type), 1) / attn_gain
    model_width = tokens.shape[1]
    small = jnp.concatenate([table_part.reshape(-1), gate_part])
    small = jnp.pad(small, (0, model_width - small.shape[0]))
    extra = jnp.stack([attn_gain_part, mlp_gain_part, small], 1)
    extra = jnp.pad(extra, ((0, 0), (0, 125)))
    joined_low = jnp.concatenate([joined_part, extra], 1).astype(low_type)
    joined_half = joined_low.shape[0] // 2
    last = [
        joined_low[:joined_half],
        joined_low[joined_half:],
        dot_outer(mixed_rows, middle_full).astype(low_type),
    ]
    for step in range(steps):
        last = add_low(*halve_step(last, orders, step))
    last, (hidden_sum, return_sum) = double_all(last, (hidden_sum, return_sum))
    *joined_sum, output_sum = last

    normed_delta = fold(
        lambda rows: dot_inner(rows, joined), lambda k: share_of(project_delta, k, share_rows)
    )
    first_back = jax.vjp(rms_scaled, token_full, attn_gain)[1]
    tokens_grad = (middle_delta + first_back(normed_delta)[0]).astype(low_type)

    def joined_columns(start, stop):
        return jnp.concatenate([part[:, start:stop].astype(full_type) for part in joined_sum], 0)

    last_columns = joined_columns(3 * inner_width, 3 * inner_width + 128)
    gains = sum(fetch(last_columns[:, :2].T))
    small_sum = last_columns[:, 2]
    table_size = head_count * 32
    return (
        layer_output,
        tokens_grad,
        gains[0],
        joined_columns(0, inner_width),
        joined_columns(inner_width, 2 * inner_width),
        joined_columns(2 * inner_width, 3 * inner_width),
        output_sum.astype(full_type),
        small_sum[:table_size].reshape(head_count, 32).T,
        small_sum[table_size : table_size + head_count],
        gains[1],
        hidden_sum,
        return_sum,
    )


def solution(mesh):
    def run(*arrays):
        with jax.sharding.use_abstract_mesh(mesh.abstract_mesh):
            return jax.shard_map(
                body,
                mesh=mesh,
                in_specs=(
                    P(("dp", "tensor"), None),
                    P("dp", None),
                    P("dp", "tensor", None),
                    P("tensor", None, None),
                    P("tensor", None, None),
                    P(),
                    P(None, "tensor"),
                    P(None, "tensor"),
                    P(None, "tensor"),
                    P("tensor", None),
                    P(None, "tensor"),
                    P("tensor"),
                    P(),
                    P(None, "tensor"),
                    P("tensor", None),
                    P(("dp", "tensor"), None),
                ),
                out_specs=(
                    P(("dp", "tensor"), None),
                    P(("dp", "tensor"), None),
                    P(),
                    P(None, "tensor"),
                    P(None, "tensor"),
                    P(None, "tensor"),
                    P("tensor", None),
                    P(None, "tensor"),
                    P("tensor"),
                    P(),
                    P(None, "tensor"),
                    P("tensor", None),
                ),
                check_vma=False,
            )(*arrays)

    return run
```

```python
import functools
import math

import jax
import jax.numpy as jnp
from jax import lax
from jax.experimental import pallas as pl
from jax.experimental.pallas import tpu as pltpu
from jax.sharding import PartitionSpec as P

eps_norm = 1e-06
far_steps = (12, 16, 23, 32, 46, 64, 91)
exact_mode = lax.Precision.HIGHEST
low_type = jnp.bfloat16
full_type = jnp.float32
log2_e = math.log2(math.e)
tile = 256
span = 3 * tile
ring = 1024
mask_gap = -(2.0**100)
vmem_most = 60 * 2**20


def bucket_of(relative):
    upper_half = jnp.where(relative > 0, 16, 0).astype(jnp.int32)
    distance = jnp.abs(relative)
    far_bucket = 8 + sum(((distance >= step_size).astype(jnp.int32) for step_size in far_steps))
    return upper_half + jnp.where(distance < 8, distance, far_bucket)


def rms_scaled(rows, gain):
    return rows * lax.rsqrt(jnp.mean(rows * rows, -1, keepdims=True) + eps_norm) * gain


def gelu_pair(rows):
    reach = math.sqrt(2.0 / math.pi)
    square = rows * rows
    turn = jnp.tanh(reach * rows * (1.0 + 0.044715 * square))
    share = 0.5 * (1.0 + turn)
    steep = 0.5 * (1.0 - turn * turn) * reach * (1.0 + 3.0 * 0.044715 * square)
    return (rows * share).astype(low_type), (share + rows * steep).astype(low_type)


def dot_rows(left, right):
    return jnp.dot(left, right, preferred_element_type=full_type)


def dot_outer(left, right):
    return lax.dot_general(
        left, right, (((0,), (0,)), ((), ())), preferred_element_type=full_type
    )


def dot_inner(left, right):
    return lax.dot_general(
        left, right, (((1,), (1,)), ((), ())), preferred_element_type=full_type
    )


def interleave_kernel(key_ref, value_ref, table_ref):
    rows = key_ref.shape[1]
    row = lax.broadcasted_iota(jnp.int32, (256, 256), 0)
    column = lax.broadcasted_iota(jnp.int32, (256, 256), 1)
    order = jnp.where(column == (row // 2 + (row % 2) * 128), 1.0, 0.0).astype(low_type)
    for part in range(rows // 256):
        low, high = pl.ds(part * 256, 128), pl.ds(part * 256 + 128, 128)
        both = jnp.concatenate(
            [
                jnp.concatenate([key_ref[0, low], key_ref[0, high]], 1),
                jnp.concatenate([value_ref[0, low], value_ref[0, high]], 1),
            ],
            0,
        )
        mixed = dot_rows(order, both).astype(low_type)
        table_ref[pl.ds(part * 512, 256), :] = mixed[:, :128]
        table_ref[pl.ds(part * 512 + 256, 256), :] = mixed[:, 128:]


def interleave(memory_keys, memory_values):
    heads, rows, width = memory_keys.shape
    step = min(8192, rows)
    spec = pl.BlockSpec((1, step, width), lambda h, i: (h, i, 0))
    return pl.pallas_call(
        interleave_kernel,
        grid=(heads, rows // step),
        in_specs=[spec, spec],
        out_specs=pl.BlockSpec((2 * step, width), lambda h, i: (h * (rows // step) + i, 0)),
        out_shape=jax.ShapeDtypeStruct((heads * rows * 2, width), low_type),
        compiler_params=pltpu.CompilerParams(vmem_limit_bytes=vmem_most),
        cost_estimate=pl.CostEstimate(
            flops=heads * rows * 4 * 256 * width,
            bytes_accessed=heads * rows * width * 8,
            transcendentals=0,
        ),
        name="interleave",
    )(memory_keys, memory_values).reshape(heads, rows, 2, width)


def own_columns(picks):
    shape = (8, 8 * picks * 2)
    lane = lax.broadcasted_iota(jnp.int32, shape, 1)
    row = lax.broadcasted_iota(jnp.int32, shape, 0)
    return jnp.logical_and(lane // (2 * picks) == row, lane % 2 == 0)


def copy_rows(picked, first, table_ref, found_ref, start, count):
    for at in range(0, count, 8):
        rows_now = [
            table_ref[picked[(first + at + j) // 128, (first + at + j) % 128]] for j in range(8)
        ]
        for j in range(8):
            found_ref[start + at + j] = rows_now[j]
        yield


def recall_rows(picks, scale, own, query_ref, query_at, rows_ref, read_ref, read_at, tokens):
    wide = 8 * picks * 2
    groups = range(tokens // 8)
    scores = []
    for g in groups:
        rows = rows_ref[pl.ds(g * wide, wide), :]
        scores.append(dot_inner(query_ref[pl.ds(query_at + g * 8, 8), :], rows))
        yield
    shifted = []
    totals = []
    for g in groups:
        masked = jnp.where(own, scores[g] * (scale * log2_e), -jnp.inf)
        exponent = jnp.exp2(masked - jnp.max(masked, 1, keepdims=True))
        totals.append(jnp.sum(exponent, 1, keepdims=True))
        shifted.append(pltpu.roll(exponent, 1, 1).astype(low_type))
        yield
    for g in groups:
        rows = rows_ref[pl.ds(g * wide, wide), :]
        read_ref[pl.ds(read_at + g * 8, 8), :] = dot_rows(shifted[g], rows) / totals[g]
        yield


def weave(many, many_count, few, few_count):
    done = 0
    for number in range(few_count):
        until = (number + 1) * many_count // few_count
        while done < until:
            next(many)
            done += 1
        next(few)


def gather_kernel(
    picks, scale, index_hbm, table_hbm, now_ref, before_ref, found_ref, late_ref, early_ref,
    table_ref, table_sems, index_a, index_b, index_sems, stage_ref, stage_sems,
):
    step = pl.program_id(0)
    steps = pl.num_programs(0) - 1
    heads = table_sems.shape[0]
    blocks = steps // heads
    chunk = found_ref.shape[0] // 2
    rows = table_ref.shape[0] // heads
    slots = (index_a, index_b)
    part = chunk // 2
    tokens = part // picks
    own = own_columns(picks)
    flat = found_ref.reshape(4 * chunk, 128)

    def index_copy(number, slot):
        return pltpu.make_async_copy(index_hbm.at[number], slots[slot], index_sems.at[slot])

    def table_copy(number):
        where = pl.ds(number * rows, rows)
        return pltpu.make_async_copy(
            table_hbm.at[where], table_ref.at[where], table_sems.at[number]
        )

    def stage_copy(number):
        return pltpu.make_async_copy(
            flat.at[pl.ds(number * 2 * part, 2 * part)], stage_ref.at[number], stage_sems.at[number]
        )

    def reads(number, query_ref, read_ref):
        return recall_rows(
            picks, scale, own, query_ref, (number % 2) * tokens, stage_ref.at[number], read_ref,
            (number % 2) * tokens, tokens,
        )

    @pl.when(step == 0)
    def start_all():
        index_copy(0, 0).start()
        index_copy(1, 1).start()
        for number in range(heads):
            table_copy(number).start()
        stage_copy(2).start()
        stage_copy(3).start()

    @pl.when(jnp.logical_and(step < steps, step % blocks == 0))
    def wait_table():
        table_copy(step // blocks).wait()

    @pl.when(step < steps)
    def work():
        following = jnp.minimum(step + 1, steps - 1)
        for number in range(4):
            slot = number // 2
            if number % 2 == 0:
                index_copy(2 * step + slot, slot).wait()
            finished = (number + 2) % 4
            stage_copy(finished).wait()
            copied = copy_rows(
                slots[slot], (number % 2) * part, table_ref, found_ref, number * part, part
            )
            if number < 2:
                read = reads(finished, before_ref, late_ref)
            else:
                read = reads(finished, now_ref, early_ref)
            weave(copied, part // 8, read, 3 * (tokens // 8))
            stage_copy(number).start()
            if number % 2 == 1:
                index_copy(2 * following + slot, slot).start()

    @pl.when(step == steps)
    def finish():
        for number in (2, 3):
            stage_copy(number).wait()
            for unused in reads(number, before_ref, late_ref):
                pass
        for slot in range(2):
            index_copy(2 * (steps - 1) + slot, slot).wait()


def gather_found(index_rows, table, queries, picks, scale):
    heads, rows, unused, width = table.shape
    tokens = queries.shape[0]
    half = 128
    blocks = tokens // (2 * half)
    steps = heads * blocks
    chunk = half * picks

    def query_spec(shift):
        def place(t):
            at = jnp.clip(t - shift, 0, steps - 1)
            return (2 * (at % blocks) + shift, at // blocks)

        return pl.BlockSpec((half, width), place)

    return pl.pallas_call(
        functools.partial(gather_kernel, picks, scale),
        grid=(steps + 1,),
        in_specs=[
            pl.BlockSpec(memory_space=pl.ANY),
            pl.BlockSpec(memory_space=pl.ANY),
            query_spec(0),
            query_spec(1),
        ],
        out_specs=[
            pl.BlockSpec((2 * chunk, 2, width), lambda t: (jnp.minimum(t, steps - 1), 0, 0)),
            pl.BlockSpec((half, width), lambda t: (jnp.maximum(t - 1, 0), 0)),
            pl.BlockSpec((half, width), lambda t: (jnp.minimum(t, steps - 1), 0)),
        ],
        out_shape=[
            jax.ShapeDtypeStruct((heads * tokens * picks, 2, width), low_type),
            jax.ShapeDtypeStruct((heads * tokens // 2, width), full_type),
            jax.ShapeDtypeStruct((heads * tokens // 2, width), full_type),
        ],
        scratch_shapes=[
            pltpu.VMEM((heads * rows, 2, width), low_type),
            pltpu.SemaphoreType.DMA((heads,)),
            pltpu.SMEM((chunk // 128, 128), jnp.int32),
            pltpu.SMEM((chunk // 128, 128), jnp.int32),
            pltpu.SemaphoreType.DMA((2,)),
            pltpu.VMEM((4, chunk, width), low_type),
            pltpu.SemaphoreType.DMA((4,)),
        ],
        compiler_params=pltpu.CompilerParams(vmem_limit_bytes=vmem_most),
        cost_estimate=pl.CostEstimate(
            flops=0, bytes_accessed=4 * heads * tokens * picks * width * 4, transcendentals=0
        ),
        name="gather_found",
    )(
        index_rows.reshape(-1, chunk // 128, 128), table.reshape(heads * rows, 2, width), queries,
        queries,
    )


def band(column_ref):
    wide = jnp.broadcast_to(column_ref[0], (tile, ring))
    return pltpu.roll(wide, 0, 1, stride=1, stride_axis=0)[:, :span]


def local_kernel(
    scale, gate_ref, far_ref, column_ref, query_ref, key_ref, value_ref, query_mask_ref,
    key_mask_ref, early_ref, late_ref, mixed_ref, bias_ref,
):
    head = pl.program_id(0)

    @pl.when(pl.program_id(1) == 0)
    def make_band():
        bias_ref[...] = band(column_ref)

    gate = gate_ref[head]
    count = query_ref.shape[0] // tile
    at = [pl.ds(t * tile, tile) for t in range(count)]
    keys = [jnp.concatenate([key_ref[a, :], key_mask_ref[0, a, :]], 1) for a in at]
    for t in range(count):
        rows = jnp.concatenate([query_ref[at[t], :], query_mask_ref[0, at[t], :]], 1)
        parts = []
        for j in range(count):
            step = j - t
            if step < -1:
                bias = far_ref[head, 0]
            elif step > 1:
                bias = far_ref[head, 1]
            else:
                bias = bias_ref[:, pl.ds((step + 1) * tile, tile)]
            parts.append(dot_inner(rows, keys[j]) * (scale * log2_e) + bias)
        top = jnp.max(functools.reduce(jnp.maximum, parts), 1, keepdims=True)
        parts = [jnp.exp2(part - top) for part in parts]
        total = jnp.sum(functools.reduce(jnp.add, parts), 1, keepdims=True)
        read = sum(dot_rows(parts[j].astype(low_type), value_ref[at[j], :]) for j in range(count))
        half = pl.ds(t * (tile // 2), tile // 2)
        recalled = jnp.concatenate([early_ref[half, :], late_ref[half, :]], 0)
        mixed_ref[at[t], :] = (gate * recalled + ((1.0 - gate) / total) * read).astype(low_type)


def local_read(projected, query_mask, key_mask, early, late, columns, far, gates, seq_len, scale):
    tokens, width = projected.shape
    heads = gates.shape[0]
    width = width // (3 * heads)
    sequences = tokens // seq_len
    half_spec = pl.BlockSpec((seq_len // 2, width), lambda h, s: (h * sequences + s, 0))

    def rows_of(shift):
        return pl.BlockSpec((seq_len, width), lambda h, s: (s, h + shift * heads))

    mask_spec = pl.BlockSpec((1, seq_len, 128), lambda h, s: (s, 0, 0))
    smem = pl.BlockSpec(memory_space=pltpu.SMEM)
    return pl.pallas_call(
        functools.partial(local_kernel, scale),
        grid=(heads, tokens // seq_len),
        in_specs=[
            smem,
            smem,
            pl.BlockSpec((1, 1, ring), lambda h, s: (h, 0, 0)),
            rows_of(0),
            rows_of(1),
            rows_of(2),
            mask_spec,
            mask_spec,
            half_spec,
            half_spec,
        ],
        out_specs=rows_of(0),
        out_shape=jax.ShapeDtypeStruct((tokens, heads * width), low_type),
        scratch_shapes=[pltpu.VMEM((tile, span), full_type)],
        compiler_params=pltpu.CompilerParams(vmem_limit_bytes=vmem_most),
        cost_estimate=pl.CostEstimate(
            flops=0, bytes_accessed=heads * tokens * seq_len * 20, transcendentals=0
        ),
        name="local_read",
    )(gates, far, columns, projected, projected, projected, query_mask, key_mask, early, late)


def recall_back_rows(
    picks, scale, own, gate, query_ref, delta_ref, at, rows_ref, read_ref, gains, tokens
):
    wide = 8 * picks * 2
    flight = 8
    groups = tokens // 8
    both = {}
    for first in range(-flight, groups, flight):
        for g in range(first + flight, min(first + 2 * flight, groups)):
            where = pl.ds(at + g * 8, 8)
            pair = jnp.concatenate([query_ref[where, :], delta_ref[where, :]], 0)
            both[g] = dot_inner(pair, rows_ref[pl.ds(g * wide, wide), :])
            yield
        for g in range(max(first, 0), first + flight if first >= 0 else 0):
            pair = both.pop(g)
            masked = jnp.where(own, pair[:8] * (scale * log2_e), -jnp.inf)
            exponent = jnp.exp2(masked - jnp.max(masked, 1, keepdims=True))
            weights = exponent / jnp.sum(exponent, 1, keepdims=True)
            reads = pltpu.roll(pair[8:], wide - 1, 1)
            expected = jnp.sum(weights * reads, 1, keepdims=True)
            gains.append(expected)
            score_delta = (weights * (reads - expected)).astype(low_type)
            rows = rows_ref[pl.ds(g * wide, wide), :]
            read_ref[pl.ds(g * 8, 8), :] = dot_rows(score_delta, rows) * (scale * gate)
            yield


def local_back_tile(
    t, scale, gate, far_ref, query_ref, keys, turned, value_ref, query_mask_ref, delta_ref,
    bias_ref, near_ref, key_sum_ref, value_sum_ref, gains, far_sums, result,
):
    count = len(keys)
    at = [pl.ds(j * tile, tile) for j in range(count)]
    rows = jnp.concatenate([query_ref[at[t], :], query_mask_ref[0, at[t], :]], 1)
    delta = ((1.0 - gate) * delta_ref[at[t], :].astype(full_type)).astype(low_type)
    parts = []
    for j in range(count):
        step = j - t
        if step < -1:
            bias = far_ref[0, 0]
        elif step > 1:
            bias = far_ref[0, 1]
        else:
            bias = bias_ref[:, pl.ds((1 - step) * tile, tile)]
        parts.append(dot_inner(keys[j], rows) * (scale * log2_e) + bias)
        yield
    top = jnp.max(functools.reduce(jnp.maximum, parts), 0, keepdims=True)
    yield
    for j in range(count):
        parts[j] = jnp.exp2(parts[j] - top)
        yield
    inverse = 1.0 / jnp.sum(functools.reduce(jnp.add, parts), 0, keepdims=True)
    moves = []
    products = []
    for j in range(count):
        parts[j] = parts[j] * inverse
        moves.append(dot_inner(value_ref[at[j], :], delta))
        products.append(parts[j] * moves[j])
        yield
    expected = jnp.sum(functools.reduce(jnp.add, products), 0, keepdims=True)
    gains.append(expected)
    query_sum = None
    for j in range(count):
        step = j - t
        score_delta = parts[j] * (moves[j] - expected)
        if abs(step) > 1:
            side = 0 if step < 0 else 1
            far_sums[side].append(jnp.sum(score_delta.reshape(tile // 8, 8, tile), 0))
        else:
            near_ref[:, pl.ds((1 - step) * tile, tile)] += score_delta
        yield
        low_delta = score_delta.astype(low_type)
        value_part = dot_rows(parts[j].astype(low_type), delta)
        yield
        key_part = dot_rows(low_delta, query_ref[at[t], :])
        yield
        query_part = dot_rows(turned[j], low_delta)
        if t == 0:
            value_sum_ref[at[j], :] = value_part
            key_sum_ref[at[j], :] = key_part
        else:
            value_sum_ref[at[j], :] += value_part
            key_sum_ref[at[j], :] += key_part
        query_sum = query_part if j == 0 else query_sum + query_part
        yield
    result.append(query_sum.T * scale)
    yield


def run_together(first, second):
    first, second = list_steps(first), list_steps(second)
    first_total, second_total = next(first), next(second)
    done = 0
    for number in range(second_total):
        until = (number + 1) * first_total // second_total
        while done < until:
            next(first)
            done += 1
        next(second)


def list_steps(counted):
    count, steps = counted
    yield count
    yield from steps


def back_kernel(
    picks, scale, head, gate_ref, far_ref, column_ref, query_ref, key_ref, value_ref,
    query_mask_ref, key_mask_ref, delta_ref, found_hbm, query_delta_ref, key_delta_ref,
    value_delta_ref, diagonal_ref, sums_ref, bias_ref, near_ref, key_sum_ref, value_sum_ref,
    read_ref, rows_ref, rows_sems,
):
    sequence = pl.program_id(0)
    sequences = pl.num_programs(0)
    count = query_ref.shape[0] // tile
    block = rows_ref.shape[1]
    own = own_columns(picks)
    gate = gate_ref[0]

    def rows_copy(number, slot):
        start = (head * sequences * count + number) * block
        return pltpu.make_async_copy(
            found_hbm.at[pl.ds(pl.multiple_of(start, block), block)],
            rows_ref.at[slot],
            rows_sems.at[slot],
        )

    @pl.when(sequence == 0)
    def begin():
        for slot in range(2):
            rows_copy(slot, slot).start()
        bias_ref[...] = band(column_ref)
        near_ref[...] = jnp.zeros(near_ref.shape, full_type)
        sums_ref[...] = jnp.zeros(sums_ref.shape, full_type)

    at = [pl.ds(t * tile, tile) for t in range(count)]
    keys = [jnp.concatenate([key_ref[a, :], key_mask_ref[0, a, :]], 1) for a in at]
    turned = [key_ref[a, :].astype(full_type).T.astype(low_type) for a in at]
    gains, recall_gains, far_sums = [], [], [[], []]
    for t in range(count):
        slot = t % 2
        number = sequence * count + t
        rows_copy(number, slot).wait()
        result = []
        run_together(
            (
                2 * (tile // 8),
                recall_back_rows(
                    picks, scale, own, gate, query_ref, delta_ref, t * tile, rows_ref.at[slot],
                    read_ref, recall_gains, tile,
                ),
            ),
            (
                7 * count + 2,
                local_back_tile(
                    t, scale, gate, far_ref, query_ref, keys, turned, value_ref, query_mask_ref,
                    delta_ref, bias_ref, near_ref, key_sum_ref, value_sum_ref, gains, far_sums,
                    result,
                ),
            ),
        )
        query_delta_ref[at[t], :] = (result[0] + read_ref[...]).astype(low_type)

        @pl.when(number + 2 < sequences * count)
        def ahead():
            rows_copy(number + 2, slot).start()

    key_delta_ref[...] = (key_sum_ref[...] * scale).astype(low_type)
    value_delta_ref[...] = value_sum_ref[...].astype(low_type)
    sums_ref[0, 0:1] += functools.reduce(jnp.add, gains)
    for side in range(2):
        if far_sums[side]:
            sums_ref[0, 8 + 8 * side : 16 + 8 * side] += functools.reduce(jnp.add, far_sums[side])
    sums_ref[0, 24:32] += jnp.broadcast_to(functools.reduce(jnp.add, recall_gains), (8, tile))

    @pl.when(sequence == sequences - 1)
    def fold_diagonals():
        total = jnp.zeros((8, ring), full_type)
        for g in range(tile // 8):
            part = jnp.concatenate(
                [near_ref[pl.ds(g * 8, 8), :], jnp.zeros((8, ring - span), full_type)], 1
            )
            total = total + (pltpu.roll(part, ring - 8 * g, 1) if g else part)
        row = lax.broadcasted_iota(jnp.int32, (8, ring), 0)
        for bit in (1, 2, 4):
            total = jnp.where((row & bit) != 0, pltpu.roll(total, ring - bit, 1), total)
        diagonal_ref[0] = total


def back_head(
    projected, query_mask, key_mask, mixed_delta, found, columns, far, gates, seq_len, picks, scale,
    head, kept, carried, after,
):
    tokens = mixed_delta.shape[0]
    heads = gates.shape[0]
    width = mixed_delta.shape[1] // heads
    anywhere = pl.BlockSpec(memory_space=pl.ANY)
    chosen = slice(head, head + 1)
    extra = len(kept) + len(carried) + len(after)

    def rows_of(shift):
        return pl.BlockSpec((seq_len, width), lambda s: (s, head + shift * heads))

    def kernel(*refs):
        outs = refs[10 + extra :]
        back_kernel(picks, scale, head, *refs[:10], *outs[:5], *outs[5 + len(carried) :])

    mask_spec = pl.BlockSpec((1, seq_len, 128), lambda s: (s, 0, 0))
    smem = pl.BlockSpec(memory_space=pltpu.SMEM)
    rows_shape = jax.ShapeDtypeStruct((tokens, heads * width), low_type)
    first = 10 + len(kept)
    out = pl.pallas_call(
        kernel,
        grid=(tokens // seq_len,),
        in_specs=[
            smem,
            smem,
            pl.BlockSpec((1, 1, ring), lambda s: (0, 0, 0)),
            rows_of(0),
            rows_of(1),
            rows_of(2),
            mask_spec,
            mask_spec,
            rows_of(0),
            anywhere,
        ]
        + [anywhere] * extra,
        out_specs=[
            rows_of(0),
            rows_of(0),
            rows_of(0),
            pl.BlockSpec((1, 8, ring), lambda s: (0, 0, 0)),
            pl.BlockSpec((1, 32, tile), lambda s: (0, 0, 0)),
        ]
        + [anywhere] * len(carried),
        out_shape=[
            rows_shape,
            rows_shape,
            rows_shape,
            jax.ShapeDtypeStruct((1, 8, ring), full_type),
            jax.ShapeDtypeStruct((1, 32, tile), full_type),
        ]
        + [jax.ShapeDtypeStruct(part.shape, part.dtype) for part in carried],
        input_output_aliases={10 + i: i for i in range(len(kept))}
        | {first + i: 5 + i for i in range(len(carried))},
        scratch_shapes=[
            pltpu.VMEM((tile, span), full_type),
            pltpu.VMEM((tile, span), full_type),
            pltpu.VMEM((seq_len, width), full_type),
            pltpu.VMEM((seq_len, width), full_type),
            pltpu.VMEM((tile, width), full_type),
            pltpu.VMEM((2, tile * picks * 2, width), low_type),
            pltpu.SemaphoreType.DMA((2,)),
        ],
        compiler_params=pltpu.CompilerParams(vmem_limit_bytes=vmem_most),
        cost_estimate=pl.CostEstimate(
            flops=0, bytes_accessed=tokens * picks * width * 8, transcendentals=0
        ),
        name="back_head",
    )(
        gates[chosen], far[chosen], columns[chosen], projected, projected, projected, query_mask,
        key_mask, mixed_delta, found, *kept, *carried, *after,
    )
    return list(out[:3]), out[3], out[4], list(out[5:])


def mask_rows(block_ids):
    level = jnp.arange(128, dtype=jnp.int32)
    gap = block_ids[:, :, None] - level
    query_mask = jnp.where((gap >= 0) & (gap <= 1), 0.0, mask_gap).astype(low_type)
    key_mask = (gap == 0).astype(low_type)
    return query_mask, key_mask


def fetch(rows):
    group = lax.axis_size("tensor")
    return [rows] + [
        lax.ppermute(rows, "tensor", [((i + k) % group, i) for i in range(group)])
        for k in range(1, group)
    ]


def in_order(shares):
    group = lax.axis_size("tensor")
    rows = shares[0].shape[0]
    whole = jnp.zeros((group * rows,) + shares[0].shape[1:], shares[0].dtype)
    for k in range(group):
        start = ((lax.axis_index("tensor") + k) % group) * rows
        whole = lax.dynamic_update_slice_in_dim(whole, shares[k], start, 0)
    return whole


def share_of(whole, k, rows):
    start = ((lax.axis_index("tensor") + k) % lax.axis_size("tensor")) * rows
    return lax.dynamic_slice_in_dim(whole, start, rows, 0)


def fold(term, piece):
    group = lax.axis_size("tensor")
    sent = [
        lax.ppermute(
            term(piece(k)).astype(low_type), "tensor", [(i, (i + k) % group) for i in range(group)]
        )
        for k in range(1, group)
    ]
    return sum((part.astype(full_type) for part in sent), term(piece(0)))


def bit_orders():
    bits = lax.axis_size("dp").bit_length() - 1
    near = [(0, 1, 2), (1, 2, 0), (2, 0, 1)]
    return [list(head) + list(range(3, bits)) for head in near]


def swap_over(rows, bit):
    return lax.ppermute(rows, "dp", [(i, i ^ (1 << bit)) for i in range(lax.axis_size("dp"))])


def side_of(bit):
    return (lax.axis_index("dp") >> bit) & 1


def halve_step(parts, orders, step):
    kept, sent = [], []
    for part, order in zip(parts, orders):
        half = part.shape[0] // 2
        side = side_of(order[step])
        sent.append(
            swap_over(
                lax.dynamic_slice_in_dim(part, (1 - side) * half, half, 0), order[step]
            )
        )
        kept.append(lax.dynamic_slice_in_dim(part, side * half, half, 0))
    return kept, sent


def add_low(kept, sent):
    return [
        (a.astype(full_type) + b.astype(full_type)).astype(low_type) for a, b in zip(kept, sent)
    ]


def double_all(parts, beside):
    orders = bit_orders()
    for step in reversed(range(len(orders[0]))):
        got = [swap_over(part, order[step]) for part, order in zip(parts, orders)]
        if step == 1:
            got, beside = lax.optimization_barrier((got, beside))
        wider = []
        for part, other, order in zip(parts, got, orders):
            rows = part.shape[0]
            side = side_of(order[step])
            whole = jnp.zeros((2 * rows,) + part.shape[1:], part.dtype)
            whole = lax.dynamic_update_slice_in_dim(whole, part, side * rows, 0)
            wider.append(lax.dynamic_update_slice_in_dim(whole, other, (1 - side) * rows, 0))
        parts = wider
    return parts, beside


def pack(parts):
    width = min(part.shape[1] for part in parts)
    return jnp.concatenate(
        [
            part[:, start : start + width]
            for part in parts
            for start in range(0, part.shape[1], width)
        ],
        0,
    )


def gather_all(packed, parts, orders):
    whole = lax.all_gather(packed, "dp", axis=0)
    width = packed.shape[1]
    wide = []
    start = 0
    for part, order in zip(parts, orders):
        bits = len(order)
        rows = part.shape[0]
        columns = []
        for unused in range(part.shape[1] // width):
            piece = whole[:, start : start + rows].reshape((2,) * bits + (rows, width))
            piece = piece.transpose([bits - 1 - bit for bit in order] + [bits, bits + 1])
            columns.append(piece.reshape(-1, width))
            start += rows
        wide.append(jnp.concatenate(columns, 1).astype(full_type))
    return wide


def body(
    tokens,
    block_ids,
    memory_index,
    memory_keys,
    memory_values,
    attn_gain,
    query_weight,
    key_weight,
    value_weight,
    output_weight,
    position_table,
    memory_gate,
    mlp_gain,
    hidden_weight,
    return_weight,
    grad_output,
):
    share_rows = tokens.shape[0]
    seq_len = block_ids.shape[1]
    head_count, memory_rows, head_width = memory_keys.shape
    picks = memory_index.shape[2]
    inner_width = head_count * head_width
    scale = head_width ** (-0.5)

    offsets = jnp.arange(head_count, dtype=jnp.int32) * memory_rows
    index_rows = memory_index.transpose(1, 0, 2) + offsets[:, None, None]
    table = interleave(memory_keys, memory_values)

    token_full = tokens.astype(full_type)
    normed_rows = rms_scaled(token_full, attn_gain).astype(low_type)
    normed = lax.all_gather(normed_rows, "tensor", axis=0, tiled=True)
    joined = jnp.concatenate([query_weight, key_weight, value_weight], 1)
    projected = dot_rows(normed, joined).astype(low_type)
    found, late, early = gather_found(index_rows, table, projected, picks, scale)
    found = found.reshape(-1, head_width)

    query_mask, key_mask = mask_rows(block_ids)
    place = jnp.arange(ring, dtype=jnp.int32)
    place = jnp.where(place < span, place, place - ring)
    ahead = bucket_of(place - tile)
    behind = bucket_of(tile - place)
    level = jnp.arange(32, dtype=jnp.int32)
    ahead_hot = (ahead[:, None] == level).astype(full_type)
    behind_hot = (behind[:, None] == level).astype(full_type)
    scaled_table = position_table * log2_e
    ahead_columns = jnp.dot(ahead_hot, scaled_table, precision=exact_mode).T[:, None, :]
    behind_columns = jnp.dot(behind_hot, scaled_table, precision=exact_mode).T[:, None, :]
    far = jnp.stack([scaled_table[15], scaled_table[31]], 1)
    gates = jax.nn.sigmoid(memory_gate)

    mixed_rows = local_read(
        projected, query_mask, key_mask, early, late, ahead_columns, far, gates, seq_len, scale
    )
    middle = token_full + fold(
        lambda rows: dot_rows(rows, output_weight), lambda k: share_of(mixed_rows, k, share_rows)
    )
    second_rows = rms_scaled(middle, mlp_gain).astype(low_type)
    grad_full = jnp.concatenate(fetch(grad_output), 0)
    second = jnp.concatenate(fetch(second_rows), 0)
    active, slope = gelu_pair(dot_rows(second, hidden_weight))
    slope = lax.optimization_barrier(slope)
    orders = bit_orders()
    steps = len(orders[0])

    return_low = dot_outer(active, grad_full).astype(low_type)
    return_half = return_low.shape[0] // 2
    kept_back, sent_back = halve_step(
        [return_low[:return_half], return_low[return_half:]], orders[1:], 0
    )
    active_delta = dot_inner(grad_full, return_weight)
    hidden_delta = (active_delta * slope.astype(full_type)).astype(low_type)
    second_delta = fold(
        lambda rows: dot_inner(rows, hidden_weight),
        lambda k: lax.slice_in_dim(hidden_delta, k * share_rows, (k + 1) * share_rows),
    )
    hidden_half = hidden_delta.shape[1] // 2
    hidden_parts = [
        dot_outer(second, hidden_delta[:, :hidden_half]).astype(low_type),
        dot_outer(second, hidden_delta[:, hidden_half:]).astype(low_type),
    ]
    kept, sent = halve_step(hidden_parts, orders[:2], 0)

    kept_back, kept = lax.optimization_barrier((kept_back, kept))
    kept_back, sent_back = halve_step(add_low(kept_back, sent_back), orders[1:], 1)

    second_back = jax.vjp(rms_scaled, middle, mlp_gain)[1]
    middle_part, mlp_gain_part = second_back(second_delta)
    middle_delta = grad_output.astype(full_type) + middle_part
    middle_low = middle_delta.astype(low_type)
    kept, kept_back, middle_low = lax.optimization_barrier((kept, kept_back, middle_low))
    kept, sent = halve_step(add_low(kept, sent), orders[:2], 1)
    kept_back, sent_back = halve_step(add_low(kept_back, sent_back), orders[1:], 2)
    middle_full = in_order(fetch(middle_low))
    mixed_delta = dot_inner(middle_full, output_weight).astype(low_type)
    kept, kept_back, mixed_delta = lax.optimization_barrier((kept, kept_back, mixed_delta))
    kept, sent = halve_step(add_low(kept, sent), orders[:2], 2)
    kept_back, sent_back = halve_step(add_low(kept_back, sent_back), orders[1:], 3)
    taken = 2
    for step in range(4, steps):
        kept_back, sent_back = halve_step(add_low(kept_back, sent_back), orders[1:], step)
    layer_output = (
        middle
        + fold(
            lambda rows: dot_rows(rows, return_weight),
            lambda k: lax.slice_in_dim(active, k * share_rows, (k + 1) * share_rows),
        )
    ).astype(low_type)

    shards, packed = [], []
    deltas = []
    diagonals = []
    local_sums = []
    for head in range(head_count):
        deltas, diagonal_now, sums_now, kept = back_head(
            projected, query_mask, key_mask, mixed_delta, found, behind_columns, far, gates,
            seq_len, picks, scale, head, deltas, kept, packed,
        )
        diagonals.append(diagonal_now)
        local_sums.append(sums_now)
        if taken < steps - 1:
            taken += 1
            kept, sent = halve_step(add_low(kept, sent), orders[:2], taken)
        elif not shards:
            shards = add_low(kept, sent) + add_low(kept_back, sent_back)
            packed = [pack(shards)]
            kept = []
    while taken < steps - 1:
        taken += 1
        kept, sent = halve_step(add_low(kept, sent), orders[:2], taken)
    if not shards:
        shards = add_low(kept, sent) + add_low(kept_back, sent_back)
        packed = [pack(shards)]
    hidden_low_sum, hidden_high_sum, return_low_sum, return_high_sum = gather_all(
        packed[0], shards, orders[:2] + orders[1:]
    )
    hidden_sum = jnp.concatenate([hidden_low_sum, hidden_high_sum], 1)
    return_sum = jnp.concatenate([return_low_sum, return_high_sum], 0)
    query_delta, key_delta, value_delta = deltas
    diagonals = jnp.concatenate(diagonals, 0)
    local_sums = jnp.concatenate(local_sums, 0)
    recall_gain = jnp.sum(local_sums[:, 24:32, 0], 1)
    local_gain = jnp.sum(local_sums[:, 0], 1)
    gate_part = gates * (1.0 - gates) * recall_gain - gates * local_gain
    diagonal_sums = jnp.sum(diagonals, 1)
    table_part = jnp.dot(diagonal_sums, behind_hot, precision=exact_mode)
    far_left = jnp.sum(local_sums[:, 8:16], (1, 2))
    far_right = jnp.sum(local_sums[:, 16:24], (1, 2))
    table_part = table_part + far_left[:, None] * (level == 15) + far_right[:, None] * (level == 31)

    project_delta = jnp.concatenate([query_delta, key_delta, value_delta], 1)
    joined_part = dot_outer(normed, project_delta)
    attn_gain_part = jnp.sum(joined_part * joined.astype(full_type), 1) / attn_gain
    model_width = tokens.shape[1]
    small = jnp.concatenate([table_part.reshape(-1), gate_part])
    small = jnp.pad(small, (0, model_width - small.shape[0]))
    extra = jnp.stack([attn_gain_part, mlp_gain_part, small], 1)
    extra = jnp.pad(extra, ((0, 0), (0, 125)))
    joined_low = jnp.concatenate([joined_part, extra], 1).astype(low_type)
    joined_half = joined_low.shape[0] // 2
    last = [
        joined_low[:joined_half],
        joined_low[joined_half:],
        dot_outer(mixed_rows, middle_full).astype(low_type),
    ]
    for step in range(steps):
        last = add_low(*halve_step(last, orders, step))
    last, (hidden_sum, return_sum) = double_all(last, (hidden_sum, return_sum))
    *joined_sum, output_sum = last

    normed_delta = fold(
        lambda rows: dot_inner(rows, joined), lambda k: share_of(project_delta, k, share_rows)
    )
    first_back = jax.vjp(rms_scaled, token_full, attn_gain)[1]
    tokens_grad = (middle_delta + first_back(normed_delta)[0]).astype(low_type)

    def joined_columns(start, stop):
        return jnp.concatenate([part[:, start:stop].astype(full_type) for part in joined_sum], 0)

    last_columns = joined_columns(3 * inner_width, 3 * inner_width + 128)
    gains = sum(fetch(last_columns[:, :2].T))
    small_sum = last_columns[:, 2]
    table_size = head_count * 32
    return (
        layer_output,
        tokens_grad,
        gains[0],
        joined_columns(0, inner_width),
        joined_columns(inner_width, 2 * inner_width),
        joined_columns(2 * inner_width, 3 * inner_width),
        output_sum.astype(full_type),
        small_sum[:table_size].reshape(head_count, 32).T,
        small_sum[table_size : table_size + head_count],
        gains[1],
        hidden_sum,
        return_sum,
    )


def solution(mesh):
    def run(*arrays):
        with jax.sharding.use_abstract_mesh(mesh.abstract_mesh):
            return jax.shard_map(
                body,
                mesh=mesh,
                in_specs=(
                    P(("dp", "tensor"), None),
                    P("dp", None),
                    P("dp", "tensor", None),
                    P("tensor", None, None),
                    P("tensor", None, None),
                    P(),
                    P(None, "tensor"),
                    P(None, "tensor"),
                    P(None, "tensor"),
                    P("tensor", None),
                    P(None, "tensor"),
                    P("tensor"),
                    P(),
                    P(None, "tensor"),
                    P("tensor", None),
                    P(("dp", "tensor"), None),
                ),
                out_specs=(
                    P(("dp", "tensor"), None),
                    P(("dp", "tensor"), None),
                    P(),
                    P(None, "tensor"),
                    P(None, "tensor"),
                    P(None, "tensor"),
                    P("tensor", None),
                    P(None, "tensor"),
                    P("tensor"),
                    P(),
                    P(None, "tensor"),
                    P("tensor", None),
                ),
                check_vma=False,
            )(*arrays)

    return run
```

```python
import functools
import math

import jax
import jax.numpy as jnp
from jax import lax
from jax.experimental import pallas as pl
from jax.experimental.pallas import tpu as pltpu
from jax.sharding import PartitionSpec as P

eps_norm = 1e-06
far_steps = (12, 16, 23, 32, 46, 64, 91)
exact_mode = lax.Precision.HIGHEST
low_type = jnp.bfloat16
full_type = jnp.float32
log2_e = math.log2(math.e)
tile = 256
span = 3 * tile
ring = 1024
mask_gap = -(2.0**100)
vmem_most = 60 * 2**20


def bucket_of(relative):
    upper_half = jnp.where(relative > 0, 16, 0).astype(jnp.int32)
    distance = jnp.abs(relative)
    far_bucket = 8 + sum(((distance >= step_size).astype(jnp.int32) for step_size in far_steps))
    return upper_half + jnp.where(distance < 8, distance, far_bucket)


def rms_scaled(rows, gain):
    return rows * lax.rsqrt(jnp.mean(rows * rows, -1, keepdims=True) + eps_norm) * gain


def gelu_pair(rows):
    reach = math.sqrt(2.0 / math.pi)
    square = rows * rows
    turn = jnp.tanh(reach * rows * (1.0 + 0.044715 * square))
    share = 0.5 * (1.0 + turn)
    steep = 0.5 * (1.0 - turn * turn) * reach * (1.0 + 3.0 * 0.044715 * square)
    return (rows * share).astype(low_type), (share + rows * steep).astype(low_type)


def dot_rows(left, right):
    return jnp.dot(left, right, preferred_element_type=full_type)


def dot_outer(left, right):
    return lax.dot_general(
        left, right, (((0,), (0,)), ((), ())), preferred_element_type=full_type
    )


def dot_inner(left, right):
    return lax.dot_general(
        left, right, (((1,), (1,)), ((), ())), preferred_element_type=full_type
    )


def interleave_kernel(key_ref, value_ref, table_ref):
    rows = key_ref.shape[1]
    row = lax.broadcasted_iota(jnp.int32, (256, 256), 0)
    column = lax.broadcasted_iota(jnp.int32, (256, 256), 1)
    order = jnp.where(column == (row // 2 + (row % 2) * 128), 1.0, 0.0).astype(low_type)
    for part in range(rows // 256):
        low, high = pl.ds(part * 256, 128), pl.ds(part * 256 + 128, 128)
        both = jnp.concatenate(
            [
                jnp.concatenate([key_ref[0, low], key_ref[0, high]], 1),
                jnp.concatenate([value_ref[0, low], value_ref[0, high]], 1),
            ],
            0,
        )
        mixed = dot_rows(order, both).astype(low_type)
        table_ref[pl.ds(part * 512, 256), :] = mixed[:, :128]
        table_ref[pl.ds(part * 512 + 256, 256), :] = mixed[:, 128:]


def interleave(memory_keys, memory_values):
    heads, rows, width = memory_keys.shape
    step = min(8192, rows)
    spec = pl.BlockSpec((1, step, width), lambda h, i: (h, i, 0))
    return pl.pallas_call(
        interleave_kernel,
        grid=(heads, rows // step),
        in_specs=[spec, spec],
        out_specs=pl.BlockSpec((2 * step, width), lambda h, i: (h * (rows // step) + i, 0)),
        out_shape=jax.ShapeDtypeStruct((heads * rows * 2, width), low_type),
        compiler_params=pltpu.CompilerParams(vmem_limit_bytes=vmem_most),
        cost_estimate=pl.CostEstimate(
            flops=heads * rows * 4 * 256 * width,
            bytes_accessed=heads * rows * width * 8,
            transcendentals=0,
        ),
        name="interleave",
    )(memory_keys, memory_values).reshape(heads, rows, 2, width)


def own_columns(picks):
    shape = (8, 8 * picks * 2)
    lane = lax.broadcasted_iota(jnp.int32, shape, 1)
    row = lax.broadcasted_iota(jnp.int32, shape, 0)
    return jnp.logical_and(lane // (2 * picks) == row, lane % 2 == 0)


def copy_rows(picked, first, table_ref, found_ref, start, count):
    for at in range(0, count, 8):
        rows_now = [
            table_ref[picked[(first + at + j) // 128, (first + at + j) % 128]] for j in range(8)
        ]
        for j in range(8):
            found_ref[start + at + j] = rows_now[j]
        yield


def recall_rows(picks, scale, own, query_ref, query_at, rows_ref, read_ref, read_at, tokens):
    wide = 8 * picks * 2
    groups = range(tokens // 8)
    scores = []
    for g in groups:
        rows = rows_ref[pl.ds(g * wide, wide), :]
        scores.append(dot_inner(query_ref[pl.ds(query_at + g * 8, 8), :], rows))
        yield
    shifted = []
    totals = []
    for g in groups:
        masked = jnp.where(own, scores[g] * (scale * log2_e), -jnp.inf)
        exponent = jnp.exp2(masked - jnp.max(masked, 1, keepdims=True))
        totals.append(jnp.sum(exponent, 1, keepdims=True))
        shifted.append(pltpu.roll(exponent, 1, 1).astype(low_type))
        yield
    for g in groups:
        rows = rows_ref[pl.ds(g * wide, wide), :]
        read_ref[pl.ds(read_at + g * 8, 8), :] = dot_rows(shifted[g], rows) / totals[g]
        yield


def weave(many, many_count, few, few_count):
    done = 0
    for number in range(few_count):
        until = (number + 1) * many_count // few_count
        while done < until:
            next(many)
            done += 1
        next(few)


def gather_kernel(
    picks, scale, index_hbm, table_hbm, now_ref, before_ref, found_ref, late_ref, early_ref,
    table_ref, table_sems, index_a, index_b, index_sems, stage_ref, stage_sems,
):
    step = pl.program_id(0)
    steps = pl.num_programs(0) - 1
    heads = table_sems.shape[0]
    blocks = steps // heads
    chunk = found_ref.shape[0] // 2
    rows = table_ref.shape[0] // heads
    slots = (index_a, index_b)
    part = chunk // 2
    tokens = part // picks
    own = own_columns(picks)
    flat = found_ref.reshape(4 * chunk, 128)

    def index_copy(number, slot):
        return pltpu.make_async_copy(index_hbm.at[number], slots[slot], index_sems.at[slot])

    def table_copy(number):
        where = pl.ds(number * rows, rows)
        return pltpu.make_async_copy(
            table_hbm.at[where], table_ref.at[where], table_sems.at[number]
        )

    def stage_copy(number):
        return pltpu.make_async_copy(
            flat.at[pl.ds(number * 2 * part, 2 * part)], stage_ref.at[number], stage_sems.at[number]
        )

    def reads(number, query_ref, read_ref):
        return recall_rows(
            picks, scale, own, query_ref, (number % 2) * tokens, stage_ref.at[number], read_ref,
            (number % 2) * tokens, tokens,
        )

    @pl.when(step == 0)
    def start_all():
        index_copy(0, 0).start()
        index_copy(1, 1).start()
        for number in range(heads):
            table_copy(number).start()
        stage_copy(2).start()
        stage_copy(3).start()

    @pl.when(jnp.logical_and(step < steps, step % blocks == 0))
    def wait_table():
        table_copy(step // blocks).wait()

    @pl.when(step < steps)
    def work():
        following = jnp.minimum(step + 1, steps - 1)
        for number in range(4):
            slot = number // 2
            if number % 2 == 0:
                index_copy(2 * step + slot, slot).wait()
            finished = (number + 2) % 4
            stage_copy(finished).wait()
            copied = copy_rows(
                slots[slot], (number % 2) * part, table_ref, found_ref, number * part, part
            )
            if number < 2:
                read = reads(finished, before_ref, late_ref)
            else:
                read = reads(finished, now_ref, early_ref)
            weave(copied, part // 8, read, 3 * (tokens // 8))
            stage_copy(number).start()
            if number % 2 == 1:
                index_copy(2 * following + slot, slot).start()

    @pl.when(step == steps)
    def finish():
        for number in (2, 3):
            stage_copy(number).wait()
            for unused in reads(number, before_ref, late_ref):
                pass
        for slot in range(2):
            index_copy(2 * (steps - 1) + slot, slot).wait()


def gather_found(index_rows, table, queries, picks, scale):
    heads, rows, unused, width = table.shape
    tokens = queries.shape[0]
    half = 128
    blocks = tokens // (2 * half)
    steps = heads * blocks
    chunk = half * picks

    def query_spec(shift):
        def place(t):
            at = jnp.clip(t - shift, 0, steps - 1)
            return (2 * (at % blocks) + shift, at // blocks)

        return pl.BlockSpec((half, width), place)

    return pl.pallas_call(
        functools.partial(gather_kernel, picks, scale),
        grid=(steps + 1,),
        in_specs=[
            pl.BlockSpec(memory_space=pl.ANY),
            pl.BlockSpec(memory_space=pl.ANY),
            query_spec(0),
            query_spec(1),
        ],
        out_specs=[
            pl.BlockSpec((2 * chunk, 2, width), lambda t: (jnp.minimum(t, steps - 1), 0, 0)),
            pl.BlockSpec((half, width), lambda t: (jnp.maximum(t - 1, 0), 0)),
            pl.BlockSpec((half, width), lambda t: (jnp.minimum(t, steps - 1), 0)),
        ],
        out_shape=[
            jax.ShapeDtypeStruct((heads * tokens * picks, 2, width), low_type),
            jax.ShapeDtypeStruct((heads * tokens // 2, width), full_type),
            jax.ShapeDtypeStruct((heads * tokens // 2, width), full_type),
        ],
        scratch_shapes=[
            pltpu.VMEM((heads * rows, 2, width), low_type),
            pltpu.SemaphoreType.DMA((heads,)),
            pltpu.SMEM((chunk // 128, 128), jnp.int32),
            pltpu.SMEM((chunk // 128, 128), jnp.int32),
            pltpu.SemaphoreType.DMA((2,)),
            pltpu.VMEM((4, chunk, width), low_type),
            pltpu.SemaphoreType.DMA((4,)),
        ],
        compiler_params=pltpu.CompilerParams(vmem_limit_bytes=vmem_most),
        cost_estimate=pl.CostEstimate(
            flops=0, bytes_accessed=4 * heads * tokens * picks * width * 4, transcendentals=0
        ),
        name="gather_found",
    )(
        index_rows.reshape(-1, chunk // 128, 128), table.reshape(heads * rows, 2, width), queries,
        queries,
    )


def band(column_ref):
    wide = jnp.broadcast_to(column_ref[0], (tile, ring))
    return pltpu.roll(wide, 0, 1, stride=1, stride_axis=0)[:, :span]


def local_kernel(
    scale, gate_ref, far_ref, column_ref, query_ref, key_ref, value_ref, query_mask_ref,
    key_mask_ref, early_ref, late_ref, mixed_ref, bias_ref,
):
    head = pl.program_id(0)

    @pl.when(pl.program_id(1) == 0)
    def make_band():
        bias_ref[...] = band(column_ref)

    gate = gate_ref[head]
    count = query_ref.shape[0] // tile
    at = [pl.ds(t * tile, tile) for t in range(count)]
    keys = [jnp.concatenate([key_ref[a, :], key_mask_ref[0, a, :]], 1) for a in at]
    for t in range(count):
        rows = jnp.concatenate([query_ref[at[t], :], query_mask_ref[0, at[t], :]], 1)
        parts = []
        for j in range(count):
            step = j - t
            if step < -1:
                bias = far_ref[head, 0]
            elif step > 1:
                bias = far_ref[head, 1]
            else:
                bias = bias_ref[:, pl.ds((step + 1) * tile, tile)]
            parts.append(dot_inner(rows, keys[j]) * (scale * log2_e) + bias)
        top = jnp.max(functools.reduce(jnp.maximum, parts), 1, keepdims=True)
        parts = [jnp.exp2(part - top) for part in parts]
        total = jnp.sum(functools.reduce(jnp.add, parts), 1, keepdims=True)
        read = sum(dot_rows(parts[j].astype(low_type), value_ref[at[j], :]) for j in range(count))
        half = pl.ds(t * (tile // 2), tile // 2)
        recalled = jnp.concatenate([early_ref[half, :], late_ref[half, :]], 0)
        mixed_ref[at[t], :] = (gate * recalled + ((1.0 - gate) / total) * read).astype(low_type)


def local_read(projected, query_mask, key_mask, early, late, columns, far, gates, seq_len, scale):
    tokens, width = projected.shape
    heads = gates.shape[0]
    width = width // (3 * heads)
    sequences = tokens // seq_len
    half_spec = pl.BlockSpec((seq_len // 2, width), lambda h, s: (h * sequences + s, 0))

    def rows_of(shift):
        return pl.BlockSpec((seq_len, width), lambda h, s: (s, h + shift * heads))

    mask_spec = pl.BlockSpec((1, seq_len, 128), lambda h, s: (s, 0, 0))
    smem = pl.BlockSpec(memory_space=pltpu.SMEM)
    return pl.pallas_call(
        functools.partial(local_kernel, scale),
        grid=(heads, tokens // seq_len),
        in_specs=[
            smem,
            smem,
            pl.BlockSpec((1, 1, ring), lambda h, s: (h, 0, 0)),
            rows_of(0),
            rows_of(1),
            rows_of(2),
            mask_spec,
            mask_spec,
            half_spec,
            half_spec,
        ],
        out_specs=rows_of(0),
        out_shape=jax.ShapeDtypeStruct((tokens, heads * width), low_type),
        scratch_shapes=[pltpu.VMEM((tile, span), full_type)],
        compiler_params=pltpu.CompilerParams(vmem_limit_bytes=vmem_most),
        cost_estimate=pl.CostEstimate(
            flops=0, bytes_accessed=heads * tokens * seq_len * 20, transcendentals=0
        ),
        name="local_read",
    )(gates, far, columns, projected, projected, projected, query_mask, key_mask, early, late)


def recall_back_rows(
    picks, scale, own, gate, query_ref, delta_ref, at, rows_ref, read_ref, gains, tokens
):
    wide = 8 * picks * 2
    flight = 8
    groups = tokens // 8
    both = {}
    for first in range(-flight, groups, flight):
        for g in range(first + flight, min(first + 2 * flight, groups)):
            where = pl.ds(at + g * 8, 8)
            pair = jnp.concatenate([query_ref[where, :], delta_ref[where, :]], 0)
            both[g] = dot_inner(pair, rows_ref[pl.ds(g * wide, wide), :])
            yield
        for g in range(max(first, 0), first + flight if first >= 0 else 0):
            pair = both.pop(g)
            masked = jnp.where(own, pair[:8] * (scale * log2_e), -jnp.inf)
            exponent = jnp.exp2(masked - jnp.max(masked, 1, keepdims=True))
            weights = exponent / jnp.sum(exponent, 1, keepdims=True)
            reads = pltpu.roll(pair[8:], wide - 1, 1)
            expected = jnp.sum(weights * reads, 1, keepdims=True)
            gains.append(expected)
            score_delta = (weights * (reads - expected)).astype(low_type)
            rows = rows_ref[pl.ds(g * wide, wide), :]
            read_ref[pl.ds(g * 8, 8), :] = dot_rows(score_delta, rows) * (scale * gate)
            yield


def local_back_tile(
    t, scale, gate, far_ref, query_ref, keys, turned, value_ref, query_mask_ref, delta_ref,
    bias_ref, near_ref, key_sum_ref, value_sum_ref, gains, far_sums, result,
):
    count = len(keys)
    at = [pl.ds(j * tile, tile) for j in range(count)]
    rows = jnp.concatenate([query_ref[at[t], :], query_mask_ref[0, at[t], :]], 1)
    delta = ((1.0 - gate) * delta_ref[at[t], :].astype(full_type)).astype(low_type)
    parts = []
    for j in range(count):
        step = j - t
        if step < -1:
            bias = far_ref[0, 0]
        elif step > 1:
            bias = far_ref[0, 1]
        else:
            bias = bias_ref[:, pl.ds((1 - step) * tile, tile)]
        parts.append(dot_inner(keys[j], rows) * (scale * log2_e) + bias)
        yield
    top = jnp.max(functools.reduce(jnp.maximum, parts), 0, keepdims=True)
    yield
    for j in range(count):
        parts[j] = jnp.exp2(parts[j] - top)
        yield
    inverse = 1.0 / jnp.sum(functools.reduce(jnp.add, parts), 0, keepdims=True)
    moves = []
    products = []
    for j in range(count):
        parts[j] = parts[j] * inverse
        moves.append(dot_inner(value_ref[at[j], :], delta))
        products.append(parts[j] * moves[j])
        yield
    expected = jnp.sum(functools.reduce(jnp.add, products), 0, keepdims=True)
    gains.append(expected)
    query_sum = None
    for j in range(count):
        step = j - t
        score_delta = parts[j] * (moves[j] - expected)
        if abs(step) > 1:
            side = 0 if step < 0 else 1
            far_sums[side].append(jnp.sum(score_delta.reshape(tile // 8, 8, tile), 0))
        else:
            near_ref[:, pl.ds((1 - step) * tile, tile)] += score_delta
        yield
        low_delta = score_delta.astype(low_type)
        value_part = dot_rows(parts[j].astype(low_type), delta)
        yield
        key_part = dot_rows(low_delta, query_ref[at[t], :])
        yield
        query_part = dot_rows(turned[j], low_delta)
        if t == 0:
            value_sum_ref[at[j], :] = value_part
            key_sum_ref[at[j], :] = key_part
        else:
            value_sum_ref[at[j], :] += value_part
            key_sum_ref[at[j], :] += key_part
        query_sum = query_part if j == 0 else query_sum + query_part
        yield
    result.append(query_sum.T * scale)
    yield


def run_together(first, second):
    first, second = list_steps(first), list_steps(second)
    first_total, second_total = next(first), next(second)
    done = 0
    for number in range(second_total):
        until = (number + 1) * first_total // second_total
        while done < until:
            next(first)
            done += 1
        next(second)


def list_steps(counted):
    count, steps = counted
    yield count
    yield from steps


def back_kernel(
    picks, scale, head, gate_ref, far_ref, column_ref, query_ref, key_ref, value_ref,
    query_mask_ref, key_mask_ref, delta_ref, found_hbm, query_delta_ref, key_delta_ref,
    value_delta_ref, diagonal_ref, sums_ref, bias_ref, near_ref, key_sum_ref, value_sum_ref,
    read_ref, rows_ref, rows_sems,
):
    sequence = pl.program_id(0)
    sequences = pl.num_programs(0)
    count = query_ref.shape[0] // tile
    block = rows_ref.shape[1]
    own = own_columns(picks)
    gate = gate_ref[0]

    def rows_copy(number, slot):
        start = (head * sequences * count + number) * block
        return pltpu.make_async_copy(
            found_hbm.at[pl.ds(pl.multiple_of(start, block), block)],
            rows_ref.at[slot],
            rows_sems.at[slot],
        )

    @pl.when(sequence == 0)
    def begin():
        for slot in range(2):
            rows_copy(slot, slot).start()
        bias_ref[...] = band(column_ref)
        near_ref[...] = jnp.zeros(near_ref.shape, full_type)
        sums_ref[...] = jnp.zeros(sums_ref.shape, full_type)

    at = [pl.ds(t * tile, tile) for t in range(count)]
    keys = [jnp.concatenate([key_ref[a, :], key_mask_ref[0, a, :]], 1) for a in at]
    turned = [key_ref[a, :].astype(full_type).T.astype(low_type) for a in at]
    gains, recall_gains, far_sums = [], [], [[], []]
    for t in range(count):
        slot = t % 2
        number = sequence * count + t
        rows_copy(number, slot).wait()
        result = []
        run_together(
            (
                2 * (tile // 8),
                recall_back_rows(
                    picks, scale, own, gate, query_ref, delta_ref, t * tile, rows_ref.at[slot],
                    read_ref, recall_gains, tile,
                ),
            ),
            (
                7 * count + 2,
                local_back_tile(
                    t, scale, gate, far_ref, query_ref, keys, turned, value_ref, query_mask_ref,
                    delta_ref, bias_ref, near_ref, key_sum_ref, value_sum_ref, gains, far_sums,
                    result,
                ),
            ),
        )
        query_delta_ref[at[t], :] = (result[0] + read_ref[...]).astype(low_type)

        @pl.when(number + 2 < sequences * count)
        def ahead():
            rows_copy(number + 2, slot).start()

    key_delta_ref[...] = (key_sum_ref[...] * scale).astype(low_type)
    value_delta_ref[...] = value_sum_ref[...].astype(low_type)
    sums_ref[0, 0:1] += functools.reduce(jnp.add, gains)
    for side in range(2):
        if far_sums[side]:
            sums_ref[0, 8 + 8 * side : 16 + 8 * side] += functools.reduce(jnp.add, far_sums[side])
    sums_ref[0, 24:32] += jnp.broadcast_to(functools.reduce(jnp.add, recall_gains), (8, tile))

    @pl.when(sequence == sequences - 1)
    def fold_diagonals():
        total = jnp.zeros((8, ring), full_type)
        for g in range(tile // 8):
            part = jnp.concatenate(
                [near_ref[pl.ds(g * 8, 8), :], jnp.zeros((8, ring - span), full_type)], 1
            )
            total = total + (pltpu.roll(part, ring - 8 * g, 1) if g else part)
        row = lax.broadcasted_iota(jnp.int32, (8, ring), 0)
        for bit in (1, 2, 4):
            total = jnp.where((row & bit) != 0, pltpu.roll(total, ring - bit, 1), total)
        diagonal_ref[0] = total


def back_head(
    projected, query_mask, key_mask, mixed_delta, found, columns, far, gates, seq_len, picks, scale,
    head, kept, carried, after,
):
    tokens = mixed_delta.shape[0]
    heads = gates.shape[0]
    width = mixed_delta.shape[1] // heads
    anywhere = pl.BlockSpec(memory_space=pl.ANY)
    chosen = slice(head, head + 1)
    extra = len(kept) + len(carried) + len(after)

    def rows_of(shift):
        return pl.BlockSpec((seq_len, width), lambda s: (s, head + shift * heads))

    def kernel(*refs):
        outs = refs[10 + extra :]
        back_kernel(picks, scale, head, *refs[:10], *outs[:5], *outs[5 + len(carried) :])

    mask_spec = pl.BlockSpec((1, seq_len, 128), lambda s: (s, 0, 0))
    smem = pl.BlockSpec(memory_space=pltpu.SMEM)
    rows_shape = jax.ShapeDtypeStruct((tokens, heads * width), low_type)
    first = 10 + len(kept)
    out = pl.pallas_call(
        kernel,
        grid=(tokens // seq_len,),
        in_specs=[
            smem,
            smem,
            pl.BlockSpec((1, 1, ring), lambda s: (0, 0, 0)),
            rows_of(0),
            rows_of(1),
            rows_of(2),
            mask_spec,
            mask_spec,
            rows_of(0),
            anywhere,
        ]
        + [anywhere] * extra,
        out_specs=[
            rows_of(0),
            rows_of(0),
            rows_of(0),
            pl.BlockSpec((1, 8, ring), lambda s: (0, 0, 0)),
            pl.BlockSpec((1, 32, tile), lambda s: (0, 0, 0)),
        ]
        + [anywhere] * len(carried),
        out_shape=[
            rows_shape,
            rows_shape,
            rows_shape,
            jax.ShapeDtypeStruct((1, 8, ring), full_type),
            jax.ShapeDtypeStruct((1, 32, tile), full_type),
        ]
        + [jax.ShapeDtypeStruct(part.shape, part.dtype) for part in carried],
        input_output_aliases={10 + i: i for i in range(len(kept))}
        | {first + i: 5 + i for i in range(len(carried))},
        scratch_shapes=[
            pltpu.VMEM((tile, span), full_type),
            pltpu.VMEM((tile, span), full_type),
            pltpu.VMEM((seq_len, width), full_type),
            pltpu.VMEM((seq_len, width), full_type),
            pltpu.VMEM((tile, width), full_type),
            pltpu.VMEM((2, tile * picks * 2, width), low_type),
            pltpu.SemaphoreType.DMA((2,)),
        ],
        compiler_params=pltpu.CompilerParams(vmem_limit_bytes=vmem_most),
        cost_estimate=pl.CostEstimate(
            flops=0, bytes_accessed=tokens * picks * width * 8, transcendentals=0
        ),
        name="back_head",
    )(
        gates[chosen], far[chosen], columns[chosen], projected, projected, projected, query_mask,
        key_mask, mixed_delta, found, *kept, *carried, *after,
    )
    return list(out[:3]), out[3], out[4], list(out[5:])


def mask_rows(block_ids):
    level = jnp.arange(128, dtype=jnp.int32)
    gap = block_ids[:, :, None] - level
    query_mask = jnp.where((gap >= 0) & (gap <= 1), 0.0, mask_gap).astype(low_type)
    key_mask = (gap == 0).astype(low_type)
    return query_mask, key_mask


def fetch(rows):
    group = lax.axis_size("tensor")
    return [rows] + [
        lax.ppermute(rows, "tensor", [((i + k) % group, i) for i in range(group)])
        for k in range(1, group)
    ]


def in_order(shares):
    group = lax.axis_size("tensor")
    rows = shares[0].shape[0]
    whole = jnp.zeros((group * rows,) + shares[0].shape[1:], shares[0].dtype)
    for k in range(group):
        start = ((lax.axis_index("tensor") + k) % group) * rows
        whole = lax.dynamic_update_slice_in_dim(whole, shares[k], start, 0)
    return whole


def share_of(whole, k, rows):
    start = ((lax.axis_index("tensor") + k) % lax.axis_size("tensor")) * rows
    return lax.dynamic_slice_in_dim(whole, start, rows, 0)


def fold(term, piece):
    group = lax.axis_size("tensor")
    sent = [
        lax.ppermute(
            term(piece(k)).astype(low_type), "tensor", [(i, (i + k) % group) for i in range(group)]
        )
        for k in range(1, group)
    ]
    return sum((part.astype(full_type) for part in sent), term(piece(0)))


def bit_orders():
    bits = lax.axis_size("dp").bit_length() - 1
    near = [(0, 1, 2), (1, 2, 0), (2, 0, 1)]
    return [list(head) + list(range(3, bits)) for head in near]


def swap_over(rows, bit):
    return lax.ppermute(rows, "dp", [(i, i ^ (1 << bit)) for i in range(lax.axis_size("dp"))])


def side_of(bit):
    return (lax.axis_index("dp") >> bit) & 1


def halve_step(parts, orders, step):
    kept, sent = [], []
    for part, order in zip(parts, orders):
        half = part.shape[0] // 2
        side = side_of(order[step])
        sent.append(
            swap_over(
                lax.dynamic_slice_in_dim(part, (1 - side) * half, half, 0), order[step]
            )
        )
        kept.append(lax.dynamic_slice_in_dim(part, side * half, half, 0))
    return kept, sent


def add_low(kept, sent):
    return [
        (a.astype(full_type) + b.astype(full_type)).astype(low_type) for a, b in zip(kept, sent)
    ]


def double_all(parts, beside):
    orders = bit_orders()
    for step in reversed(range(len(orders[0]))):
        got = [swap_over(part, order[step]) for part, order in zip(parts, orders)]
        if step == 1:
            got, beside = lax.optimization_barrier((got, beside))
        wider = []
        for part, other, order in zip(parts, got, orders):
            rows = part.shape[0]
            side = side_of(order[step])
            whole = jnp.zeros((2 * rows,) + part.shape[1:], part.dtype)
            whole = lax.dynamic_update_slice_in_dim(whole, part, side * rows, 0)
            wider.append(lax.dynamic_update_slice_in_dim(whole, other, (1 - side) * rows, 0))
        parts = wider
    return parts, beside


def pack(parts):
    width = min(part.shape[1] for part in parts)
    return jnp.concatenate(
        [
            part[:, start : start + width]
            for part in parts
            for start in range(0, part.shape[1], width)
        ],
        0,
    )


def gather_all(packed, parts, orders):
    whole = lax.all_gather(packed, "dp", axis=0)
    width = packed.shape[1]
    wide = []
    start = 0
    for part, order in zip(parts, orders):
        bits = len(order)
        rows = part.shape[0]
        columns = []
        for unused in range(part.shape[1] // width):
            piece = whole[:, start : start + rows].reshape((2,) * bits + (rows, width))
            piece = piece.transpose([bits - 1 - bit for bit in order] + [bits, bits + 1])
            columns.append(piece.reshape(-1, width))
            start += rows
        wide.append(jnp.concatenate(columns, 1).astype(full_type))
    return wide


def body(
    tokens,
    block_ids,
    memory_index,
    memory_keys,
    memory_values,
    attn_gain,
    query_weight,
    key_weight,
    value_weight,
    output_weight,
    position_table,
    memory_gate,
    mlp_gain,
    hidden_weight,
    return_weight,
    grad_output,
):
    share_rows = tokens.shape[0]
    seq_len = block_ids.shape[1]
    head_count, memory_rows, head_width = memory_keys.shape
    picks = memory_index.shape[2]
    inner_width = head_count * head_width
    scale = head_width ** (-0.5)

    offsets = jnp.arange(head_count, dtype=jnp.int32) * memory_rows
    index_rows = memory_index.transpose(1, 0, 2) + offsets[:, None, None]
    table = interleave(memory_keys, memory_values)

    token_full = tokens.astype(full_type)
    normed_rows = rms_scaled(token_full, attn_gain).astype(low_type)
    normed = lax.all_gather(normed_rows, "tensor", axis=0, tiled=True)
    joined = jnp.concatenate([query_weight, key_weight, value_weight], 1)
    projected = dot_rows(normed, joined).astype(low_type)
    found, late, early = gather_found(index_rows, table, projected, picks, scale)
    found = found.reshape(-1, head_width)

    query_mask, key_mask = mask_rows(block_ids)
    place = jnp.arange(ring, dtype=jnp.int32)
    place = jnp.where(place < span, place, place - ring)
    ahead = bucket_of(place - tile)
    behind = bucket_of(tile - place)
    level = jnp.arange(32, dtype=jnp.int32)
    ahead_hot = (ahead[:, None] == level).astype(full_type)
    behind_hot = (behind[:, None] == level).astype(full_type)
    scaled_table = position_table * log2_e
    ahead_columns = jnp.dot(ahead_hot, scaled_table, precision=exact_mode).T[:, None, :]
    behind_columns = jnp.dot(behind_hot, scaled_table, precision=exact_mode).T[:, None, :]
    far = jnp.stack([scaled_table[15], scaled_table[31]], 1)
    gates = jax.nn.sigmoid(memory_gate)

    mixed_rows = local_read(
        projected, query_mask, key_mask, early, late, ahead_columns, far, gates, seq_len, scale
    )
    middle = token_full + fold(
        lambda rows: dot_rows(rows, output_weight), lambda k: share_of(mixed_rows, k, share_rows)
    )
    second_rows = rms_scaled(middle, mlp_gain).astype(low_type)
    grad_full = jnp.concatenate(fetch(grad_output), 0)
    second = jnp.concatenate(fetch(second_rows), 0)
    active, slope = gelu_pair(dot_rows(second, hidden_weight))
    slope = lax.optimization_barrier(slope)
    orders = bit_orders()
    steps = len(orders[0])

    return_low = dot_outer(active, grad_full).astype(low_type)
    return_half = return_low.shape[0] // 2
    kept_back, sent_back = halve_step(
        [return_low[:return_half], return_low[return_half:]], orders[1:], 0
    )
    active_delta = dot_inner(grad_full, return_weight)
    hidden_delta = (active_delta * slope.astype(full_type)).astype(low_type)
    second_delta = fold(
        lambda rows: dot_inner(rows, hidden_weight),
        lambda k: lax.slice_in_dim(hidden_delta, k * share_rows, (k + 1) * share_rows),
    )
    hidden_half = hidden_delta.shape[1] // 2
    hidden_parts = [
        dot_outer(second, hidden_delta[:, :hidden_half]).astype(low_type),
        dot_outer(second, hidden_delta[:, hidden_half:]).astype(low_type),
    ]
    kept, sent = halve_step(hidden_parts, orders[:2], 0)

    kept_back, kept = lax.optimization_barrier((kept_back, kept))
    kept_back, sent_back = halve_step(add_low(kept_back, sent_back), orders[1:], 1)

    second_back = jax.vjp(rms_scaled, middle, mlp_gain)[1]
    middle_part, mlp_gain_part = second_back(second_delta)
    middle_delta = grad_output.astype(full_type) + middle_part
    middle_low = middle_delta.astype(low_type)
    kept, kept_back, middle_low = lax.optimization_barrier((kept, kept_back, middle_low))
    kept, sent = halve_step(add_low(kept, sent), orders[:2], 1)
    kept_back, sent_back = halve_step(add_low(kept_back, sent_back), orders[1:], 2)
    middle_full = in_order(fetch(middle_low))
    mixed_delta = dot_inner(middle_full, output_weight).astype(low_type)
    kept, kept_back, mixed_delta = lax.optimization_barrier((kept, kept_back, mixed_delta))
    kept, sent = halve_step(add_low(kept, sent), orders[:2], 2)
    kept_back, sent_back = halve_step(add_low(kept_back, sent_back), orders[1:], 3)
    kept, sent = halve_step(add_low(kept, sent), orders[:2], 3)
    taken = 3
    for step in range(4, steps):
        kept_back, sent_back = halve_step(add_low(kept_back, sent_back), orders[1:], step)
    layer_output = (
        middle
        + fold(
            lambda rows: dot_rows(rows, return_weight),
            lambda k: lax.slice_in_dim(active, k * share_rows, (k + 1) * share_rows),
        )
    ).astype(low_type)

    shards, packed = [], []
    deltas = []
    diagonals = []
    local_sums = []
    for head in range(head_count):
        deltas, diagonal_now, sums_now, kept = back_head(
            projected, query_mask, key_mask, mixed_delta, found, behind_columns, far, gates,
            seq_len, picks, scale, head, deltas, kept, packed,
        )
        diagonals.append(diagonal_now)
        local_sums.append(sums_now)
        if taken < steps - 1:
            taken += 1
            kept, sent = halve_step(add_low(kept, sent), orders[:2], taken)
        elif not shards:
            shards = add_low(kept, sent) + add_low(kept_back, sent_back)
            packed = [pack(shards)]
            kept = []
    while taken < steps - 1:
        taken += 1
        kept, sent = halve_step(add_low(kept, sent), orders[:2], taken)
    if not shards:
        shards = add_low(kept, sent) + add_low(kept_back, sent_back)
        packed = [pack(shards)]
    hidden_low_sum, hidden_high_sum, return_low_sum, return_high_sum = gather_all(
        packed[0], shards, orders[:2] + orders[1:]
    )
    hidden_sum = jnp.concatenate([hidden_low_sum, hidden_high_sum], 1)
    return_sum = jnp.concatenate([return_low_sum, return_high_sum], 0)
    diagonals = jnp.concatenate(diagonals, 0)
    local_sums = jnp.concatenate(local_sums, 0)
    recall_gain = jnp.sum(local_sums[:, 24:32, 0], 1)
    local_gain = jnp.sum(local_sums[:, 0], 1)
    gate_part = gates * (1.0 - gates) * recall_gain - gates * local_gain
    diagonal_sums = jnp.sum(diagonals, 1)
    table_part = jnp.dot(diagonal_sums, behind_hot, precision=exact_mode)
    far_left = jnp.sum(local_sums[:, 8:16], (1, 2))
    far_right = jnp.sum(local_sums[:, 16:24], (1, 2))
    table_part = table_part + far_left[:, None] * (level == 15) + far_right[:, None] * (level == 31)

    joined_parts = [dot_outer(normed, delta) for delta in deltas]
    weights = (query_weight, key_weight, value_weight)
    attn_gain_part = sum(
        jnp.sum(part * weight.astype(full_type), 1) for part, weight in zip(joined_parts, weights)
    )
    attn_gain_part = attn_gain_part / attn_gain
    model_width = tokens.shape[1]
    small = jnp.concatenate([table_part.reshape(-1), gate_part])
    small = jnp.pad(small, (0, model_width - small.shape[0]))
    extra = jnp.stack([attn_gain_part, mlp_gain_part, small], 1)
    extra = jnp.pad(extra, ((0, 0), (0, 125)))
    joined_low = jnp.concatenate([part.astype(low_type) for part in joined_parts + [extra]], 1)
    joined_half = joined_low.shape[0] // 2
    last = [
        joined_low[:joined_half],
        joined_low[joined_half:],
        dot_outer(mixed_rows, middle_full).astype(low_type),
    ]
    for step in range(steps):
        last = add_low(*halve_step(last, orders, step))
    last, (hidden_sum, return_sum) = double_all(last, (hidden_sum, return_sum))
    *joined_sum, output_sum = last

    project_delta = jnp.concatenate(deltas, 1)
    normed_delta = fold(
        lambda rows: dot_inner(rows, joined), lambda k: share_of(project_delta, k, share_rows)
    )
    first_back = jax.vjp(rms_scaled, token_full, attn_gain)[1]
    tokens_grad = (middle_delta + first_back(normed_delta)[0]).astype(low_type)

    def joined_columns(start, stop):
        return jnp.concatenate([part[:, start:stop].astype(full_type) for part in joined_sum], 0)

    last_columns = joined_columns(3 * inner_width, 3 * inner_width + 128)
    gains = sum(fetch(last_columns[:, :2].T))
    small_sum = last_columns[:, 2]
    table_size = head_count * 32
    return (
        layer_output,
        tokens_grad,
        gains[0],
        joined_columns(0, inner_width),
        joined_columns(inner_width, 2 * inner_width),
        joined_columns(2 * inner_width, 3 * inner_width),
        output_sum.astype(full_type),
        small_sum[:table_size].reshape(head_count, 32).T,
        small_sum[table_size : table_size + head_count],
        gains[1],
        hidden_sum,
        return_sum,
    )


def solution(mesh):
    def run(*arrays):
        with jax.sharding.use_abstract_mesh(mesh.abstract_mesh):
            return jax.shard_map(
                body,
                mesh=mesh,
                in_specs=(
                    P(("dp", "tensor"), None),
                    P("dp", None),
                    P("dp", "tensor", None),
                    P("tensor", None, None),
                    P("tensor", None, None),
                    P(),
                    P(None, "tensor"),
                    P(None, "tensor"),
                    P(None, "tensor"),
                    P("tensor", None),
                    P(None, "tensor"),
                    P("tensor"),
                    P(),
                    P(None, "tensor"),
                    P("tensor", None),
                    P(("dp", "tensor"), None),
                ),
                out_specs=(
                    P(("dp", "tensor"), None),
                    P(("dp", "tensor"), None),
                    P(),
                    P(None, "tensor"),
                    P(None, "tensor"),
                    P(None, "tensor"),
                    P("tensor", None),
                    P(None, "tensor"),
                    P("tensor"),
                    P(),
                    P(None, "tensor"),
                    P("tensor", None),
                ),
                check_vma=False,
            )(*arrays)

    return run
```

```python
import functools
import math

import jax
import jax.numpy as jnp
from jax import lax
from jax.experimental import pallas as pl
from jax.experimental.pallas import tpu as pltpu
from jax.sharding import PartitionSpec as P

eps_norm = 1e-06
far_steps = (12, 16, 23, 32, 46, 64, 91)
exact_mode = lax.Precision.HIGHEST
low_type = jnp.bfloat16
full_type = jnp.float32
log2_e = math.log2(math.e)
tile = 256
span = 3 * tile
ring = 1024
mask_gap = -(2.0**100)
vmem_most = 60 * 2**20


def bucket_of(relative):
    upper_half = jnp.where(relative > 0, 16, 0).astype(jnp.int32)
    distance = jnp.abs(relative)
    far_bucket = 8 + sum(((distance >= step_size).astype(jnp.int32) for step_size in far_steps))
    return upper_half + jnp.where(distance < 8, distance, far_bucket)


def rms_scaled(rows, gain):
    return rows * lax.rsqrt(jnp.mean(rows * rows, -1, keepdims=True) + eps_norm) * gain


def gelu_pair(rows):
    reach = math.sqrt(2.0 / math.pi)
    square = rows * rows
    turn = jnp.tanh(reach * rows * (1.0 + 0.044715 * square))
    share = 0.5 * (1.0 + turn)
    steep = 0.5 * (1.0 - turn * turn) * reach * (1.0 + 3.0 * 0.044715 * square)
    return (rows * share).astype(low_type), (share + rows * steep).astype(low_type)


def dot_rows(left, right):
    return jnp.dot(left, right, preferred_element_type=full_type)


def dot_outer(left, right):
    return lax.dot_general(
        left, right, (((0,), (0,)), ((), ())), preferred_element_type=full_type
    )


def dot_inner(left, right):
    return lax.dot_general(
        left, right, (((1,), (1,)), ((), ())), preferred_element_type=full_type
    )


def interleave_kernel(key_ref, value_ref, table_ref):
    rows = key_ref.shape[1]
    row = lax.broadcasted_iota(jnp.int32, (256, 256), 0)
    column = lax.broadcasted_iota(jnp.int32, (256, 256), 1)
    order = jnp.where(column == (row // 2 + (row % 2) * 128), 1.0, 0.0).astype(low_type)
    for part in range(rows // 256):
        low, high = pl.ds(part * 256, 128), pl.ds(part * 256 + 128, 128)
        both = jnp.concatenate(
            [
                jnp.concatenate([key_ref[0, low], key_ref[0, high]], 1),
                jnp.concatenate([value_ref[0, low], value_ref[0, high]], 1),
            ],
            0,
        )
        mixed = dot_rows(order, both).astype(low_type)
        table_ref[pl.ds(part * 512, 256), :] = mixed[:, :128]
        table_ref[pl.ds(part * 512 + 256, 256), :] = mixed[:, 128:]


def interleave(memory_keys, memory_values):
    heads, rows, width = memory_keys.shape
    step = min(8192, rows)
    spec = pl.BlockSpec((1, step, width), lambda h, i: (h, i, 0))
    return pl.pallas_call(
        interleave_kernel,
        grid=(heads, rows // step),
        in_specs=[spec, spec],
        out_specs=pl.BlockSpec((2 * step, width), lambda h, i: (h * (rows // step) + i, 0)),
        out_shape=jax.ShapeDtypeStruct((heads * rows * 2, width), low_type),
        compiler_params=pltpu.CompilerParams(vmem_limit_bytes=vmem_most),
        cost_estimate=pl.CostEstimate(
            flops=heads * rows * 4 * 256 * width,
            bytes_accessed=heads * rows * width * 8,
            transcendentals=0,
        ),
        name="interleave",
    )(memory_keys, memory_values).reshape(heads, rows, 2, width)


def own_columns(picks):
    shape = (8, 8 * picks * 2)
    lane = lax.broadcasted_iota(jnp.int32, shape, 1)
    row = lax.broadcasted_iota(jnp.int32, shape, 0)
    return jnp.logical_and(lane // (2 * picks) == row, lane % 2 == 0)


def copy_rows(picked, first, table_ref, found_ref, start, count):
    for at in range(0, count, 8):
        rows_now = [
            table_ref[picked[(first + at + j) // 128, (first + at + j) % 128]] for j in range(8)
        ]
        for j in range(8):
            found_ref[start + at + j] = rows_now[j]
        yield


def recall_rows(picks, scale, own, query_ref, query_at, rows_ref, read_ref, read_at, tokens):
    wide = 8 * picks * 2
    groups = range(tokens // 8)
    scores = []
    for g in groups:
        rows = rows_ref[pl.ds(g * wide, wide), :]
        scores.append(dot_inner(query_ref[pl.ds(query_at + g * 8, 8), :], rows))
        yield
    shifted = []
    totals = []
    for g in groups:
        masked = jnp.where(own, scores[g] * (scale * log2_e), -jnp.inf)
        exponent = jnp.exp2(masked - jnp.max(masked, 1, keepdims=True))
        totals.append(jnp.sum(exponent, 1, keepdims=True))
        shifted.append(pltpu.roll(exponent, 1, 1).astype(low_type))
        yield
    for g in groups:
        rows = rows_ref[pl.ds(g * wide, wide), :]
        read_ref[pl.ds(read_at + g * 8, 8), :] = dot_rows(shifted[g], rows) / totals[g]
        yield


def weave(many, many_count, few, few_count):
    done = 0
    for number in range(few_count):
        until = (number + 1) * many_count // few_count
        while done < until:
            next(many)
            done += 1
        next(few)


def gather_kernel(
    picks, scale, index_hbm, table_hbm, now_ref, before_ref, found_ref, late_ref, early_ref,
    table_ref, table_sems, index_a, index_b, index_sems, stage_ref, stage_sems,
):
    step = pl.program_id(0)
    steps = pl.num_programs(0) - 1
    heads = table_sems.shape[0]
    blocks = steps // heads
    chunk = found_ref.shape[0] // 2
    rows = table_ref.shape[0] // heads
    slots = (index_a, index_b)
    part = chunk // 2
    tokens = part // picks
    own = own_columns(picks)
    flat = found_ref.reshape(4 * chunk, 128)

    def index_copy(number, slot):
        return pltpu.make_async_copy(index_hbm.at[number], slots[slot], index_sems.at[slot])

    def table_copy(number):
        where = pl.ds(number * rows, rows)
        return pltpu.make_async_copy(
            table_hbm.at[where], table_ref.at[where], table_sems.at[number]
        )

    def stage_copy(number):
        return pltpu.make_async_copy(
            flat.at[pl.ds(number * 2 * part, 2 * part)], stage_ref.at[number], stage_sems.at[number]
        )

    def reads(number, query_ref, read_ref):
        return recall_rows(
            picks, scale, own, query_ref, (number % 2) * tokens, stage_ref.at[number], read_ref,
            (number % 2) * tokens, tokens,
        )

    @pl.when(step == 0)
    def start_all():
        index_copy(0, 0).start()
        index_copy(1, 1).start()
        for number in range(heads):
            table_copy(number).start()
        stage_copy(2).start()
        stage_copy(3).start()

    @pl.when(jnp.logical_and(step < steps, step % blocks == 0))
    def wait_table():
        table_copy(step // blocks).wait()

    @pl.when(step < steps)
    def work():
        following = jnp.minimum(step + 1, steps - 1)
        for number in range(4):
            slot = number // 2
            if number % 2 == 0:
                index_copy(2 * step + slot, slot).wait()
            finished = (number + 2) % 4
            stage_copy(finished).wait()
            copied = copy_rows(
                slots[slot], (number % 2) * part, table_ref, found_ref, number * part, part
            )
            if number < 2:
                read = reads(finished, before_ref, late_ref)
            else:
                read = reads(finished, now_ref, early_ref)
            weave(copied, part // 8, read, 3 * (tokens // 8))
            stage_copy(number).start()
            if number % 2 == 1:
                index_copy(2 * following + slot, slot).start()

    @pl.when(step == steps)
    def finish():
        for number in (2, 3):
            stage_copy(number).wait()
            for unused in reads(number, before_ref, late_ref):
                pass
        for slot in range(2):
            index_copy(2 * (steps - 1) + slot, slot).wait()


def gather_found(index_rows, table, queries, picks, scale):
    heads, rows, unused, width = table.shape
    tokens = queries.shape[0]
    half = 256
    blocks = tokens // (2 * half)
    steps = heads * blocks
    chunk = half * picks

    def query_spec(shift):
        def place(t):
            at = jnp.clip(t - shift, 0, steps - 1)
            return (2 * (at % blocks) + shift, at // blocks)

        return pl.BlockSpec((half, width), place)

    return pl.pallas_call(
        functools.partial(gather_kernel, picks, scale),
        grid=(steps + 1,),
        in_specs=[
            pl.BlockSpec(memory_space=pl.ANY),
            pl.BlockSpec(memory_space=pl.ANY),
            query_spec(0),
            query_spec(1),
        ],
        out_specs=[
            pl.BlockSpec((2 * chunk, 2, width), lambda t: (jnp.minimum(t, steps - 1), 0, 0)),
            pl.BlockSpec((half, width), lambda t: (jnp.maximum(t - 1, 0), 0)),
            pl.BlockSpec((half, width), lambda t: (jnp.minimum(t, steps - 1), 0)),
        ],
        out_shape=[
            jax.ShapeDtypeStruct((heads * tokens * picks, 2, width), low_type),
            jax.ShapeDtypeStruct((heads * tokens // 2, width), full_type),
            jax.ShapeDtypeStruct((heads * tokens // 2, width), full_type),
        ],
        scratch_shapes=[
            pltpu.VMEM((heads * rows, 2, width), low_type),
            pltpu.SemaphoreType.DMA((heads,)),
            pltpu.SMEM((chunk // 128, 128), jnp.int32),
            pltpu.SMEM((chunk // 128, 128), jnp.int32),
            pltpu.SemaphoreType.DMA((2,)),
            pltpu.VMEM((4, chunk, width), low_type),
            pltpu.SemaphoreType.DMA((4,)),
        ],
        compiler_params=pltpu.CompilerParams(vmem_limit_bytes=vmem_most),
        cost_estimate=pl.CostEstimate(
            flops=0, bytes_accessed=4 * heads * tokens * picks * width * 4, transcendentals=0
        ),
        name="gather_found",
    )(
        index_rows.reshape(-1, chunk // 128, 128), table.reshape(heads * rows, 2, width), queries,
        queries,
    )


def band(column_ref):
    wide = jnp.broadcast_to(column_ref[0], (tile, ring))
    return pltpu.roll(wide, 0, 1, stride=1, stride_axis=0)[:, :span]


def local_kernel(
    scale, gate_ref, far_ref, column_ref, query_ref, key_ref, value_ref, query_mask_ref,
    key_mask_ref, early_ref, late_ref, mixed_ref, bias_ref,
):
    head = pl.program_id(0)

    @pl.when(pl.program_id(1) == 0)
    def make_band():
        bias_ref[...] = band(column_ref)

    gate = gate_ref[head]
    count = query_ref.shape[0] // tile
    at = [pl.ds(t * tile, tile) for t in range(count)]
    keys = [jnp.concatenate([key_ref[a, :], key_mask_ref[0, a, :]], 1) for a in at]
    for t in range(count):
        rows = jnp.concatenate([query_ref[at[t], :], query_mask_ref[0, at[t], :]], 1)
        parts = []
        for j in range(count):
            step = j - t
            if step < -1:
                bias = far_ref[head, 0]
            elif step > 1:
                bias = far_ref[head, 1]
            else:
                bias = bias_ref[:, pl.ds((step + 1) * tile, tile)]
            parts.append(dot_inner(rows, keys[j]) * (scale * log2_e) + bias)
        top = jnp.max(functools.reduce(jnp.maximum, parts), 1, keepdims=True)
        parts = [jnp.exp2(part - top) for part in parts]
        total = jnp.sum(functools.reduce(jnp.add, parts), 1, keepdims=True)
        read = sum(dot_rows(parts[j].astype(low_type), value_ref[at[j], :]) for j in range(count))
        recalled = (early_ref, late_ref)[t % 2][pl.ds((t // 2) * tile, tile), :]
        mixed_ref[at[t], :] = (gate * recalled + ((1.0 - gate) / total) * read).astype(low_type)


def local_read(projected, query_mask, key_mask, early, late, columns, far, gates, seq_len, scale):
    tokens, width = projected.shape
    heads = gates.shape[0]
    width = width // (3 * heads)
    sequences = tokens // seq_len
    half_spec = pl.BlockSpec((seq_len // 2, width), lambda h, s: (h * sequences + s, 0))

    def rows_of(shift):
        return pl.BlockSpec((seq_len, width), lambda h, s: (s, h + shift * heads))

    mask_spec = pl.BlockSpec((1, seq_len, 128), lambda h, s: (s, 0, 0))
    smem = pl.BlockSpec(memory_space=pltpu.SMEM)
    return pl.pallas_call(
        functools.partial(local_kernel, scale),
        grid=(heads, tokens // seq_len),
        in_specs=[
            smem,
            smem,
            pl.BlockSpec((1, 1, ring), lambda h, s: (h, 0, 0)),
            rows_of(0),
            rows_of(1),
            rows_of(2),
            mask_spec,
            mask_spec,
            half_spec,
            half_spec,
        ],
        out_specs=rows_of(0),
        out_shape=jax.ShapeDtypeStruct((tokens, heads * width), low_type),
        scratch_shapes=[pltpu.VMEM((tile, span), full_type)],
        compiler_params=pltpu.CompilerParams(vmem_limit_bytes=vmem_most),
        cost_estimate=pl.CostEstimate(
            flops=0, bytes_accessed=heads * tokens * seq_len * 20, transcendentals=0
        ),
        name="local_read",
    )(gates, far, columns, projected, projected, projected, query_mask, key_mask, early, late)


def recall_back_rows(
    picks, scale, own, gate, query_ref, delta_ref, at, rows_ref, read_ref, gains, tokens
):
    wide = 8 * picks * 2
    flight = 8
    groups = tokens // 8
    both = {}
    for first in range(-flight, groups, flight):
        for g in range(first + flight, min(first + 2 * flight, groups)):
            where = pl.ds(at + g * 8, 8)
            pair = jnp.concatenate([query_ref[where, :], delta_ref[where, :]], 0)
            both[g] = dot_inner(pair, rows_ref[pl.ds(g * wide, wide), :])
            yield
        for g in range(max(first, 0), first + flight if first >= 0 else 0):
            pair = both.pop(g)
            masked = jnp.where(own, pair[:8] * (scale * log2_e), -jnp.inf)
            exponent = jnp.exp2(masked - jnp.max(masked, 1, keepdims=True))
            weights = exponent / jnp.sum(exponent, 1, keepdims=True)
            reads = pltpu.roll(pair[8:], wide - 1, 1)
            expected = jnp.sum(weights * reads, 1, keepdims=True)
            gains.append(expected)
            score_delta = (weights * (reads - expected)).astype(low_type)
            rows = rows_ref[pl.ds(g * wide, wide), :]
            read_ref[pl.ds(g * 8, 8), :] = dot_rows(score_delta, rows) * (scale * gate)
            yield


def local_back_tile(
    t, scale, gate, far, query_ref, keys, turned, value_ref, query_mask_ref, delta_ref,
    bias_ref, near_ref, key_sum_ref, value_sum_ref, gains, far_sums, result,
):
    count = len(keys)
    at = [pl.ds(j * tile, tile) for j in range(count)]
    rows = jnp.concatenate([query_ref[at[t], :], query_mask_ref[0, at[t], :]], 1)
    delta = ((1.0 - gate) * delta_ref[at[t], :].astype(full_type)).astype(low_type)
    parts = []
    for j in range(count):
        step = j - t
        if step < -1:
            bias = far[0]
        elif step > 1:
            bias = far[1]
        else:
            bias = bias_ref[:, pl.ds((1 - step) * tile, tile)]
        parts.append(dot_inner(keys[j], rows) * (scale * log2_e) + bias)
        yield
    top = jnp.max(functools.reduce(jnp.maximum, parts), 0, keepdims=True)
    yield
    for j in range(count):
        parts[j] = jnp.exp2(parts[j] - top)
        yield
    inverse = 1.0 / jnp.sum(functools.reduce(jnp.add, parts), 0, keepdims=True)
    moves = []
    products = []
    for j in range(count):
        parts[j] = parts[j] * inverse
        moves.append(dot_inner(value_ref[at[j], :], delta))
        products.append(parts[j] * moves[j])
        yield
    expected = jnp.sum(functools.reduce(jnp.add, products), 0, keepdims=True)
    gains.append(expected)
    query_sum = None
    for j in range(count):
        step = j - t
        score_delta = parts[j] * (moves[j] - expected)
        if abs(step) > 1:
            side = 0 if step < 0 else 1
            far_sums[side].append(jnp.sum(score_delta.reshape(tile // 8, 8, tile), 0))
        else:
            near_ref[:, pl.ds((1 - step) * tile, tile)] += score_delta
        yield
        low_delta = score_delta.astype(low_type)
        value_part = dot_rows(parts[j].astype(low_type), delta)
        yield
        key_part = dot_rows(low_delta, query_ref[at[t], :])
        yield
        query_part = dot_rows(turned[j], low_delta)
        if t == 0:
            value_sum_ref[at[j], :] = value_part
            key_sum_ref[at[j], :] = key_part
        else:
            value_sum_ref[at[j], :] += value_part
            key_sum_ref[at[j], :] += key_part
        query_sum = query_part if j == 0 else query_sum + query_part
        yield
    result.append(query_sum.T * scale)
    yield


def run_together(first, second):
    first, second = list_steps(first), list_steps(second)
    first_total, second_total = next(first), next(second)
    done = 0
    for number in range(second_total):
        until = (number + 1) * first_total // second_total
        while done < until:
            next(first)
            done += 1
        next(second)


def list_steps(counted):
    count, steps = counted
    yield count
    yield from steps


def back_kernel(
    picks, scale, head, gate_ref, far_ref, column_ref, query_ref, key_ref, value_ref,
    query_mask_ref, key_mask_ref, delta_ref, found_hbm, query_delta_ref, key_delta_ref,
    value_delta_ref, diagonal_ref, sums_ref, bias_ref, near_ref, key_sum_ref, value_sum_ref,
    read_ref, rows_ref, rows_sems,
):
    place = pl.program_id(0)
    sequence = pl.program_id(1)
    sequences = pl.num_programs(1)
    total_tiles = pl.num_programs(0) * sequences * (query_ref.shape[0] // tile)
    count = query_ref.shape[0] // tile
    block = rows_ref.shape[1]
    own = own_columns(picks)
    gate = gate_ref[place]
    far_left, far_right = far_ref[place, 0], far_ref[place, 1]

    def rows_copy(number, slot):
        start = (head * sequences * count + number) * block
        return pltpu.make_async_copy(
            found_hbm.at[pl.ds(pl.multiple_of(start, block), block)],
            rows_ref.at[slot],
            rows_sems.at[slot],
        )

    @pl.when(jnp.logical_and(place == 0, sequence == 0))
    def begin():
        for slot in range(2):
            rows_copy(slot, slot).start()

    @pl.when(sequence == 0)
    def begin_head():
        bias_ref[...] = band(column_ref)
        near_ref[...] = jnp.zeros(near_ref.shape, full_type)
        sums_ref[...] = jnp.zeros(sums_ref.shape, full_type)

    at = [pl.ds(t * tile, tile) for t in range(count)]
    keys = [jnp.concatenate([key_ref[a, :], key_mask_ref[0, a, :]], 1) for a in at]
    turned = [key_ref[a, :].astype(full_type).T.astype(low_type) for a in at]
    gains, recall_gains, far_sums = [], [], [[], []]
    for t in range(count):
        slot = t % 2
        number = (place * sequences + sequence) * count + t
        rows_copy(number, slot).wait()
        result = []
        run_together(
            (
                2 * (tile // 8),
                recall_back_rows(
                    picks, scale, own, gate, query_ref, delta_ref, t * tile, rows_ref.at[slot],
                    read_ref, recall_gains, tile,
                ),
            ),
            (
                7 * count + 2,
                local_back_tile(
                    t, scale, gate, (far_left, far_right), query_ref, keys, turned, value_ref, query_mask_ref,
                    delta_ref, bias_ref, near_ref, key_sum_ref, value_sum_ref, gains, far_sums,
                    result,
                ),
            ),
        )
        query_delta_ref[at[t], :] = (result[0] + read_ref[...]).astype(low_type)

        @pl.when(number + 2 < total_tiles)
        def ahead():
            rows_copy(number + 2, slot).start()

    key_delta_ref[...] = (key_sum_ref[...] * scale).astype(low_type)
    value_delta_ref[...] = value_sum_ref[...].astype(low_type)
    sums_ref[0, 0:1] += functools.reduce(jnp.add, gains)
    for side in range(2):
        if far_sums[side]:
            sums_ref[0, 8 + 8 * side : 16 + 8 * side] += functools.reduce(jnp.add, far_sums[side])
    sums_ref[0, 24:32] += jnp.broadcast_to(functools.reduce(jnp.add, recall_gains), (8, tile))

    @pl.when(sequence == sequences - 1)
    def fold_diagonals():
        total = jnp.zeros((8, ring), full_type)
        for g in range(tile // 8):
            part = jnp.concatenate(
                [near_ref[pl.ds(g * 8, 8), :], jnp.zeros((8, ring - span), full_type)], 1
            )
            total = total + (pltpu.roll(part, ring - 8 * g, 1) if g else part)
        row = lax.broadcasted_iota(jnp.int32, (8, ring), 0)
        for bit in (1, 2, 4):
            total = jnp.where((row & bit) != 0, pltpu.roll(total, ring - bit, 1), total)
        diagonal_ref[0] = total


def back_heads(
    projected, query_mask, key_mask, mixed_delta, found, columns, far, gates, seq_len, picks, scale,
    heads_now, kept, carried, after,
):
    tokens = mixed_delta.shape[0]
    heads = gates.shape[0]
    width = mixed_delta.shape[1] // heads
    anywhere = pl.BlockSpec(memory_space=pl.ANY)
    head, number = heads_now
    chosen = slice(head, head + number)
    extra = len(kept) + len(carried) + len(after)

    def rows_of(shift):
        return pl.BlockSpec((seq_len, width), lambda h, s: (s, h + head + shift * heads))

    def kernel(*refs):
        outs = refs[10 + extra :]
        back_kernel(picks, scale, head, *refs[:10], *outs[:5], *outs[5 + len(carried) :])

    mask_spec = pl.BlockSpec((1, seq_len, 128), lambda h, s: (s, 0, 0))
    smem = pl.BlockSpec(memory_space=pltpu.SMEM)
    rows_shape = jax.ShapeDtypeStruct((tokens, heads * width), low_type)
    first = 10 + len(kept)
    out = pl.pallas_call(
        kernel,
        grid=(number, tokens // seq_len),
        in_specs=[
            smem,
            smem,
            pl.BlockSpec((1, 1, ring), lambda h, s: (h, 0, 0)),
            rows_of(0),
            rows_of(1),
            rows_of(2),
            mask_spec,
            mask_spec,
            rows_of(0),
            anywhere,
        ]
        + [anywhere] * extra,
        out_specs=[
            rows_of(0),
            rows_of(0),
            rows_of(0),
            pl.BlockSpec((1, 8, ring), lambda h, s: (h, 0, 0)),
            pl.BlockSpec((1, 32, tile), lambda h, s: (h, 0, 0)),
        ]
        + [anywhere] * len(carried),
        out_shape=[
            rows_shape,
            rows_shape,
            rows_shape,
            jax.ShapeDtypeStruct((number, 8, ring), full_type),
            jax.ShapeDtypeStruct((number, 32, tile), full_type),
        ]
        + [jax.ShapeDtypeStruct(part.shape, part.dtype) for part in carried],
        input_output_aliases={10 + i: i for i in range(len(kept))}
        | {first + i: 5 + i for i in range(len(carried))},
        scratch_shapes=[
            pltpu.VMEM((tile, span), full_type),
            pltpu.VMEM((tile, span), full_type),
            pltpu.VMEM((seq_len, width), full_type),
            pltpu.VMEM((seq_len, width), full_type),
            pltpu.VMEM((tile, width), full_type),
            pltpu.VMEM((2, tile * picks * 2, width), low_type),
            pltpu.SemaphoreType.DMA((2,)),
        ],
        compiler_params=pltpu.CompilerParams(vmem_limit_bytes=vmem_most),
        cost_estimate=pl.CostEstimate(
            flops=0, bytes_accessed=number * tokens * picks * width * 8, transcendentals=0
        ),
        name="back_heads",
    )(
        gates[chosen], far[chosen], columns[chosen], projected, projected, projected, query_mask,
        key_mask, mixed_delta, found, *kept, *carried, *after,
    )
    return list(out[:3]), out[3], out[4], list(out[5:])


def mask_rows(block_ids):
    level = jnp.arange(128, dtype=jnp.int32)
    gap = block_ids[:, :, None] - level
    query_mask = jnp.where((gap >= 0) & (gap <= 1), 0.0, mask_gap).astype(low_type)
    key_mask = (gap == 0).astype(low_type)
    return query_mask, key_mask


def fetch(rows):
    group = lax.axis_size("tensor")
    return [rows] + [
        lax.ppermute(rows, "tensor", [((i + k) % group, i) for i in range(group)])
        for k in range(1, group)
    ]


def in_order(shares):
    group = lax.axis_size("tensor")
    rows = shares[0].shape[0]
    whole = jnp.zeros((group * rows,) + shares[0].shape[1:], shares[0].dtype)
    for k in range(group):
        start = ((lax.axis_index("tensor") + k) % group) * rows
        whole = lax.dynamic_update_slice_in_dim(whole, shares[k], start, 0)
    return whole


def share_of(whole, k, rows):
    start = ((lax.axis_index("tensor") + k) % lax.axis_size("tensor")) * rows
    return lax.dynamic_slice_in_dim(whole, start, rows, 0)


def fold(term, piece):
    group = lax.axis_size("tensor")
    sent = [
        lax.ppermute(
            term(piece(k)).astype(low_type), "tensor", [(i, (i + k) % group) for i in range(group)]
        )
        for k in range(1, group)
    ]
    return sum((part.astype(full_type) for part in sent), term(piece(0)))


def bit_orders():
    bits = lax.axis_size("dp").bit_length() - 1
    near = [(0, 1, 2), (1, 2, 0), (2, 0, 1)]
    return [list(head) + list(range(3, bits)) for head in near]


def swap_over(rows, bit):
    return lax.ppermute(rows, "dp", [(i, i ^ (1 << bit)) for i in range(lax.axis_size("dp"))])


def side_of(bit):
    return (lax.axis_index("dp") >> bit) & 1


def halve_step(parts, orders, step):
    kept, sent = [], []
    for part, order in zip(parts, orders):
        half = part.shape[0] // 2
        side = side_of(order[step])
        sent.append(
            swap_over(
                lax.dynamic_slice_in_dim(part, (1 - side) * half, half, 0), order[step]
            )
        )
        kept.append(lax.dynamic_slice_in_dim(part, side * half, half, 0))
    return kept, sent


def add_low(kept, sent):
    return [
        (a.astype(full_type) + b.astype(full_type)).astype(low_type) for a, b in zip(kept, sent)
    ]


def double_all(parts, beside):
    orders = bit_orders()
    for step in reversed(range(len(orders[0]))):
        got = [swap_over(part, order[step]) for part, order in zip(parts, orders)]
        if step == 1:
            got, beside = lax.optimization_barrier((got, beside))
        wider = []
        for part, other, order in zip(parts, got, orders):
            rows = part.shape[0]
            side = side_of(order[step])
            whole = jnp.zeros((2 * rows,) + part.shape[1:], part.dtype)
            whole = lax.dynamic_update_slice_in_dim(whole, part, side * rows, 0)
            wider.append(lax.dynamic_update_slice_in_dim(whole, other, (1 - side) * rows, 0))
        parts = wider
    return parts, beside


def pack(parts):
    width = min(part.shape[1] for part in parts)
    return jnp.concatenate(
        [
            part[:, start : start + width]
            for part in parts
            for start in range(0, part.shape[1], width)
        ],
        0,
    )


def gather_all(packed, parts, orders):
    whole = lax.all_gather(packed, "dp", axis=0)
    width = packed.shape[1]
    wide = []
    start = 0
    for part, order in zip(parts, orders):
        bits = len(order)
        rows = part.shape[0]
        columns = []
        for unused in range(part.shape[1] // width):
            piece = whole[:, start : start + rows].reshape((2,) * bits + (rows, width))
            piece = piece.transpose([bits - 1 - bit for bit in order] + [bits, bits + 1])
            columns.append(piece.reshape(-1, width))
            start += rows
        wide.append(jnp.concatenate(columns, 1).astype(full_type))
    return wide


def body(
    tokens,
    block_ids,
    memory_index,
    memory_keys,
    memory_values,
    attn_gain,
    query_weight,
    key_weight,
    value_weight,
    output_weight,
    position_table,
    memory_gate,
    mlp_gain,
    hidden_weight,
    return_weight,
    grad_output,
):
    share_rows = tokens.shape[0]
    seq_len = block_ids.shape[1]
    head_count, memory_rows, head_width = memory_keys.shape
    picks = memory_index.shape[2]
    inner_width = head_count * head_width
    scale = head_width ** (-0.5)

    offsets = jnp.arange(head_count, dtype=jnp.int32) * memory_rows
    index_rows = memory_index.transpose(1, 0, 2) + offsets[:, None, None]
    table = interleave(memory_keys, memory_values)

    token_full = tokens.astype(full_type)
    normed_rows = rms_scaled(token_full, attn_gain).astype(low_type)
    normed = lax.all_gather(normed_rows, "tensor", axis=0, tiled=True)
    joined = jnp.concatenate([query_weight, key_weight, value_weight], 1)
    projected = dot_rows(normed, joined).astype(low_type)
    found, late, early = gather_found(index_rows, table, projected, picks, scale)
    found = found.reshape(-1, head_width)

    query_mask, key_mask = mask_rows(block_ids)
    place = jnp.arange(ring, dtype=jnp.int32)
    place = jnp.where(place < span, place, place - ring)
    ahead = bucket_of(place - tile)
    behind = bucket_of(tile - place)
    level = jnp.arange(32, dtype=jnp.int32)
    ahead_hot = (ahead[:, None] == level).astype(full_type)
    behind_hot = (behind[:, None] == level).astype(full_type)
    scaled_table = position_table * log2_e
    ahead_columns = jnp.dot(ahead_hot, scaled_table, precision=exact_mode).T[:, None, :]
    behind_columns = jnp.dot(behind_hot, scaled_table, precision=exact_mode).T[:, None, :]
    far = jnp.stack([scaled_table[15], scaled_table[31]], 1)
    gates = jax.nn.sigmoid(memory_gate)

    mixed_rows = local_read(
        projected, query_mask, key_mask, early, late, ahead_columns, far, gates, seq_len, scale
    )
    middle = token_full + fold(
        lambda rows: dot_rows(rows, output_weight), lambda k: share_of(mixed_rows, k, share_rows)
    )
    second_rows = rms_scaled(middle, mlp_gain).astype(low_type)
    grad_full = jnp.concatenate(fetch(grad_output), 0)
    second = jnp.concatenate(fetch(second_rows), 0)
    active, slope = gelu_pair(dot_rows(second, hidden_weight))
    slope = lax.optimization_barrier(slope)
    orders = bit_orders()
    steps = len(orders[0])

    return_low = dot_outer(active, grad_full).astype(low_type)
    return_half = return_low.shape[0] // 2
    kept_back, sent_back = halve_step(
        [return_low[:return_half], return_low[return_half:]], orders[1:], 0
    )
    active_delta = dot_inner(grad_full, return_weight)
    hidden_delta = (active_delta * slope.astype(full_type)).astype(low_type)
    second_delta = fold(
        lambda rows: dot_inner(rows, hidden_weight),
        lambda k: lax.slice_in_dim(hidden_delta, k * share_rows, (k + 1) * share_rows),
    )
    hidden_half = hidden_delta.shape[1] // 2
    hidden_parts = [
        dot_outer(second, hidden_delta[:, :hidden_half]).astype(low_type),
        dot_outer(second, hidden_delta[:, hidden_half:]).astype(low_type),
    ]
    kept, sent = halve_step(hidden_parts, orders[:2], 0)

    kept_back, kept = lax.optimization_barrier((kept_back, kept))
    kept_back, sent_back = halve_step(add_low(kept_back, sent_back), orders[1:], 1)

    second_back = jax.vjp(rms_scaled, middle, mlp_gain)[1]
    middle_part, mlp_gain_part = second_back(second_delta)
    middle_delta = grad_output.astype(full_type) + middle_part
    middle_low = middle_delta.astype(low_type)
    kept, kept_back, middle_low = lax.optimization_barrier((kept, kept_back, middle_low))
    kept, sent = halve_step(add_low(kept, sent), orders[:2], 1)
    kept_back, sent_back = halve_step(add_low(kept_back, sent_back), orders[1:], 2)
    middle_full = in_order(fetch(middle_low))
    mixed_delta = dot_inner(middle_full, output_weight).astype(low_type)
    kept, kept_back, mixed_delta = lax.optimization_barrier((kept, kept_back, mixed_delta))
    kept, sent = halve_step(add_low(kept, sent), orders[:2], 2)
    kept_back, sent_back = halve_step(add_low(kept_back, sent_back), orders[1:], 3)
    taken = 2
    for step in range(4, steps):
        kept_back, sent_back = halve_step(add_low(kept_back, sent_back), orders[1:], step)
    layer_output = (
        middle
        + fold(
            lambda rows: dot_rows(rows, return_weight),
            lambda k: lax.slice_in_dim(active, k * share_rows, (k + 1) * share_rows),
        )
    ).astype(low_type)

    shards, packed = [], []
    deltas = []
    diagonals = []
    local_sums = []
    heads_in_turn = [(0, 1)]
    if head_count > 1:
        heads_in_turn.append((1, 1))
    if head_count > 2:
        heads_in_turn.append((2, head_count - 2))
    for heads_now in heads_in_turn:
        deltas, diagonal_now, sums_now, kept = back_heads(
            projected, query_mask, key_mask, mixed_delta, found, behind_columns, far, gates,
            seq_len, picks, scale, heads_now, deltas, kept, packed,
        )
        diagonals.append(diagonal_now)
        local_sums.append(sums_now)
        if taken < steps - 1:
            taken += 1
            kept, sent = halve_step(add_low(kept, sent), orders[:2], taken)
        elif not shards:
            shards = add_low(kept, sent) + add_low(kept_back, sent_back)
            packed = [pack(shards)]
            kept = []
    while taken < steps - 1:
        taken += 1
        kept, sent = halve_step(add_low(kept, sent), orders[:2], taken)
    if not shards:
        shards = add_low(kept, sent) + add_low(kept_back, sent_back)
        packed = [pack(shards)]
    hidden_low_sum, hidden_high_sum, return_low_sum, return_high_sum = gather_all(
        packed[0], shards, orders[:2] + orders[1:]
    )
    hidden_sum = jnp.concatenate([hidden_low_sum, hidden_high_sum], 1)
    return_sum = jnp.concatenate([return_low_sum, return_high_sum], 0)
    query_delta, key_delta, value_delta = deltas
    diagonals = jnp.concatenate(diagonals, 0)
    local_sums = jnp.concatenate(local_sums, 0)
    recall_gain = jnp.sum(local_sums[:, 24:32, 0], 1)
    local_gain = jnp.sum(local_sums[:, 0], 1)
    gate_part = gates * (1.0 - gates) * recall_gain - gates * local_gain
    diagonal_sums = jnp.sum(diagonals, 1)
    table_part = jnp.dot(diagonal_sums, behind_hot, precision=exact_mode)
    far_left = jnp.sum(local_sums[:, 8:16], (1, 2))
    far_right = jnp.sum(local_sums[:, 16:24], (1, 2))
    table_part = table_part + far_left[:, None] * (level == 15) + far_right[:, None] * (level == 31)

    project_delta = jnp.concatenate([query_delta, key_delta, value_delta], 1)
    joined_part = dot_outer(normed, project_delta)
    attn_gain_part = jnp.sum(joined_part * joined.astype(full_type), 1) / attn_gain
    model_width = tokens.shape[1]
    small = jnp.concatenate([table_part.reshape(-1), gate_part])
    small = jnp.pad(small, (0, model_width - small.shape[0]))
    extra = jnp.stack([attn_gain_part, mlp_gain_part, small], 1)
    extra = jnp.pad(extra, ((0, 0), (0, 125)))
    joined_low = jnp.concatenate([joined_part, extra], 1).astype(low_type)
    joined_half = joined_low.shape[0] // 2
    last = [
        joined_low[:joined_half],
        joined_low[joined_half:],
        dot_outer(mixed_rows, middle_full).astype(low_type),
    ]
    for step in range(steps):
        last = add_low(*halve_step(last, orders, step))
    last, (hidden_sum, return_sum) = double_all(last, (hidden_sum, return_sum))
    *joined_sum, output_sum = last

    normed_delta = fold(
        lambda rows: dot_inner(rows, joined), lambda k: share_of(project_delta, k, share_rows)
    )
    first_back = jax.vjp(rms_scaled, token_full, attn_gain)[1]
    tokens_grad = (middle_delta + first_back(normed_delta)[0]).astype(low_type)

    def joined_columns(start, stop):
        return jnp.concatenate([part[:, start:stop].astype(full_type) for part in joined_sum], 0)

    last_columns = joined_columns(3 * inner_width, 3 * inner_width + 128)
    gains = sum(fetch(last_columns[:, :2].T))
    small_sum = last_columns[:, 2]
    table_size = head_count * 32
    return (
        layer_output,
        tokens_grad,
        gains[0],
        joined_columns(0, inner_width),
        joined_columns(inner_width, 2 * inner_width),
        joined_columns(2 * inner_width, 3 * inner_width),
        output_sum.astype(full_type),
        small_sum[:table_size].reshape(head_count, 32).T,
        small_sum[table_size : table_size + head_count],
        gains[1],
        hidden_sum,
        return_sum,
    )


def solution(mesh):
    def run(*arrays):
        with jax.sharding.use_abstract_mesh(mesh.abstract_mesh):
            return jax.shard_map(
                body,
                mesh=mesh,
                in_specs=(
                    P(("dp", "tensor"), None),
                    P("dp", None),
                    P("dp", "tensor", None),
                    P("tensor", None, None),
                    P("tensor", None, None),
                    P(),
                    P(None, "tensor"),
                    P(None, "tensor"),
                    P(None, "tensor"),
                    P("tensor", None),
                    P(None, "tensor"),
                    P("tensor"),
                    P(),
                    P(None, "tensor"),
                    P("tensor", None),
                    P(("dp", "tensor"), None),
                ),
                out_specs=(
                    P(("dp", "tensor"), None),
                    P(("dp", "tensor"), None),
                    P(),
                    P(None, "tensor"),
                    P(None, "tensor"),
                    P(None, "tensor"),
                    P("tensor", None),
                    P(None, "tensor"),
                    P("tensor"),
                    P(),
                    P(None, "tensor"),
                    P("tensor", None),
                ),
                check_vma=False,
            )(*arrays)

    return run
```

```python
import functools
import math

import jax
import jax.numpy as jnp
from jax import lax
from jax.experimental import pallas as pl
from jax.experimental.pallas import tpu as pltpu
from jax.sharding import PartitionSpec as P

eps_norm = 1e-06
far_steps = (12, 16, 23, 32, 46, 64, 91)
exact_mode = lax.Precision.HIGHEST
low_type = jnp.bfloat16
full_type = jnp.float32
log2_e = math.log2(math.e)
tile = 256
span = 3 * tile
ring = 1024
mask_gap = -(2.0**100)
vmem_most = 60 * 2**20


def bucket_of(relative):
    upper_half = jnp.where(relative > 0, 16, 0).astype(jnp.int32)
    distance = jnp.abs(relative)
    far_bucket = 8 + sum(((distance >= step_size).astype(jnp.int32) for step_size in far_steps))
    return upper_half + jnp.where(distance < 8, distance, far_bucket)


def rms_scaled(rows, gain):
    return rows * lax.rsqrt(jnp.mean(rows * rows, -1, keepdims=True) + eps_norm) * gain


def gelu_pair(rows):
    reach = math.sqrt(2.0 / math.pi)
    square = rows * rows
    turn = jnp.tanh(reach * rows * (1.0 + 0.044715 * square))
    share = 0.5 * (1.0 + turn)
    steep = 0.5 * (1.0 - turn * turn) * reach * (1.0 + 3.0 * 0.044715 * square)
    return (rows * share).astype(low_type), (share + rows * steep).astype(low_type)


def dot_rows(left, right):
    return jnp.dot(left, right, preferred_element_type=full_type)


def dot_outer(left, right):
    return lax.dot_general(
        left, right, (((0,), (0,)), ((), ())), preferred_element_type=full_type
    )


def dot_inner(left, right):
    return lax.dot_general(
        left, right, (((1,), (1,)), ((), ())), preferred_element_type=full_type
    )


def interleave_kernel(key_ref, value_ref, table_ref):
    rows = key_ref.shape[1]
    row = lax.broadcasted_iota(jnp.int32, (256, 256), 0)
    column = lax.broadcasted_iota(jnp.int32, (256, 256), 1)
    order = jnp.where(column == (row // 2 + (row % 2) * 128), 1.0, 0.0).astype(low_type)
    for part in range(rows // 256):
        low, high = pl.ds(part * 256, 128), pl.ds(part * 256 + 128, 128)
        both = jnp.concatenate(
            [
                jnp.concatenate([key_ref[0, low], key_ref[0, high]], 1),
                jnp.concatenate([value_ref[0, low], value_ref[0, high]], 1),
            ],
            0,
        )
        mixed = dot_rows(order, both).astype(low_type)
        table_ref[pl.ds(part * 512, 256), :] = mixed[:, :128]
        table_ref[pl.ds(part * 512 + 256, 256), :] = mixed[:, 128:]


def interleave(memory_keys, memory_values):
    heads, rows, width = memory_keys.shape
    step = min(8192, rows)
    spec = pl.BlockSpec((1, step, width), lambda h, i: (h, i, 0))
    return pl.pallas_call(
        interleave_kernel,
        grid=(heads, rows // step),
        in_specs=[spec, spec],
        out_specs=pl.BlockSpec((2 * step, width), lambda h, i: (h * (rows // step) + i, 0)),
        out_shape=jax.ShapeDtypeStruct((heads * rows * 2, width), low_type),
        compiler_params=pltpu.CompilerParams(vmem_limit_bytes=vmem_most),
        cost_estimate=pl.CostEstimate(
            flops=heads * rows * 4 * 256 * width,
            bytes_accessed=heads * rows * width * 8,
            transcendentals=0,
        ),
        name="interleave",
    )(memory_keys, memory_values).reshape(heads, rows, 2, width)


def own_columns(picks):
    shape = (8, 8 * picks * 2)
    lane = lax.broadcasted_iota(jnp.int32, shape, 1)
    row = lax.broadcasted_iota(jnp.int32, shape, 0)
    return jnp.logical_and(lane // (2 * picks) == row, lane % 2 == 0)


def copy_rows(picked, first, table_ref, found_ref, start, count):
    for at in range(0, count, 8):
        rows_now = [
            table_ref[picked[(first + at + j) // 128, (first + at + j) % 128]] for j in range(8)
        ]
        for j in range(8):
            found_ref[start + at + j] = rows_now[j]
        yield


def recall_rows(picks, scale, own, query_ref, query_at, rows_ref, read_ref, read_at, tokens):
    wide = 8 * picks * 2
    groups = range(tokens // 8)
    scores = []
    for g in groups:
        rows = rows_ref[pl.ds(g * wide, wide), :]
        scores.append(dot_inner(query_ref[pl.ds(query_at + g * 8, 8), :], rows))
        yield
    shifted = []
    totals = []
    for g in groups:
        masked = jnp.where(own, scores[g] * (scale * log2_e), -jnp.inf)
        exponent = jnp.exp2(masked - jnp.max(masked, 1, keepdims=True))
        totals.append(jnp.sum(exponent, 1, keepdims=True))
        shifted.append(pltpu.roll(exponent, 1, 1).astype(low_type))
        yield
    for g in groups:
        rows = rows_ref[pl.ds(g * wide, wide), :]
        read_ref[pl.ds(read_at + g * 8, 8), :] = dot_rows(shifted[g], rows) / totals[g]
        yield


def weave(many, many_count, few, few_count):
    done = 0
    for number in range(few_count):
        until = (number + 1) * many_count // few_count
        while done < until:
            next(many)
            done += 1
        next(few)


def gather_kernel(
    picks, scale, index_hbm, table_hbm, now_ref, before_ref, found_ref, late_ref, early_ref,
    table_ref, table_sems, index_a, index_b, index_sems, stage_ref, stage_sems,
):
    step = pl.program_id(0)
    steps = pl.num_programs(0) - 1
    heads = table_sems.shape[0]
    blocks = steps // heads
    chunk = found_ref.shape[0] // 2
    rows = table_ref.shape[0] // heads
    slots = (index_a, index_b)
    part = chunk // 2
    tokens = part // picks
    own = own_columns(picks)
    flat = found_ref.reshape(4 * chunk, 128)

    def index_copy(number, slot):
        return pltpu.make_async_copy(index_hbm.at[number], slots[slot], index_sems.at[slot])

    def table_copy(number):
        where = pl.ds(number * rows, rows)
        return pltpu.make_async_copy(
            table_hbm.at[where], table_ref.at[where], table_sems.at[number]
        )

    def stage_copy(number):
        return pltpu.make_async_copy(
            flat.at[pl.ds(number * 2 * part, 2 * part)], stage_ref.at[number], stage_sems.at[number]
        )

    def reads(number, query_ref, read_ref):
        return recall_rows(
            picks, scale, own, query_ref, (number % 2) * tokens, stage_ref.at[number], read_ref,
            (number % 2) * tokens, tokens,
        )

    @pl.when(step == 0)
    def start_all():
        index_copy(0, 0).start()
        index_copy(1, 1).start()
        for number in range(heads):
            table_copy(number).start()
        stage_copy(2).start()
        stage_copy(3).start()

    @pl.when(jnp.logical_and(step < steps, step % blocks == 0))
    def wait_table():
        table_copy(step // blocks).wait()

    @pl.when(step < steps)
    def work():
        following = jnp.minimum(step + 1, steps - 1)
        for number in range(4):
            slot = number // 2
            if number % 2 == 0:
                index_copy(2 * step + slot, slot).wait()
            finished = (number + 2) % 4
            stage_copy(finished).wait()
            copied = copy_rows(
                slots[slot], (number % 2) * part, table_ref, found_ref, number * part, part
            )
            if number < 2:
                read = reads(finished, before_ref, late_ref)
            else:
                read = reads(finished, now_ref, early_ref)
            weave(copied, part // 8, read, 3 * (tokens // 8))
            stage_copy(number).start()
            if number % 2 == 1:
                index_copy(2 * following + slot, slot).start()

    @pl.when(step == steps)
    def finish():
        for number in (2, 3):
            stage_copy(number).wait()
            for unused in reads(number, before_ref, late_ref):
                pass
        for slot in range(2):
            index_copy(2 * (steps - 1) + slot, slot).wait()


def gather_found(index_rows, table, queries, picks, scale):
    heads, rows, unused, width = table.shape
    tokens = queries.shape[0]
    half = 128
    blocks = tokens // (2 * half)
    steps = heads * blocks
    chunk = half * picks

    def query_spec(shift):
        def place(t):
            at = jnp.clip(t - shift, 0, steps - 1)
            return (2 * (at % blocks) + shift, at // blocks)

        return pl.BlockSpec((half, width), place)

    return pl.pallas_call(
        functools.partial(gather_kernel, picks, scale),
        grid=(steps + 1,),
        in_specs=[
            pl.BlockSpec(memory_space=pl.ANY),
            pl.BlockSpec(memory_space=pl.ANY),
            query_spec(0),
            query_spec(1),
        ],
        out_specs=[
            pl.BlockSpec((2 * chunk, 2, width), lambda t: (jnp.minimum(t, steps - 1), 0, 0)),
            pl.BlockSpec((half, width), lambda t: (jnp.maximum(t - 1, 0), 0)),
            pl.BlockSpec((half, width), lambda t: (jnp.minimum(t, steps - 1), 0)),
        ],
        out_shape=[
            jax.ShapeDtypeStruct((heads * tokens * picks, 2, width), low_type),
            jax.ShapeDtypeStruct((heads * tokens // 2, width), full_type),
            jax.ShapeDtypeStruct((heads * tokens // 2, width), full_type),
        ],
        scratch_shapes=[
            pltpu.VMEM((heads * rows, 2, width), low_type),
            pltpu.SemaphoreType.DMA((heads,)),
            pltpu.SMEM((chunk // 128, 128), jnp.int32),
            pltpu.SMEM((chunk // 128, 128), jnp.int32),
            pltpu.SemaphoreType.DMA((2,)),
            pltpu.VMEM((4, chunk, width), low_type),
            pltpu.SemaphoreType.DMA((4,)),
        ],
        compiler_params=pltpu.CompilerParams(vmem_limit_bytes=vmem_most),
        cost_estimate=pl.CostEstimate(
            flops=0, bytes_accessed=4 * heads * tokens * picks * width * 4, transcendentals=0
        ),
        name="gather_found",
    )(
        index_rows.reshape(-1, chunk // 128, 128), table.reshape(heads * rows, 2, width), queries,
        queries,
    )


def band(column_ref):
    wide = jnp.broadcast_to(column_ref[0], (tile, ring))
    return pltpu.roll(wide, 0, 1, stride=1, stride_axis=0)[:, :span]


def local_kernel(
    scale, gate_ref, far_ref, column_ref, query_ref, key_ref, value_ref, query_mask_ref,
    key_mask_ref, early_ref, late_ref, mixed_ref, bias_ref,
):
    head = pl.program_id(0)

    @pl.when(pl.program_id(1) == 0)
    def make_band():
        bias_ref[...] = band(column_ref)

    gate = gate_ref[head]
    count = query_ref.shape[0] // tile
    at = [pl.ds(t * tile, tile) for t in range(count)]
    keys = [jnp.concatenate([key_ref[a, :], key_mask_ref[0, a, :]], 1) for a in at]
    for t in range(count):
        rows = jnp.concatenate([query_ref[at[t], :], query_mask_ref[0, at[t], :]], 1)
        parts = []
        for j in range(count):
            step = j - t
            if step < -1:
                bias = far_ref[head, 0]
            elif step > 1:
                bias = far_ref[head, 1]
            else:
                bias = bias_ref[:, pl.ds((step + 1) * tile, tile)]
            parts.append(dot_inner(rows, keys[j]) * (scale * log2_e) + bias)
        top = jnp.max(functools.reduce(jnp.maximum, parts), 1, keepdims=True)
        parts = [jnp.exp2(part - top) for part in parts]
        total = jnp.sum(functools.reduce(jnp.add, parts), 1, keepdims=True)
        read = sum(dot_rows(parts[j].astype(low_type), value_ref[at[j], :]) for j in range(count))
        half = pl.ds(t * (tile // 2), tile // 2)
        recalled = jnp.concatenate([early_ref[half, :], late_ref[half, :]], 0)
        mixed_ref[at[t], :] = (gate * recalled + ((1.0 - gate) / total) * read).astype(low_type)


def local_read(projected, query_mask, key_mask, early, late, columns, far, gates, seq_len, scale):
    tokens, width = projected.shape
    heads = gates.shape[0]
    width = width // (3 * heads)
    sequences = tokens // seq_len
    half_spec = pl.BlockSpec((seq_len // 2, width), lambda h, s: (h * sequences + s, 0))

    def rows_of(shift):
        return pl.BlockSpec((seq_len, width), lambda h, s: (s, h + shift * heads))

    mask_spec = pl.BlockSpec((1, seq_len, 128), lambda h, s: (s, 0, 0))
    smem = pl.BlockSpec(memory_space=pltpu.SMEM)
    return pl.pallas_call(
        functools.partial(local_kernel, scale),
        grid=(heads, tokens // seq_len),
        in_specs=[
            smem,
            smem,
            pl.BlockSpec((1, 1, ring), lambda h, s: (h, 0, 0)),
            rows_of(0),
            rows_of(1),
            rows_of(2),
            mask_spec,
            mask_spec,
            half_spec,
            half_spec,
        ],
        out_specs=rows_of(0),
        out_shape=jax.ShapeDtypeStruct((tokens, heads * width), low_type),
        scratch_shapes=[pltpu.VMEM((tile, span), full_type)],
        compiler_params=pltpu.CompilerParams(vmem_limit_bytes=vmem_most),
        cost_estimate=pl.CostEstimate(
            flops=0, bytes_accessed=heads * tokens * seq_len * 20, transcendentals=0
        ),
        name="local_read",
    )(gates, far, columns, projected, projected, projected, query_mask, key_mask, early, late)


def recall_back_rows(
    picks, scale, own, gate, query_ref, delta_ref, at, rows_ref, read_ref, gains, tokens
):
    wide = 8 * picks * 2
    flight = 8
    groups = tokens // 8
    both = {}
    for first in range(-flight, groups, flight):
        for g in range(first + flight, min(first + 2 * flight, groups)):
            where = pl.ds(at + g * 8, 8)
            pair = jnp.concatenate([query_ref[where, :], delta_ref[where, :]], 0)
            both[g] = dot_inner(pair, rows_ref[pl.ds(g * wide, wide), :])
            yield
        for g in range(max(first, 0), first + flight if first >= 0 else 0):
            pair = both.pop(g)
            masked = jnp.where(own, pair[:8] * (scale * log2_e), -jnp.inf)
            exponent = jnp.exp2(masked - jnp.max(masked, 1, keepdims=True))
            weights = exponent / jnp.sum(exponent, 1, keepdims=True)
            reads = pltpu.roll(pair[8:], wide - 1, 1)
            expected = jnp.sum(weights * reads, 1, keepdims=True)
            gains.append(expected)
            score_delta = (weights * (reads - expected)).astype(low_type)
            rows = rows_ref[pl.ds(g * wide, wide), :]
            read_ref[pl.ds(g * 8, 8), :] = dot_rows(score_delta, rows) * (scale * gate)
            yield


def local_back_tile(
    t, scale, gate, far, query_ref, keys, turned, value_ref, query_mask_ref, delta_ref,
    bias_ref, near_ref, key_sum_ref, value_sum_ref, gains, far_sums, result,
):
    count = len(keys)
    at = [pl.ds(j * tile, tile) for j in range(count)]
    rows = jnp.concatenate([query_ref[at[t], :], query_mask_ref[0, at[t], :]], 1)
    delta = ((1.0 - gate) * delta_ref[at[t], :].astype(full_type)).astype(low_type)
    parts = []
    for j in range(count):
        step = j - t
        if step < -1:
            bias = far[0]
        elif step > 1:
            bias = far[1]
        else:
            bias = bias_ref[:, pl.ds((1 - step) * tile, tile)]
        parts.append(dot_inner(keys[j], rows) * (scale * log2_e) + bias)
        yield
    top = jnp.max(functools.reduce(jnp.maximum, parts), 0, keepdims=True)
    yield
    for j in range(count):
        parts[j] = jnp.exp2(parts[j] - top)
        yield
    inverse = 1.0 / jnp.sum(functools.reduce(jnp.add, parts), 0, keepdims=True)
    moves = []
    products = []
    for j in range(count):
        parts[j] = parts[j] * inverse
        moves.append(dot_inner(value_ref[at[j], :], delta))
        products.append(parts[j] * moves[j])
        yield
    expected = jnp.sum(functools.reduce(jnp.add, products), 0, keepdims=True)
    gains.append(expected)
    query_sum = None
    for j in range(count):
        step = j - t
        score_delta = parts[j] * (moves[j] - expected)
        if abs(step) > 1:
            side = 0 if step < 0 else 1
            far_sums[side].append(jnp.sum(score_delta.reshape(tile // 8, 8, tile), 0))
        else:
            near_ref[:, pl.ds((1 - step) * tile, tile)] += score_delta
        yield
        low_delta = score_delta.astype(low_type)
        value_part = dot_rows(parts[j].astype(low_type), delta)
        yield
        key_part = dot_rows(low_delta, query_ref[at[t], :])
        yield
        query_part = dot_rows(turned[j], low_delta)
        if t == 0:
            value_sum_ref[at[j], :] = value_part
            key_sum_ref[at[j], :] = key_part
        else:
            value_sum_ref[at[j], :] += value_part
            key_sum_ref[at[j], :] += key_part
        query_sum = query_part if j == 0 else query_sum + query_part
        yield
    result.append(query_sum.T * scale)
    yield


def run_together(first, second):
    first, second = list_steps(first), list_steps(second)
    first_total, second_total = next(first), next(second)
    done = 0
    for number in range(second_total):
        until = (number + 1) * first_total // second_total
        while done < until:
            next(first)
            done += 1
        next(second)


def list_steps(counted):
    count, steps = counted
    yield count
    yield from steps


def back_kernel(
    picks, scale, head, gate_ref, far_ref, column_ref, query_ref, key_ref, value_ref,
    query_mask_ref, key_mask_ref, delta_ref, found_hbm, query_delta_ref, key_delta_ref,
    value_delta_ref, diagonal_ref, sums_ref, bias_ref, near_ref, key_sum_ref, value_sum_ref,
    read_ref, rows_ref, rows_sems,
):
    place = pl.program_id(0)
    sequence = pl.program_id(1)
    sequences = pl.num_programs(1)
    total_tiles = pl.num_programs(0) * sequences * (query_ref.shape[0] // tile)
    count = query_ref.shape[0] // tile
    block = rows_ref.shape[1]
    own = own_columns(picks)
    gate = gate_ref[place]
    far_left, far_right = far_ref[place, 0], far_ref[place, 1]

    def rows_copy(number, slot):
        start = (head * sequences * count + number) * block
        return pltpu.make_async_copy(
            found_hbm.at[pl.ds(pl.multiple_of(start, block), block)],
            rows_ref.at[slot],
            rows_sems.at[slot],
        )

    @pl.when(jnp.logical_and(place == 0, sequence == 0))
    def begin():
        for slot in range(2):
            rows_copy(slot, slot).start()

    @pl.when(sequence == 0)
    def begin_head():
        bias_ref[...] = band(column_ref)
        near_ref[...] = jnp.zeros(near_ref.shape, full_type)
        sums_ref[...] = jnp.zeros(sums_ref.shape, full_type)

    at = [pl.ds(t * tile, tile) for t in range(count)]
    keys = [jnp.concatenate([key_ref[a, :], key_mask_ref[0, a, :]], 1) for a in at]
    turned = [key_ref[a, :].astype(full_type).T.astype(low_type) for a in at]
    gains, recall_gains, far_sums = [], [], [[], []]
    for t in range(count):
        slot = t % 2
        number = (place * sequences + sequence) * count + t
        rows_copy(number, slot).wait()
        result = []
        run_together(
            (
                2 * (tile // 8),
                recall_back_rows(
                    picks, scale, own, gate, query_ref, delta_ref, t * tile, rows_ref.at[slot],
                    read_ref, recall_gains, tile,
                ),
            ),
            (
                7 * count + 2,
                local_back_tile(
                    t, scale, gate, (far_left, far_right), query_ref, keys, turned, value_ref, query_mask_ref,
                    delta_ref, bias_ref, near_ref, key_sum_ref, value_sum_ref, gains, far_sums,
                    result,
                ),
            ),
        )
        query_delta_ref[at[t], :] = (result[0] + read_ref[...]).astype(low_type)

        @pl.when(number + 2 < total_tiles)
        def ahead():
            rows_copy(number + 2, slot).start()

    key_delta_ref[...] = (key_sum_ref[...] * scale).astype(low_type)
    value_delta_ref[...] = value_sum_ref[...].astype(low_type)
    sums_ref[0, 0:1] += functools.reduce(jnp.add, gains)
    for side in range(2):
        if far_sums[side]:
            sums_ref[0, 8 + 8 * side : 16 + 8 * side] += functools.reduce(jnp.add, far_sums[side])
    sums_ref[0, 24:32] += jnp.broadcast_to(functools.reduce(jnp.add, recall_gains), (8, tile))

    @pl.when(sequence == sequences - 1)
    def fold_diagonals():
        total = jnp.zeros((8, ring), full_type)
        for g in range(tile // 8):
            part = jnp.concatenate(
                [near_ref[pl.ds(g * 8, 8), :], jnp.zeros((8, ring - span), full_type)], 1
            )
            total = total + (pltpu.roll(part, ring - 8 * g, 1) if g else part)
        row = lax.broadcasted_iota(jnp.int32, (8, ring), 0)
        for bit in (1, 2, 4):
            total = jnp.where((row & bit) != 0, pltpu.roll(total, ring - bit, 1), total)
        diagonal_ref[0] = total


def back_heads(
    projected, query_mask, key_mask, mixed_delta, found, columns, far, gates, seq_len, picks, scale,
    heads_now, kept, carried, after,
):
    tokens = mixed_delta.shape[0]
    heads = gates.shape[0]
    width = mixed_delta.shape[1] // heads
    anywhere = pl.BlockSpec(memory_space=pl.ANY)
    head, number = heads_now
    chosen = slice(head, head + number)
    extra = len(kept) + len(carried) + len(after)

    def rows_of(shift):
        return pl.BlockSpec((seq_len, width), lambda h, s: (s, h + head + shift * heads))

    def kernel(*refs):
        outs = refs[10 + extra :]
        back_kernel(picks, scale, head, *refs[:10], *outs[:5], *outs[5 + len(carried) :])

    mask_spec = pl.BlockSpec((1, seq_len, 128), lambda h, s: (s, 0, 0))
    smem = pl.BlockSpec(memory_space=pltpu.SMEM)
    rows_shape = jax.ShapeDtypeStruct((tokens, heads * width), low_type)
    first = 10 + len(kept)
    out = pl.pallas_call(
        kernel,
        grid=(number, tokens // seq_len),
        in_specs=[
            smem,
            smem,
            pl.BlockSpec((1, 1, ring), lambda h, s: (h, 0, 0)),
            rows_of(0),
            rows_of(1),
            rows_of(2),
            mask_spec,
            mask_spec,
            rows_of(0),
            anywhere,
        ]
        + [anywhere] * extra,
        out_specs=[
            rows_of(0),
            rows_of(0),
            rows_of(0),
            pl.BlockSpec((1, 8, ring), lambda h, s: (h, 0, 0)),
            pl.BlockSpec((1, 32, tile), lambda h, s: (h, 0, 0)),
        ]
        + [anywhere] * len(carried),
        out_shape=[
            rows_shape,
            rows_shape,
            rows_shape,
            jax.ShapeDtypeStruct((number, 8, ring), full_type),
            jax.ShapeDtypeStruct((number, 32, tile), full_type),
        ]
        + [jax.ShapeDtypeStruct(part.shape, part.dtype) for part in carried],
        input_output_aliases={10 + i: i for i in range(len(kept))}
        | {first + i: 5 + i for i in range(len(carried))},
        scratch_shapes=[
            pltpu.VMEM((tile, span), full_type),
            pltpu.VMEM((tile, span), full_type),
            pltpu.VMEM((seq_len, width), full_type),
            pltpu.VMEM((seq_len, width), full_type),
            pltpu.VMEM((tile, width), full_type),
            pltpu.VMEM((2, tile * picks * 2, width), low_type),
            pltpu.SemaphoreType.DMA((2,)),
        ],
        compiler_params=pltpu.CompilerParams(vmem_limit_bytes=vmem_most),
        cost_estimate=pl.CostEstimate(
            flops=0, bytes_accessed=number * tokens * picks * width * 8, transcendentals=0
        ),
        name="back_heads",
    )(
        gates[chosen], far[chosen], columns[chosen], projected, projected, projected, query_mask,
        key_mask, mixed_delta, found, *kept, *carried, *after,
    )
    return list(out[:3]), out[3], out[4], list(out[5:])


def mask_rows(block_ids):
    level = jnp.arange(128, dtype=jnp.int32)
    gap = block_ids[:, :, None] - level
    query_mask = jnp.where((gap >= 0) & (gap <= 1), 0.0, mask_gap).astype(low_type)
    key_mask = (gap == 0).astype(low_type)
    return query_mask, key_mask


def fetch(rows):
    group = lax.axis_size("tensor")
    return [rows] + [
        lax.ppermute(rows, "tensor", [((i + k) % group, i) for i in range(group)])
        for k in range(1, group)
    ]


def in_order(shares):
    group = lax.axis_size("tensor")
    rows = shares[0].shape[0]
    whole = jnp.zeros((group * rows,) + shares[0].shape[1:], shares[0].dtype)
    for k in range(group):
        start = ((lax.axis_index("tensor") + k) % group) * rows
        whole = lax.dynamic_update_slice_in_dim(whole, shares[k], start, 0)
    return whole


def share_of(whole, k, rows):
    start = ((lax.axis_index("tensor") + k) % lax.axis_size("tensor")) * rows
    return lax.dynamic_slice_in_dim(whole, start, rows, 0)


def fold(term, piece):
    group = lax.axis_size("tensor")
    sent = [
        lax.ppermute(
            term(piece(k)).astype(low_type), "tensor", [(i, (i + k) % group) for i in range(group)]
        )
        for k in range(1, group)
    ]
    return sum((part.astype(full_type) for part in sent), term(piece(0)))


def bit_orders():
    bits = lax.axis_size("dp").bit_length() - 1
    near = [(0, 1, 2), (1, 2, 0), (2, 0, 1)]
    return [list(head) + list(range(3, bits)) for head in near]


def swap_over(rows, bit):
    return lax.ppermute(rows, "dp", [(i, i ^ (1 << bit)) for i in range(lax.axis_size("dp"))])


def side_of(bit):
    return (lax.axis_index("dp") >> bit) & 1


def halve_step(parts, orders, step):
    kept, sent = [], []
    for part, order in zip(parts, orders):
        half = part.shape[0] // 2
        side = side_of(order[step])
        sent.append(
            swap_over(
                lax.dynamic_slice_in_dim(part, (1 - side) * half, half, 0), order[step]
            )
        )
        kept.append(lax.dynamic_slice_in_dim(part, side * half, half, 0))
    return kept, sent


def add_low(kept, sent):
    return [
        (a.astype(full_type) + b.astype(full_type)).astype(low_type) for a, b in zip(kept, sent)
    ]


def double_all(parts, beside):
    orders = bit_orders()
    for step in reversed(range(len(orders[0]))):
        got = [swap_over(part, order[step]) for part, order in zip(parts, orders)]
        if step == 1:
            got, beside = lax.optimization_barrier((got, beside))
        wider = []
        for part, other, order in zip(parts, got, orders):
            rows = part.shape[0]
            side = side_of(order[step])
            whole = jnp.zeros((2 * rows,) + part.shape[1:], part.dtype)
            whole = lax.dynamic_update_slice_in_dim(whole, part, side * rows, 0)
            wider.append(lax.dynamic_update_slice_in_dim(whole, other, (1 - side) * rows, 0))
        parts = wider
    return parts, beside


def pack(parts):
    width = min(part.shape[1] for part in parts)
    return jnp.concatenate(
        [
            part[:, start : start + width]
            for part in parts
            for start in range(0, part.shape[1], width)
        ],
        0,
    )


def gather_all(packed, parts, orders):
    whole = lax.all_gather(packed, "dp", axis=0)
    width = packed.shape[1]
    wide = []
    start = 0
    for part, order in zip(parts, orders):
        bits = len(order)
        rows = part.shape[0]
        columns = []
        for unused in range(part.shape[1] // width):
            piece = whole[:, start : start + rows].reshape((2,) * bits + (rows, width))
            piece = piece.transpose([bits - 1 - bit for bit in order] + [bits, bits + 1])
            columns.append(piece.reshape(-1, width))
            start += rows
        wide.append(jnp.concatenate(columns, 1).astype(full_type))
    return wide


def body(
    tokens,
    block_ids,
    memory_index,
    memory_keys,
    memory_values,
    attn_gain,
    query_weight,
    key_weight,
    value_weight,
    output_weight,
    position_table,
    memory_gate,
    mlp_gain,
    hidden_weight,
    return_weight,
    grad_output,
):
    share_rows = tokens.shape[0]
    seq_len = block_ids.shape[1]
    head_count, memory_rows, head_width = memory_keys.shape
    picks = memory_index.shape[2]
    inner_width = head_count * head_width
    scale = head_width ** (-0.5)

    offsets = jnp.arange(head_count, dtype=jnp.int32) * memory_rows
    index_rows = memory_index.transpose(1, 0, 2) + offsets[:, None, None]
    table = interleave(memory_keys, memory_values)

    token_full = tokens.astype(full_type)
    normed_rows = rms_scaled(token_full, attn_gain).astype(low_type)
    normed = lax.all_gather(normed_rows, "tensor", axis=0, tiled=True)
    joined = jnp.concatenate([query_weight, key_weight, value_weight], 1)
    projected = dot_rows(normed, joined).astype(low_type)
    found, late, early = gather_found(index_rows, table, projected, picks, scale)
    found = found.reshape(-1, head_width)

    query_mask, key_mask = mask_rows(block_ids)
    place = jnp.arange(ring, dtype=jnp.int32)
    place = jnp.where(place < span, place, place - ring)
    ahead = bucket_of(place - tile)
    behind = bucket_of(tile - place)
    level = jnp.arange(32, dtype=jnp.int32)
    ahead_hot = (ahead[:, None] == level).astype(full_type)
    behind_hot = (behind[:, None] == level).astype(full_type)
    scaled_table = position_table * log2_e
    ahead_columns = jnp.dot(ahead_hot, scaled_table, precision=exact_mode).T[:, None, :]
    behind_columns = jnp.dot(behind_hot, scaled_table, precision=exact_mode).T[:, None, :]
    far = jnp.stack([scaled_table[15], scaled_table[31]], 1)
    gates = jax.nn.sigmoid(memory_gate)

    mixed_rows = local_read(
        projected, query_mask, key_mask, early, late, ahead_columns, far, gates, seq_len, scale
    )
    middle = token_full + fold(
        lambda rows: dot_rows(rows, output_weight), lambda k: share_of(mixed_rows, k, share_rows)
    )
    second_rows = rms_scaled(middle, mlp_gain).astype(low_type)
    grad_full = jnp.concatenate(fetch(grad_output), 0)
    second = jnp.concatenate(fetch(second_rows), 0)
    active, slope = gelu_pair(dot_rows(second, hidden_weight))
    slope = lax.optimization_barrier(slope)
    orders = bit_orders()
    steps = len(orders[0])

    return_low = dot_outer(active, grad_full).astype(low_type)
    return_half = return_low.shape[0] // 2
    kept_back, sent_back = halve_step(
        [return_low[:return_half], return_low[return_half:]], orders[1:], 0
    )
    active_delta = dot_inner(grad_full, return_weight)
    hidden_delta = (active_delta * slope.astype(full_type)).astype(low_type)
    second_delta = fold(
        lambda rows: dot_inner(rows, hidden_weight),
        lambda k: lax.slice_in_dim(hidden_delta, k * share_rows, (k + 1) * share_rows),
    )
    hidden_half = hidden_delta.shape[1] // 2
    hidden_parts = [
        dot_outer(second, hidden_delta[:, :hidden_half]).astype(low_type),
        dot_outer(second, hidden_delta[:, hidden_half:]).astype(low_type),
    ]
    kept, sent = halve_step(hidden_parts, orders[:2], 0)

    kept_back, kept = lax.optimization_barrier((kept_back, kept))
    kept_back, sent_back = halve_step(add_low(kept_back, sent_back), orders[1:], 1)

    second_back = jax.vjp(rms_scaled, middle, mlp_gain)[1]
    middle_part, mlp_gain_part = second_back(second_delta)
    middle_delta = grad_output.astype(full_type) + middle_part
    middle_low = middle_delta.astype(low_type)
    kept, kept_back, middle_low = lax.optimization_barrier((kept, kept_back, middle_low))
    kept, sent = halve_step(add_low(kept, sent), orders[:2], 1)
    kept_back, sent_back = halve_step(add_low(kept_back, sent_back), orders[1:], 2)
    middle_full = in_order(fetch(middle_low))
    mixed_delta = dot_inner(middle_full, output_weight).astype(low_type)
    kept, kept_back, mixed_delta = lax.optimization_barrier((kept, kept_back, mixed_delta))
    kept, sent = halve_step(add_low(kept, sent), orders[:2], 2)
    kept_back, sent_back = halve_step(add_low(kept_back, sent_back), orders[1:], 3)
    taken = 2
    for step in range(4, steps):
        kept_back, sent_back = halve_step(add_low(kept_back, sent_back), orders[1:], step)
    layer_output = (
        middle
        + fold(
            lambda rows: dot_rows(rows, return_weight),
            lambda k: lax.slice_in_dim(active, k * share_rows, (k + 1) * share_rows),
        )
    ).astype(low_type)

    shards, packed = [], []
    deltas = []
    diagonals = []
    local_sums = []
    heads_in_turn = [(0, 1)]
    if head_count > 1:
        heads_in_turn.append((1, 1))
    if head_count > 2:
        heads_in_turn.append((2, head_count - 2))
    for heads_now in heads_in_turn:
        deltas, diagonal_now, sums_now, kept = back_heads(
            projected, query_mask, key_mask, mixed_delta, found, behind_columns, far, gates,
            seq_len, picks, scale, heads_now, deltas, kept, packed,
        )
        diagonals.append(diagonal_now)
        local_sums.append(sums_now)
        if taken < steps - 1:
            taken += 1
            kept, sent = halve_step(add_low(kept, sent), orders[:2], taken)
        elif not shards:
            shards = add_low(kept, sent) + add_low(kept_back, sent_back)
            packed = [pack(shards)]
            kept = []
    while taken < steps - 1:
        taken += 1
        kept, sent = halve_step(add_low(kept, sent), orders[:2], taken)
    if not shards:
        shards = add_low(kept, sent) + add_low(kept_back, sent_back)
        packed = [pack(shards)]
    hidden_low_sum, hidden_high_sum, return_low_sum, return_high_sum = gather_all(
        packed[0], shards, orders[:2] + orders[1:]
    )
    hidden_sum = jnp.concatenate([hidden_low_sum, hidden_high_sum], 1)
    return_sum = jnp.concatenate([return_low_sum, return_high_sum], 0)
    query_delta, key_delta, value_delta = deltas
    diagonals = jnp.concatenate(diagonals, 0)
    local_sums = jnp.concatenate(local_sums, 0)
    recall_gain = jnp.sum(local_sums[:, 24:32, 0], 1)
    local_gain = jnp.sum(local_sums[:, 0], 1)
    gate_part = gates * (1.0 - gates) * recall_gain - gates * local_gain
    diagonal_sums = jnp.sum(diagonals, 1)
    table_part = jnp.dot(diagonal_sums, behind_hot, precision=exact_mode)
    far_left = jnp.sum(local_sums[:, 8:16], (1, 2))
    far_right = jnp.sum(local_sums[:, 16:24], (1, 2))
    table_part = table_part + far_left[:, None] * (level == 15) + far_right[:, None] * (level == 31)

    project_delta = jnp.concatenate([query_delta, key_delta, value_delta], 1)
    joined_part = dot_outer(normed, project_delta)
    attn_gain_part = jnp.sum(joined_part * joined.astype(full_type), 1) / attn_gain
    model_width = tokens.shape[1]
    small = jnp.concatenate([table_part.reshape(-1), gate_part])
    small = jnp.pad(small, (0, model_width - small.shape[0]))
    extra = jnp.stack([attn_gain_part, mlp_gain_part, small], 1)
    extra = jnp.pad(extra, ((0, 0), (0, 125)))
    joined_low = jnp.concatenate([joined_part, extra], 1).astype(low_type)
    joined_half = joined_low.shape[0] // 2
    last = [
        joined_low[:joined_half],
        joined_low[joined_half:],
        dot_outer(mixed_rows, middle_full).astype(low_type),
    ]
    for step in range(steps):
        last = add_low(*halve_step(last, orders, step))
    last, (hidden_sum, return_sum) = double_all(last, (hidden_sum, return_sum))
    *joined_sum, output_sum = last

    normed_delta = fold(
        lambda rows: dot_inner(rows, joined), lambda k: share_of(project_delta, k, share_rows)
    )
    first_back = jax.vjp(rms_scaled, token_full, attn_gain)[1]
    tokens_grad = (middle_delta + first_back(normed_delta)[0]).astype(low_type)

    def joined_columns(start, stop):
        return jnp.concatenate([part[:, start:stop].astype(full_type) for part in joined_sum], 0)

    last_columns = joined_columns(3 * inner_width, 3 * inner_width + 128)
    gains = sum(fetch(last_columns[:, :2].T))
    small_sum = last_columns[:, 2]
    table_size = head_count * 32
    return (
        layer_output,
        tokens_grad,
        gains[0],
        joined_columns(0, inner_width),
        joined_columns(inner_width, 2 * inner_width),
        joined_columns(2 * inner_width, 3 * inner_width),
        output_sum.astype(full_type),
        small_sum[:table_size].reshape(head_count, 32).T,
        small_sum[table_size : table_size + head_count],
        gains[1],
        hidden_sum,
        return_sum,
    )


def solution(mesh):
    def run(*arrays):
        with jax.sharding.use_abstract_mesh(mesh.abstract_mesh):
            return jax.shard_map(
                body,
                mesh=mesh,
                in_specs=(
                    P(("dp", "tensor"), None),
                    P("dp", None),
                    P("dp", "tensor", None),
                    P("tensor", None, None),
                    P("tensor", None, None),
                    P(),
                    P(None, "tensor"),
                    P(None, "tensor"),
                    P(None, "tensor"),
                    P("tensor", None),
                    P(None, "tensor"),
                    P("tensor"),
                    P(),
                    P(None, "tensor"),
                    P("tensor", None),
                    P(("dp", "tensor"), None),
                ),
                out_specs=(
                    P(("dp", "tensor"), None),
                    P(("dp", "tensor"), None),
                    P(),
                    P(None, "tensor"),
                    P(None, "tensor"),
                    P(None, "tensor"),
                    P("tensor", None),
                    P(None, "tensor"),
                    P("tensor"),
                    P(),
                    P(None, "tensor"),
                    P("tensor", None),
                ),
                check_vma=False,
            )(*arrays)

    return run
```
